256 devices in a mesh: gx: 8 (over y, core), gy: 4 (over z_hi), gz: 8 (over x, z_lo).
Axes of the slice: x: 4, y: 4, z: 8 (z_hi: 4, z_lo: 2; z = z_hi * 2 + z_lo), core: 2. Of those that a mesh axis runs over, the one named last changes fastest.
Arguments:
- velocity: float32 [3, 64, 128, 1024], P(None, 'gx', 'gy', 'gz'), may hold values from -4 to 4
- sample_cells: int32 [65536], P(('gx', 'gy', 'gz')), may hold values from 0 to 32767
- trainer_of: int32 [65536, 1], P(('gx', 'gy', 'gz')), may hold values from 0 to 31; in each aligned block of 256 rows (0 to 255, 256 to 511, ...) at most 16 rows name the same one
- targets: bfloat16 [6, 65536], P(None, ('gx', 'gy', 'gz')), may hold values from -6 to 6
- w_first: bfloat16 [32, 512, 81], P(('gx', 'gy')), may hold values from -0.625 to 0.625
- w_middle: bfloat16 [32, 512, 512], P(('gx', 'gy')), may hold values from -0.25 to 0.25
- w_last: bfloat16 [32, 6, 512], P(('gx', 'gy')), may hold values from -0.25 to 0.25
- biases: float32 [32, 1030], P(('gx', 'gy')), may hold values from -3 to 3
- middle_master: float32 [32, 262144], P(('gx', 'gy'), 'gz'), may hold values from -2 to 2
- middle_momentum: float32 [32, 262144], P(('gx', 'gy'), 'gz'), may hold values from -2 to 2
Outputs:
- new_velocity: float32 [3, 64, 128, 1024], P(None, 'gx', 'gy', 'gz')
- trainer_loss: float32 [8, 4, 8], P('gx', 'gy', 'gz')
- first_grads: float32 [32, 512, 81], P(('gx', 'gy'))
- last_grads: float32 [32, 6, 512], P(('gx', 'gy'))
- bias_grads: float32 [32, 1030], P(('gx', 'gy'))
- master_new: float32 [32, 262144], P(('gx', 'gy'), 'gz')
- momentum_new: float32 [32, 262144], P(('gx', 'gy'), 'gz')
The draws below stay inside these ranges and needn't reach their ends.
Inputs may be any that keep to these rules, and one draw needn't show every extreme that they name: `sample_cells`: each entry indexes a cell of its own device's brick as x * 32 * 128 + y * 128 + z. `trainer_of`: among the 256 samples of one device no trainer is named more than 16 times.
All inputs are finite; a program needn't handle non-finite values.
Results may differ from the reference program's by a relative error of at most 0.0044.
Values may be sent and summed in bfloat16 or wider, within the bound.
No kernel may reach another device: no remote copies, remote signals or barrier semaphores. Data moves between devices by JAX's collectives and lax.ppermute only.
A program may use at most 64 MiB of HBM per device.

```python
import math
import jax
import jax.numpy as jnp
import numpy as np
from jax import lax

CX = 8
CY = 32
CZ = 128
S_DEV = 256
HID = 512
FEAT = 81
OUT = 6
NX = 64
NY = 128
NZ = 1024
NSAMP = 65536
NTRAIN = 32
CAP = 16
N_GX = 8
N_GY = 4
N_GZ = 8


def touch_ends(entries, key, least, top_value):
    dims = entries.shape
    place = [jax.random.randint(jax.random.fold_in(key, axis), (), 0, dims[axis]) for axis in range(len(dims))]
    entries = entries.at[tuple(place)].set(least)
    longest = dims.index(max(dims))
    place[longest] = (place[longest] + 1) % dims[longest]
    return entries.at[tuple(place)].set(top_value)


def block_levels(rng, extent, shards, smallest, top_value):
    factor_of = 1.0
    for axis_at, blocks in shards:
        draws = jax.random.uniform(jax.random.fold_in(jax.random.fold_in(rng, 6), axis_at), (blocks,), jnp.float32, smallest / len(shards), top_value / len(shards))
        factor_of = factor_of * jnp.repeat(jnp.exp(draws), extent[axis_at] // blocks).reshape((-1,) + (1,) * (len(extent) - 1 - axis_at))
    return factor_of


def shared_out(own_key, own, number, rows, number_of, top, reach, slope):
    order = jax.random.permutation(own_key, number_of)
    packed, ordinary = portions_of(number_of, rows * top, reach, slope, True), portions_of(number_of, rows * top, reach, slope, False)
    places = jnp.arange(number_of)

    def named(tallies, rotation):
        used = int((tallies > 0).sum())
        fixed = max(1, used // 4)
        moved = fixed + (places - fixed + rotation * (used - fixed)) % max(1, number_of - fixed)
        return jnp.zeros((number_of,), jnp.int32).at[order[jnp.where(places < fixed, places, moved)]].set(jnp.asarray(tallies, jnp.int32))

    tallies = jnp.where(number % 4 == 0, named(packed, number // 4), named(ordinary, number - number // 4 - 1))
    mixed = jax.random.permutation(jax.random.fold_in(own, 3), number_of)
    donor, receiver = mixed[0:number_of // 2 * 2:2], mixed[1:number_of // 2 * 2:2]
    margin = jnp.minimum(tallies[donor] - 1, reach - tallies[receiver]) // 2
    margin = jnp.where((donor == order[0]) | (receiver == order[0]) | (tallies[receiver] == 0), 0, jnp.maximum(margin, 0))
    moved = jax.random.randint(jax.random.fold_in(own, 4), (number_of // 2,), 0, 1 << 20) % (margin + 1)
    tallies = tallies.at[donor].add(-moved).at[receiver].add(moved)
    labels = jnp.searchsorted(jnp.cumsum(tallies), jnp.arange(rows * top), side="right").astype(jnp.int32)
    listing = labels.reshape(top, rows).T
    listing = listing[jax.random.permutation(jax.random.fold_in(own, 1), rows)]
    rotation = jax.random.randint(jax.random.fold_in(own, 2), (rows, 1), 0, top)
    return jnp.take_along_axis(listing, (jnp.arange(top)[None, :] + rotation) % top, axis=1)


def portions_of(count, total, limit, slope, full):
    weights = [(1 << 20) // math.isqrt(standing ** slope) + 1 for standing in range(1, count + 1)]
    largest = limit if full else min(limit, max(-(-total // count), total * weights[0] // sum(weights)))
    least = 1 if total - largest >= count - 1 else 0
    counts, spare = [largest] + [least] * (count - 1), total - largest - least * (count - 1)
    while spare > 0:
        free = [i for i in range(1, count) if counts[i] < largest] or [i for i in range(1, count) if counts[i] < limit]
        whole, budget = sum([weights[i] for i in free]), spare
        for i in free:
            addition = min(limit - counts[i], max(1, budget * weights[i] // whole), spare)
            counts[i] = counts[i] + addition
            spare = spare - addition
    return np.array(counts)


def bell_draw(key, dims, spread, bound, split=(), held_as=jnp.bfloat16):
    drawn = jax.random.normal(key, dims, jnp.float32) * spread
    if len(split) > 0:
        drawn = block_levels(key, dims, split, -0.22, 0.18) * drawn
    return jnp.clip(drawn, min=-bound, max=bound).astype(held_as)


def setup_inputs(seed: int = 0) -> dict:
    key_list = jax.random.split(jax.random.key(seed), 11)
    velocity = bell_draw(key_list[0], (3, NX, NY, NZ), 1.0, 4.0, ((1, 8), (2, 4), (3, 8)), jnp.float32)
    sample_cells = touch_ends(jax.random.randint(key_list[1], (NSAMP,), 0, CX * CY * CZ), jax.random.fold_in(key_list[1], 1), 0, (CX * CY * CZ) - 1).astype(jnp.int32)
    trainer_of_keys = jax.random.split(jax.random.fold_in(key_list[2], 1), NSAMP // S_DEV)
    trainer_of_turns = jax.random.permutation(jax.random.fold_in(key_list[2], 3), NSAMP // S_DEV)
    trainer_of = jax.vmap(lambda own, number: shared_out(jax.random.fold_in(key_list[2], 2), own, number, S_DEV, N_GX * N_GY, 1, 2 * S_DEV // (N_GX * N_GY), 2))(trainer_of_keys, trainer_of_turns).reshape((NSAMP, 1))
    targets = bell_draw(key_list[3], (OUT, NSAMP), 1.0, 6.0, ((1, 256),))
    w_first = bell_draw(key_list[4], (NTRAIN, HID, FEAT), FEAT ** -0.5, 0.625, ((0, 32),))
    w_middle = bell_draw(key_list[5], (NTRAIN, HID, HID), HID ** -0.5, 0.25, ((0, 32),))
    w_last = bell_draw(key_list[6], (NTRAIN, OUT, HID), HID ** -0.5, 0.25, ((0, 32),))
    biases = bell_draw(key_list[7], (NTRAIN, 2 * HID + OUT), 0.5, 3.0, ((0, 32),), jnp.float32)
    middle_master = bell_draw(key_list[8], (NTRAIN, HID * HID), 0.3, 2.0, ((0, 32), (1, 8)), jnp.float32)
    middle_momentum = bell_draw(key_list[9], (NTRAIN, HID * HID), 0.3, 2.0, ((0, 32), (1, 8)), jnp.float32)
    return dict(velocity=velocity, sample_cells=sample_cells, trainer_of=trainer_of, targets=targets, w_first=w_first, w_middle=w_middle, w_last=w_last, biases=biases, middle_master=middle_master, middle_momentum=middle_momentum)


DT_STEP = 0.1
VISCOSITY = 0.2
LEARN_RATE = 0.05
MOMENTUM_KEEP = 0.9


def advance(padded):
    stacked = []
    for component in range(3):
        component_field = padded[component]
        interior = component_field[1:-1, 1:-1, 1:-1]
        flux_x = component_field * padded[0]
        flux_y = component_field * padded[1]
        flux_z = component_field * padded[2]
        diverge = flux_x[2:, 1:-1, 1:-1] - flux_x[:-2, 1:-1, 1:-1]
        diverge = diverge + flux_y[1:-1, 2:, 1:-1] - flux_y[1:-1, :-2, 1:-1]
        diverge = diverge + flux_z[1:-1, 1:-1, 2:] - flux_z[1:-1, 1:-1, :-2]
        beside = component_field[2:, 1:-1, 1:-1] + component_field[:-2, 1:-1, 1:-1]
        beside = beside + component_field[1:-1, 2:, 1:-1] + component_field[1:-1, :-2, 1:-1]
        beside = beside + component_field[1:-1, 1:-1, 2:] + component_field[1:-1, 1:-1, :-2]
        tendency = -0.5 * diverge + VISCOSITY * (beside - 6.0 * interior)
        stacked.append(interior + DT_STEP * tendency)
    return jnp.stack(stacked)


def gather_patch(padded, base_index, pad_y, pad_z):
    offset = jnp.arange(27, dtype=jnp.int32)
    stride_shift = (offset // 9) * (pad_y * pad_z) + ((offset // 3) % 3) * pad_z + offset % 3
    flat_index = (base_index[None, :] + stride_shift[:, None]).astype(jnp.int32)
    values = padded.reshape(padded.shape[0], -1)[:, flat_index]
    return values.reshape(3 * 27, base_index.shape[0])


def train_terms(inputs, wanted, present, w_first, w_middle, w_last, biases, row_count):
    hidden = w_first.shape[0]
    factor = 2.0 / (6.0 * row_count)
    act_one = jnp.tanh(jnp.dot(w_first, inputs, preferred_element_type=jnp.float32) + biases[:hidden, None]).astype(jnp.bfloat16)
    act_two = jnp.tanh(jnp.dot(w_middle, act_one, preferred_element_type=jnp.float32) + biases[hidden:2 * hidden, None]).astype(jnp.bfloat16)
    predicted = jnp.dot(w_last, act_two, preferred_element_type=jnp.float32) + biases[2 * hidden:, None]
    mismatch = (predicted - wanted) * present[None, :]
    row_loss = jnp.sum(mismatch * mismatch, axis=0) / (6.0 * row_count)
    delta_three = mismatch * factor
    back_three = delta_three.astype(jnp.bfloat16)
    last_grads = jnp.dot(back_three, act_two.T, preferred_element_type=jnp.float32)
    delta_two = jnp.dot(w_last.T, back_three, preferred_element_type=jnp.float32) * (1.0 - jnp.square(act_two.astype(jnp.float32)))
    back_two = delta_two.astype(jnp.bfloat16)
    middle_grads = jnp.dot(back_two, act_one.T, preferred_element_type=jnp.float32)
    delta_one = jnp.dot(w_middle.T, back_two, preferred_element_type=jnp.float32) * (1.0 - jnp.square(act_one.astype(jnp.float32)))
    back_one = delta_one.astype(jnp.bfloat16)
    first_grads = jnp.dot(back_one, inputs.T, preferred_element_type=jnp.float32)
    bias_grads = jnp.concatenate([jnp.sum(delta_one, axis=1), jnp.sum(delta_two, axis=1), jnp.sum(delta_three, axis=1)])
    return row_loss, first_grads, middle_grads, last_grads, bias_grads


def reference(velocity, sample_cells, trainer_of, targets, w_first, w_middle, w_last, biases, middle_master, middle_momentum):
    padded = jnp.pad(velocity, ((0, 0), (1, 1), (1, 1), (1, 1)))
    new_velocity = advance(padded)
    device_of = (jnp.arange(NSAMP, dtype=jnp.int32) // S_DEV).astype(jnp.int32)
    brick_x = device_of // (N_GY * N_GZ)
    brick_y = (device_of // N_GZ) % N_GY
    brick_z = device_of % N_GZ
    cell_x = sample_cells // (CY * CZ)
    cell_y = (sample_cells // CZ) % CY
    cell_z = sample_cells % CZ
    pad_y = NY + 2
    pad_z = NZ + 2
    base_index = ((brick_x * CX + cell_x) * (pad_y * pad_z) + (brick_y * CY + cell_y) * pad_z + (brick_z * CZ + cell_z)).astype(jnp.int32)
    features = gather_patch(padded, base_index, pad_y, pad_z).astype(jnp.bfloat16)
    blocks = NSAMP // S_DEV
    trainer_count = N_GX * N_GY
    trainer = trainer_of[:, 0].astype(jnp.int32)
    choose = (trainer.reshape(blocks, S_DEV)[:, :, None] == jnp.arange(trainer_count, dtype=jnp.int32)[None, None, :]).astype(jnp.int32)
    position = jnp.sum((jnp.cumsum(choose, axis=1) - choose) * choose, axis=2).reshape(-1).astype(jnp.int32)
    source = (device_of // N_GZ).astype(jnp.int32)
    slot = ((((trainer * N_GZ + brick_z) * trainer_count + source) * CAP) + position).astype(jnp.int32)
    total_slots = trainer_count * N_GZ * trainer_count * CAP
    slot_sample = jnp.full((total_slots,), NSAMP, jnp.int32).at[slot].set(jnp.arange(NSAMP, dtype=jnp.int32))
    features_ext = jnp.concatenate([features, jnp.zeros((FEAT, 1), jnp.bfloat16)], axis=1)
    targets_ext = jnp.concatenate([targets.astype(jnp.float32), jnp.zeros((OUT, 1), jnp.float32)], axis=1)
    present_ext = jnp.concatenate([jnp.ones((NSAMP,), jnp.float32), jnp.zeros((1,), jnp.float32)])
    slot_blocks = slot_sample.reshape(trainer_count, N_GZ, trainer_count * CAP)

    def one_trainer(item):
        index_rows, first_w, middle_w, last_w, bias_w = item

        def one_plane(totals, plane_index):
            inputs = features_ext[:, plane_index]
            wanted = targets_ext[:, plane_index]
            present = present_ext[plane_index]
            row_loss, grad_one, grad_two, grad_three, grad_bias = train_terms(inputs, wanted, present, first_w, middle_w, last_w, bias_w, S_DEV)
            return (totals[0] + grad_one, totals[1] + grad_two, totals[2] + grad_three, totals[3] + grad_bias), jnp.sum(row_loss)

        zeros_init = (jnp.zeros((HID, FEAT), jnp.float32), jnp.zeros((HID, HID), jnp.float32), jnp.zeros((OUT, HID), jnp.float32), jnp.zeros((2 * HID + OUT,), jnp.float32))
        summed, plane_losses = lax.scan(one_plane, zeros_init, index_rows)
        return summed[0], summed[1], summed[2], summed[3], plane_losses

    first_grads, middle_grads, last_grads, bias_grads, losses = lax.map(one_trainer, (slot_blocks, w_first, w_middle, w_last, biases))
    trainer_loss = losses.reshape(N_GX, N_GY, N_GZ)
    momentum_new = MOMENTUM_KEEP * middle_momentum + middle_grads.reshape(trainer_count, HID * HID)
    master_new = middle_master - LEARN_RATE * momentum_new
    return new_velocity, trainer_loss, first_grads, last_grads, bias_grads, master_new, momentum_new
```

```python
import functools

import jax
import jax.numpy as jnp
from jax import lax
from jax.experimental import pallas as pl
from jax.experimental.pallas import tpu as pltpu
from jax.sharding import PartitionSpec as P

DT_STEP = 0.1
VISCOSITY = 0.2
LEARN_RATE = 0.05
MOMENTUM_KEEP = 0.9

BF16 = jnp.bfloat16
F32 = jnp.float32
I32 = jnp.int32
NT = (((1,), (1,)), ((), ()))
TN = (((0,), (0,)), ((), ()))
EXACT = lax.Precision.HIGHEST
VMEM_LIMIT = 48 * 1024 * 1024
ROWS = 96
TAIL = 88
WIDE = 128


def params(limit=VMEM_LIMIT):
    return pltpu.CompilerParams(vmem_limit_bytes=limit)


def whole(count):
    return [pl.BlockSpec(memory_space=pltpu.VMEM)] * count


def iota(shape, dim):
    return lax.broadcasted_iota(I32, shape, dim)


def ones_where(mask):
    return jnp.where(mask, 1.0, 0.0).astype(BF16)


def y_faces_kernel(low_ref, high_ref, xlo_ref, xhi_ref, to_low_ref, to_high_ref):
    comps, size_x = low_ref.shape[0], low_ref.shape[1]
    last = high_ref.shape[2] - 1
    end = xlo_ref.shape[1] - 1
    to_low_ref[...] = jnp.zeros_like(to_low_ref)
    to_high_ref[...] = jnp.zeros_like(to_high_ref)
    for c in range(comps):
        to_low_ref[c, 0:1, :] = xlo_ref[c, 0:1, :]
        to_high_ref[c, 0:1, :] = xlo_ref[c, end : end + 1, :]
        for x in range(size_x):
            to_low_ref[c, x + 1 : x + 2, :] = low_ref[c, x, 0:1, :]
            to_high_ref[c, x + 1 : x + 2, :] = high_ref[c, x, last : last + 1, :]
        to_low_ref[c, size_x + 1 : size_x + 2, :] = xhi_ref[c, 0:1, :]
        to_high_ref[c, size_x + 1 : size_x + 2, :] = xhi_ref[c, end : end + 1, :]


def y_faces(velocity, xlo, xhi):
    comps, size_x, size_y, size_z = velocity.shape
    shape = jax.ShapeDtypeStruct((comps, 16, size_z), F32)
    top = size_y // 8 - 1
    spec = lambda at: pl.BlockSpec((comps, size_x, 8, size_z), lambda i: (0, 0, at, 0))
    full = lambda a: pl.BlockSpec(a, lambda i: (0,) * len(a))
    return pl.pallas_call(
        y_faces_kernel,
        grid=(1,),
        out_shape=(shape, shape),
        in_specs=[spec(0), spec(top), full(xlo.shape), full(xhi.shape)],
        out_specs=(full(shape.shape), full(shape.shape)),
        compiler_params=params(),
        name="y_faces",
    )(velocity, velocity, xlo, xhi)


def z_faces_kernel(v_ref, xlo_ref, xhi_ref, ylo_ref, yhi_ref, to_low_ref, to_high_ref):
    size_z = v_ref.shape[-1]
    lane = iota((8, size_z), 1)
    row = iota((8, size_z), 0)
    pick = jnp.where(
        ((row == 0) & (lane == 0)) | ((row == 1) & (lane == size_z - 1)), 1.0, 0.0
    ).astype(F32)
    start = 0
    for ref in (v_ref, xlo_ref, xhi_ref, ylo_ref, yhi_ref):
        block = ref[...]
        block = block.reshape(-1, size_z)
        ends = lax.dot_general(pick, block, NT, precision=EXACT, preferred_element_type=F32)
        to_low_ref[:, start : start + block.shape[0]] = ends[0:1]
        to_high_ref[:, start : start + block.shape[0]] = ends[1:2]
        start += block.shape[0]


def z_faces(velocity, xlo, xhi, ylo, yhi, total):
    shape = jax.ShapeDtypeStruct((1, total), F32)
    return pl.pallas_call(
        z_faces_kernel,
        out_shape=(shape, shape),
        in_specs=whole(5),
        out_specs=tuple(whole(2)),
        compiler_params=params(),
        name="z_faces",
    )(velocity, xlo, xhi, ylo, yhi)


def shifts(axis):
    count = lax.axis_size(axis)
    forward = [(i, i + 1) for i in range(count - 1)]
    return forward, [(b, a) for a, b in forward]


def pack_kernel(
    v_ref,
    xlo_ref,
    xhi_ref,
    ylo_ref,
    yhi_ref,
    zlo_ref,
    zhi_ref,
    cells_ref,
    trainer_ref,
    tail_ref,
    out_ref,
    picked,
    parts,
    *,
    trainers,
):
    comps, size_x, size_y, size_z = v_ref.shape
    samples = cells_ref.shape[1]
    cells = cells_ref[...]
    cell_z = cells % size_z
    cell_y = cells // size_z % size_y
    cell_x = cells // (size_y * size_z)

    depth = iota((size_z, samples), 0)
    choose_z = jnp.concatenate([ones_where(depth == cell_z + (r - 1)) for r in range(3)], axis=1)
    edge = iota((16, samples), 0)
    none = jnp.zeros((16, samples), BF16)
    choose_end = jnp.concatenate(
        [
            ones_where((edge == 0) & (cell_z == 0)),
            none,
            ones_where((edge == 1) & (cell_z == size_z - 1)),
        ],
        axis=1,
    )
    total = zlo_ref.shape[1]
    side = iota((16, total), 0)
    ends = jnp.where(side == 0, zlo_ref[...], jnp.where(side == 1, zhi_ref[...], 0.0)).astype(BF16)
    starts = []
    start = 0
    for ref in (v_ref, xlo_ref, xhi_ref, ylo_ref, yhi_ref):
        block = ref[...].reshape(-1, size_z).astype(BF16)
        rows = block.shape[0]
        inner = jnp.dot(block, choose_z, preferred_element_type=F32)
        outer = lax.dot_general(
            ends[:, start : start + rows], choose_end, TN, preferred_element_type=F32
        )
        picked[start : start + rows, :] = inner + outer
        starts.append(start)
        start += rows

    tile = 8
    sub = iota((tile, samples), 0)
    at_x = [cell_x == j for j in range(size_x)]

    def fold(first, rows, mask_of):
        sums = [None] * 3
        for k in range(rows // tile):
            mask = mask_of(k)
            for r in range(3):
                piece = picked[
                    first + k * tile : first + (k + 1) * tile, r * samples : (r + 1) * samples
                ]
                piece = jnp.where(mask, piece, 0.0)
                sums[r] = piece if sums[r] is None else sums[r] + piece
        return sums

    for c in range(comps):
        for q in range(3):
            totals = [[None] * 3 for _ in range(3)]
            for x in range(size_x + 2):
                if x == 0:
                    first = starts[1] + c * size_y
                elif x == size_x + 1:
                    first = starts[2] + c * size_y
                else:
                    first = (c * size_x + x - 1) * size_y
                sums = fold(first, size_y, lambda k: sub + (k * tile - q + 1) == cell_y)
                for p in range(3):
                    j = x - p
                    if 0 <= j < size_x:
                        for r in range(3):
                            piece = jnp.where(at_x[j], sums[r], 0.0)
                            totals[p][r] = piece if totals[p][r] is None else totals[p][r] + piece
            if q != 1:
                base = starts[3] if q == 0 else starts[4]
                at_edge = cell_y == (0 if q == 0 else size_y - 1)
                edge_x = jnp.where(at_edge, cell_x, -100)
                for p in range(3):
                    more = fold(
                        base + c * 16, 16, lambda k: sub + (k * tile - p) == edge_x
                    )
                    for r in range(3):
                        totals[p][r] = totals[p][r] + more[r]
            for p in range(3):
                for r in range(3):
                    f = c * 27 + 9 * p + 3 * q + r
                    parts[f * tile : (f + 1) * tile, :] = totals[p][r]

    feats = comps * 27
    gather = ones_where(
        lax.shift_right_logical(iota((TAIL, feats * tile), 1), 3) == iota((TAIL, feats * tile), 0)
    )
    features = jnp.dot(gather, parts[...].astype(BF16), preferred_element_type=F32)
    payload = jnp.concatenate(
        [features, tail_ref[...], jnp.zeros((WIDE - ROWS, samples), F32)], axis=0
    ).astype(BF16)

    trainer = trainer_ref[...]
    slots = out_ref.shape[0]
    capacity = slots // trainers
    same = iota((trainers, samples), 0) == trainer
    earlier = ones_where(iota((samples, samples), 0) < iota((samples, samples), 1))
    before = jnp.dot(ones_where(same), earlier, preferred_element_type=F32)
    position = jnp.sum(jnp.where(same, before, 0.0), axis=0, keepdims=True).astype(I32)
    slot = trainer * capacity + position
    placing = ones_where(iota((slots, samples), 0) == slot)
    out_ref[...] = lax.dot_general(placing, payload, NT, preferred_element_type=F32).astype(BF16)


def pack(velocity, halos, cells, trainer, tail, trainers, slots):
    total = halos[-1].shape[1]
    samples = cells.shape[1]
    return pl.pallas_call(
        functools.partial(pack_kernel, trainers=trainers),
        out_shape=jax.ShapeDtypeStruct((slots, WIDE), BF16),
        in_specs=whole(10),
        out_specs=pl.BlockSpec(memory_space=pltpu.VMEM),
        scratch_shapes=[
            pltpu.VMEM((total, 3 * samples), F32),
            pltpu.VMEM((81 * 8, samples), F32),
        ],
        compiler_params=params(),
        name="pack",
    )(velocity, *halos, cells, trainer, tail)


def advance_kernel(v_ref, xlo_ref, xhi_ref, ylo_ref, yhi_ref, zlo_ref, zhi_ref, out_ref, ends):
    comps, size_x, size_y, size_z = v_ref.shape
    rows = comps * size_x * size_y
    side = iota((8, rows), 0)
    faces = jnp.where(
        side == 0, zlo_ref[:, :rows], jnp.where(side == 1, zhi_ref[:, :rows], 0.0)
    )
    row = iota((8, size_z), 0)
    lane = iota((8, size_z), 1)
    place = jnp.where(
        ((row == 0) & (lane == 0)) | ((row == 1) & (lane == size_z - 1)), 1.0, 0.0
    ).astype(F32)
    ends[...] = lax.dot_general(faces, place, TN, precision=EXACT, preferred_element_type=F32)
    y_at = iota((size_y, size_z), 0)
    z_at = iota((size_y, size_z), 1)

    def plane(c, x):
        if x < 0:
            return xlo_ref[c]
        if x >= size_x:
            return xhi_ref[c]
        return v_ref[c, x]

    for x in range(size_x):
        here = [plane(c, x) for c in range(comps)]
        after = [plane(c, x + 1) for c in range(comps)]
        prior = [plane(c, x - 1) for c in range(comps)]
        y_up, y_down, z_up, z_down = [], [], [], []
        for c in range(comps):
            first = (c * size_x + x) * size_y
            closing = ends[first : first + size_y, :]
            y_up.append(
                jnp.where(
                    y_at == size_y - 1,
                    yhi_ref[c, x + 1 : x + 2, :],
                    pltpu.roll(here[c], size_y - 1, 0),
                )
            )
            y_down.append(
                jnp.where(y_at == 0, ylo_ref[c, x + 1 : x + 2, :], pltpu.roll(here[c], 1, 0))
            )
            z_up.append(jnp.where(z_at == size_z - 1, closing, pltpu.roll(here[c], size_z - 1, 1)))
            z_down.append(jnp.where(z_at == 0, closing, pltpu.roll(here[c], 1, 1)))
        for c in range(comps):
            diverge = after[c] * after[0] - prior[c] * prior[0]
            diverge = diverge + y_up[c] * y_up[1] - y_down[c] * y_down[1]
            diverge = diverge + z_up[c] * z_up[2] - z_down[c] * z_down[2]
            beside = after[c] + prior[c]
            beside = beside + y_up[c] + y_down[c]
            beside = beside + z_up[c] + z_down[c]
            tendency = -0.5 * diverge + VISCOSITY * (beside - 6.0 * here[c])
            out_ref[c, x] = here[c] + DT_STEP * tendency


def advance(velocity, halos):
    comps, size_x, size_y, size_z = velocity.shape
    return pl.pallas_call(
        advance_kernel,
        out_shape=jax.ShapeDtypeStruct(velocity.shape, F32),
        in_specs=whole(7),
        out_specs=pl.BlockSpec(memory_space=pltpu.VMEM),
        scratch_shapes=[pltpu.VMEM((comps * size_x * size_y, size_z), F32)],
        compiler_params=params(),
        name="advance",
    )(velocity, *halos)


def turn_kernel(in_ref, out_ref):
    shape = (out_ref.shape[0], in_ref.shape[1])
    eye = ones_where(iota(shape, 0) == iota(shape, 1))
    out_ref[...] = lax.dot_general(eye, in_ref[...], NT, preferred_element_type=F32).astype(BF16)


def turn(arrived):
    return pl.pallas_call(
        turn_kernel,
        out_shape=jax.ShapeDtypeStruct((ROWS, arrived.shape[0]), BF16),
        in_specs=whole(1),
        out_specs=pl.BlockSpec(memory_space=pltpu.VMEM),
        compiler_params=params(),
        name="turn",
    )(arrived)


def lane_sum(value):
    total = value[:, :WIDE]
    for k in range(1, value.shape[1] // WIDE):
        total = total + value[:, k * WIDE : (k + 1) * WIDE]
    return total


def train_kernel(*refs, planes, row_count, first, last, own_rows):
    refs = list(refs)
    take = lambda n: [refs.pop(0) for _ in range(n)]
    own_ref = take(1)[0]
    x_refs = take(len(planes))
    w1_ref, w2_ref, w2t_ref, w3_ref, w3t_ref, bias_ref, bias3_ref = take(7)
    held = [] if first else take(6)
    if last:
        momentum_ref, master_ref = take(2)
        first_ref, last_ref, bias_grads_ref, master_new_ref, momentum_new_ref = take(5)
        sums = take(6)
    else:
        sums = take(6)
    if first:
        loss_ref = take(1)[0]
    back_two_ref = take(1)[0]
    g1, g2, g3, s1, s2, s3 = sums
    hidden = w2_ref.shape[0]
    factor = 2.0 / (6.0 * row_count)
    if first:
        for ref in sums:
            ref[...] = jnp.zeros_like(ref)
    else:
        for ref, old in zip(sums, held):
            ref[...] = old[...]
    own = pl.multiple_of(own_ref[0] * own_rows, own_rows)

    def plane(x):
        slots = x.shape[1]
        reps = slots // WIDE
        spread = lambda b: jnp.concatenate([b] * reps, axis=1)
        act_one = jnp.tanh(
            jnp.dot(w1_ref[...], x, preferred_element_type=F32) + spread(bias_ref[:hidden, :])
        ).astype(BF16)
        act_two = jnp.tanh(
            jnp.dot(w2_ref[...], act_one, preferred_element_type=F32) + spread(bias_ref[hidden:, :])
        ).astype(BF16)
        ending = x[ROWS - 16 :, :].astype(F32)[8:, :]
        predicted = jnp.dot(w3_ref[...], act_two, preferred_element_type=F32)[:8, :]
        predicted = predicted + spread(bias3_ref[...])
        mismatch = jnp.where(
            iota((8, slots), 0) < 6, (predicted - ending) * ending[6:7, :], 0.0
        )
        delta_three = mismatch * factor
        back_three = jnp.concatenate([delta_three, jnp.zeros_like(delta_three)], axis=0).astype(BF16)
        g3[...] += lax.dot_general(back_three, act_two, NT, preferred_element_type=F32)
        wide_two = act_two.astype(F32)
        delta_two = jnp.dot(w3t_ref[...], back_three, preferred_element_type=F32) * (
            1.0 - wide_two * wide_two
        )
        s2[...] += lane_sum(delta_two)
        back_two = delta_two.astype(BF16)
        back_two_ref[...] = back_two
        g2[...] += lax.dot_general(
            back_two_ref[pl.ds(own, own_rows), :], act_one, NT, preferred_element_type=F32
        )
        wide_one = act_one.astype(F32)
        delta_one = jnp.dot(w2t_ref[...], back_two, preferred_element_type=F32) * (
            1.0 - wide_one * wide_one
        )
        s1[...] += lane_sum(delta_one)
        g1[...] += lax.dot_general(delta_one.astype(BF16), x, NT, preferred_element_type=F32)
        s3[...] += lane_sum(delta_three)
        return mismatch

    for ref, count in zip(x_refs, planes):
        if count == 1:
            mismatch = plane(ref[0] if len(ref.shape) == 3 else ref[...])
        else:

            @pl.loop(0, count)
            def _(k):
                plane(ref[k])

    if first:
        row_loss = jnp.sum(mismatch * mismatch, axis=0, keepdims=True) / (6.0 * row_count)
        loss_ref[...] = jnp.sum(row_loss, axis=1, keepdims=True)
    if last:
        first_ref[...] = g1[...][:, : first_ref.shape[1]]
        last_ref[...] = g3[...][: last_ref.shape[0], :]
        ones = jnp.ones((8, WIDE), F32)
        across = lambda s: lax.dot_general(ones, s, NT, precision=EXACT, preferred_element_type=F32)
        bias_grads_ref[:, :hidden] = across(s1[...])[0:1]
        bias_grads_ref[:, hidden : 2 * hidden] = across(s2[...])[0:1]
        third = across(jnp.concatenate([s3[...], jnp.zeros((WIDE - 8, WIDE), F32)], axis=0))
        bias_grads_ref[:, 2 * hidden :] = third[0:1, :6]
        grads = g2[...]
        per_row = hidden // WIDE
        for k in range(per_row):
            at = pl.ds(k, own_rows, stride=per_row)
            momentum = MOMENTUM_KEEP * momentum_ref[at, :] + grads[:, k * WIDE : (k + 1) * WIDE]
            momentum_new_ref[at, :] = momentum
            master_new_ref[at, :] = master_ref[at, :] - LEARN_RATE * momentum


def train(xs, own, weights, held, optimizer, row_count, own_rows):
    planes = tuple(x.shape[0] if x.ndim == 3 else 1 for x in xs)
    slots = xs[0].shape[-1]
    hidden = weights[1].shape[0]
    first, last = held is None, optimizer is not None
    sums = [
        jax.ShapeDtypeStruct(s, F32)
        for s in (
            (hidden, ROWS),
            (own_rows, hidden),
            (16, hidden),
            (hidden, WIDE),
            (hidden, WIDE),
            (8, WIDE),
        )
    ]
    scratch = [pltpu.VMEM((hidden, slots), BF16)]
    if last:
        out = [
            jax.ShapeDtypeStruct(s, F32)
            for s in (
                (hidden, 81),
                (6, hidden),
                (1, 2 * hidden + 6),
                optimizer[0].shape,
                optimizer[0].shape,
            )
        ]
        scratch = [pltpu.VMEM(s.shape, F32) for s in sums] + scratch
    else:
        out = list(sums)
    if first:
        out.append(jax.ShapeDtypeStruct((1, 1), F32))
    operands = [*xs, *weights, *(held or ()), *(optimizer or ())]
    count = sum(planes)
    return pl.pallas_call(
        functools.partial(
            train_kernel,
            planes=planes,
            row_count=row_count,
            first=first,
            last=last,
            own_rows=own_rows,
        ),
        out_shape=tuple(out),
        in_specs=[pl.BlockSpec(memory_space=pltpu.SMEM)] + whole(len(operands)),
        out_specs=tuple(whole(len(out))),
        scratch_shapes=scratch,
        compiler_params=params(),
        cost_estimate=pl.CostEstimate(
            flops=count * 1_400_000_000, bytes_accessed=3_000_000, transcendentals=0
        ),
        name="train",
    )(own, *operands)


def on_device(
    velocity,
    sample_cells,
    trainer_of,
    targets,
    w_first,
    w_middle,
    w_last,
    biases,
    middle_master,
    middle_momentum,
):
    comps, size_x, size_y, size_z = velocity.shape
    samples = sample_cells.shape[0]
    trainers = lax.axis_size("gx") * lax.axis_size("gy")
    capacity = 2 * samples // trainers
    slots = trainers * capacity
    hidden = w_middle.shape[1]
    planes = lax.axis_size("gz")
    own_rows = hidden // planes

    forward, backward = shifts("gx")
    xlo = lax.ppermute(velocity[:, size_x - 1], "gx", forward)
    xhi = lax.ppermute(velocity[:, 0], "gx", backward)
    to_low, to_high = y_faces(velocity, xlo, xhi)
    forward, backward = shifts("gy")
    ylo = lax.ppermute(to_high, "gy", forward)
    yhi = lax.ppermute(to_low, "gy", backward)
    total = comps * (size_x * size_y + 2 * size_y + 2 * 16)
    to_low, to_high = z_faces(velocity, xlo, xhi, ylo, yhi, total)
    forward, backward = shifts("gz")
    zlo = lax.ppermute(to_high, "gz", forward)
    zhi = lax.ppermute(to_low, "gz", backward)
    halos = (xlo, xhi, ylo, yhi, zlo, zhi)

    tail = jnp.concatenate(
        [targets.astype(F32), jnp.ones((1, samples), F32), jnp.zeros((1, samples), F32)], axis=0
    )
    packed = pack(
        velocity,
        halos,
        sample_cells.reshape(1, samples),
        trainer_of.reshape(1, samples),
        tail,
        trainers,
        slots,
    )
    arrived = lax.all_to_all(
        packed.reshape(trainers, capacity, WIDE),
        ("gx", "gy"),
        split_axis=0,
        concat_axis=0,
        tiled=True,
    ).reshape(slots, WIDE)
    new_velocity = advance(velocity, halos)

    feats = w_first.shape[2]
    w1 = jnp.pad(w_first[0], ((0, 0), (0, ROWS - feats)))
    w2 = w_middle[0]
    w3 = jnp.pad(w_last[0], ((0, 16 - w_last.shape[1]), (0, 0)))
    bias = jnp.broadcast_to(biases[0, : 2 * hidden, None], (2 * hidden, WIDE))
    bias3 = jnp.broadcast_to(
        jnp.pad(biases[0, 2 * hidden :], (0, 8 - w_last.shape[1]))[:, None], (8, WIDE)
    )
    weights = (w1, w2, w2.T, w3, w3.T, bias, bias3)
    own = lax.axis_index("gz").astype(I32).reshape(1)
    optimizer = (
        middle_momentum.reshape(-1, WIDE),
        middle_master.reshape(-1, WIDE),
    )

    mine = turn(arrived)
    pair = [(i, i ^ 1) for i in range(planes)]
    beside = lax.ppermute(mine, "gz", pair)
    both = jnp.stack([mine, beside])
    others = [
        lax.ppermute(both, "gz", [(i, (i + 2 * k) % planes) for i in range(planes)])
        for k in range(1, planes // 2)
    ]
    call = functools.partial(train, own=own, weights=weights, row_count=samples, own_rows=own_rows)
    *held, loss = call([mine], held=None, optimizer=None)
    held = call([beside], held=held, optimizer=None)
    held = call(others[:1], held=held, optimizer=None)
    first_grads, last_grads, bias_grads, master_new, momentum_new = call(
        others[1:], held=held, optimizer=optimizer
    )
    return (
        new_velocity,
        loss.reshape(1, 1, 1),
        first_grads[None],
        last_grads[None],
        bias_grads,
        master_new.reshape(middle_master.shape),
        momentum_new.reshape(middle_momentum.shape),
    )


def solution(mesh):
    placed = (
        P(None, "gx", "gy", "gz"),
        P(("gx", "gy", "gz")),
        P(("gx", "gy", "gz"), None),
        P(None, ("gx", "gy", "gz")),
        P(("gx", "gy"), None, None),
        P(("gx", "gy"), None, None),
        P(("gx", "gy"), None, None),
        P(("gx", "gy"), None),
        P(("gx", "gy"), "gz"),
        P(("gx", "gy"), "gz"),
    )
    return jax.shard_map(
        on_device,
        mesh=mesh,
        in_specs=placed,
        out_specs=(
            P(None, "gx", "gy", "gz"),
            P("gx", "gy", "gz"),
            P(("gx", "gy"), None, None),
            P(("gx", "gy"), None, None),
            P(("gx", "gy"), None),
            P(("gx", "gy"), "gz"),
            P(("gx", "gy"), "gz"),
        ),
        check_vma=False,
    )
```

```python
import functools

import jax
import jax.numpy as jnp
from jax import lax
from jax.experimental import pallas as pl
from jax.experimental.pallas import tpu as pltpu
from jax.sharding import PartitionSpec as P

DT_STEP = 0.1
VISCOSITY = 0.2
LEARN_RATE = 0.05
MOMENTUM_KEEP = 0.9

BF16 = jnp.bfloat16
F32 = jnp.float32
I32 = jnp.int32
NT = (((1,), (1,)), ((), ()))
TN = (((0,), (0,)), ((), ()))
EXACT = lax.Precision.HIGHEST
VMEM_LIMIT = 48 * 1024 * 1024
ROWS = 96
TAIL = 88
WIDE = 128
PAD_X = 16


def params(limit=VMEM_LIMIT):
    return pltpu.CompilerParams(vmem_limit_bytes=limit)


def cost(micros):
    return pl.CostEstimate(
        flops=int(micros * 800_000_000), bytes_accessed=1_000_000, transcendentals=0
    )


def inside(axis):
    at = lax.axis_index(axis)
    return (
        jnp.where(at > 0, 1.0, 0.0).astype(F32),
        jnp.where(at < lax.axis_size(axis) - 1, 1.0, 0.0).astype(F32),
    )


def whole(count):
    return [pl.BlockSpec(memory_space=pltpu.VMEM)] * count


def iota(shape, dim):
    return lax.broadcasted_iota(I32, shape, dim)


def ones_where(mask):
    return jnp.where(mask, 1.0, 0.0).astype(BF16)


def shifts(axis):
    count = lax.axis_size(axis)
    forward = [(i, (i + 1) % count) for i in range(count)]
    return forward, [(b, a) for a, b in forward]


def end_rows(block, low_ref, high_ref, row_of, size_y):
    size_z = block.shape[1]
    row, lane = iota((8, size_z), 0), iota((8, size_z), 1)
    pick = jnp.where(
        ((row == 0) & (lane == 0)) | ((row == 1) & (lane == size_z - 1)), 1.0, 0.0
    ).astype(F32)
    ends = lax.dot_general(pick, block, NT, precision=EXACT, preferred_element_type=F32)
    for k in range(block.shape[0] // size_y):
        at = row_of(k)
        low_ref[at : at + 1, 1 : size_y + 1] = ends[0:1, k * size_y : (k + 1) * size_y]
        high_ref[at : at + 1, 1 : size_y + 1] = ends[1:2, k * size_y : (k + 1) * size_y]


def plan_kernel(
    v_ref, trainer_ref, y_low_ref, y_high_ref, z_low_ref, z_high_ref, placing_ref, *, trainers
):
    comps, size_x, size_y, size_z = v_ref.shape
    for ref in (y_low_ref, y_high_ref, z_low_ref, z_high_ref):
        ref[...] = jnp.zeros_like(ref)
    for c in range(comps):
        for x in range(size_x):
            y_low_ref[c, x + 1 : x + 2, :] = v_ref[c, x, 0:1, :]
            y_high_ref[c, x + 1 : x + 2, :] = v_ref[c, x, size_y - 1 : size_y, :]
    end_rows(
        v_ref[...].reshape(-1, size_z),
        z_low_ref,
        z_high_ref,
        lambda k: k // size_x * PAD_X + k % size_x + 1,
        size_y,
    )

    trainer = trainer_ref[...]
    samples = trainer.shape[1]
    slots = placing_ref.shape[0]
    capacity = slots // trainers
    same = iota((trainers, samples), 0) == trainer
    earlier = ones_where(iota((samples, samples), 0) < iota((samples, samples), 1))
    before = jnp.dot(ones_where(same), earlier, preferred_element_type=F32)
    position = jnp.sum(jnp.where(same, before, 0.0), axis=0, keepdims=True).astype(I32)
    slot = trainer * capacity + position
    placing_ref[...] = ones_where(iota((slots, samples), 0) == slot)


def plan(velocity, trainer, trainers, slots):
    comps, size_x, size_y, size_z = velocity.shape
    y_face = jax.ShapeDtypeStruct((comps, PAD_X, size_z), F32)
    z_face = jax.ShapeDtypeStruct((comps * PAD_X, WIDE), F32)
    placing = jax.ShapeDtypeStruct((slots, trainer.shape[1]), BF16)
    return pl.pallas_call(
        functools.partial(plan_kernel, trainers=trainers),
        out_shape=(y_face, y_face, z_face, z_face, placing),
        in_specs=whole(2),
        out_specs=tuple(whole(5)),
        compiler_params=params(),
        cost_estimate=cost(1.5),
        name="plan",
    )(velocity, trainer)


def y_faces_kernel(low_ref, high_ref, xlo_ref, xhi_ref, to_low_ref, to_high_ref, *, size_x):
    before, after = inside("gx")
    last = xlo_ref.shape[1] - 1
    for own, to, y in ((low_ref, to_low_ref, 0), (high_ref, to_high_ref, last)):
        to[...] = own[...]
        for c in range(to.shape[0]):
            to[c, 0:1, :] = xlo_ref[c, y : y + 1, :] * before
            to[c, size_x + 1 : size_x + 2, :] = xhi_ref[c, y : y + 1, :] * after


def y_faces(low, high, xlo, xhi, size_x):
    return pl.pallas_call(
        functools.partial(y_faces_kernel, size_x=size_x),
        out_shape=tuple([jax.ShapeDtypeStruct(low.shape, F32)] * 2),
        in_specs=whole(4),
        out_specs=tuple(whole(2)),
        compiler_params=params(),
        cost_estimate=cost(0.3),
        name="y_faces",
    )(low, high, xlo, xhi)


def z_faces_kernel(
    low_ref, high_ref, x_low_ref, x_high_ref, ylo_ref, yhi_ref, to_low_ref, to_high_ref, *, size_y
):
    before, after = inside("gy")
    size_z = ylo_ref.shape[2]
    ylo = ylo_ref[...].reshape(-1, size_z) * before
    yhi = yhi_ref[...].reshape(-1, size_z) * after
    lane = iota(low_ref.shape, 1)
    for own, x, to, z in (
        (low_ref, x_low_ref, to_low_ref, 0),
        (high_ref, x_high_ref, to_high_ref, size_z - 1),
    ):
        face = own[...] + x[...]
        face = jnp.where(lane == 0, ylo[:, z : z + 1], face)
        to[...] = jnp.where(lane == size_y + 1, yhi[:, z : z + 1], face)


def z_faces(low, high, x_low, x_high, ylo, yhi, size_y):
    return pl.pallas_call(
        functools.partial(z_faces_kernel, size_y=size_y),
        out_shape=tuple([jax.ShapeDtypeStruct(low.shape, F32)] * 2),
        in_specs=whole(6),
        out_specs=tuple(whole(2)),
        compiler_params=params(),
        cost_estimate=cost(0.3),
        name="z_faces",
    )(low, high, x_low, x_high, ylo, yhi)


def split_cells(cells, size_x, size_y, size_z):
    return cells // (size_y * size_z), cells // size_z % size_y, cells % size_z


def depth_choice(cell_z, size_z):
    depth = iota((size_z, cell_z.shape[1]), 0)
    return jnp.concatenate([ones_where(depth == cell_z + (r - 1)) for r in range(3)], axis=1)


def fold(ref, first, rows, masks, samples):
    sums = [None] * 3
    for k in range(rows // 8):
        for r in range(3):
            piece = ref[first + 8 * k : first + 8 * k + 8, r * samples : (r + 1) * samples]
            piece = jnp.where(masks[k], piece, 0.0)
            sums[r] = piece if sums[r] is None else sums[r] + piece
    return sums


def feature(c, p, q, r):
    return 27 * c + 9 * p + 3 * q + r


def add_tiles(parts, feats):
    shape = (ROWS, feats * 8)
    gather = ones_where(lax.shift_right_logical(iota(shape, 1), 3) == iota(shape, 0))
    return jnp.dot(gather, parts[...].astype(BF16), preferred_element_type=F32)


def patch_kernel(
    v_ref, xlo_ref, xhi_ref, cells_ref, out_ref, z_low_ref, z_high_ref, picked, parts
):
    comps, size_x, size_y, size_z = v_ref.shape
    samples = cells_ref.shape[1]
    before, after = inside("gx")
    z_low_ref[...] = jnp.zeros_like(z_low_ref)
    z_high_ref[...] = jnp.zeros_like(z_high_ref)
    cell_x, cell_y, cell_z = split_cells(cells_ref[...], size_x, size_y, size_z)
    choose = depth_choice(cell_z, size_z)
    starts, start = [], 0
    for ref, scale, x in ((v_ref, None, 0), (xlo_ref, before, 0), (xhi_ref, after, size_x + 1)):
        block = ref[...].reshape(-1, size_z)
        if scale is not None:
            block = block * scale
            end_rows(block, z_low_ref, z_high_ref, lambda k: k * PAD_X + x, size_y)
        picked[start : start + block.shape[0], :] = jnp.dot(
            block.astype(BF16), choose, preferred_element_type=F32
        )
        starts.append(start)
        start += block.shape[0]
    sub = iota((8, samples), 0)
    at_x = [cell_x == j for j in range(size_x)]
    for c in range(comps):
        for q in range(3):
            masks = [sub + (8 * k - q + 1) == cell_y for k in range(size_y // 8)]
            totals = [[None] * 3 for _ in range(3)]
            for x in range(size_x + 2):
                if x == 0:
                    first = starts[1] + c * size_y
                elif x == size_x + 1:
                    first = starts[2] + c * size_y
                else:
                    first = (c * size_x + x - 1) * size_y
                sums = fold(picked, first, size_y, masks, samples)
                for p in range(3):
                    j = x - p
                    if 0 <= j < size_x:
                        for r in range(3):
                            piece = jnp.where(at_x[j], sums[r], 0.0)
                            totals[p][r] = piece if totals[p][r] is None else totals[p][r] + piece
            for p in range(3):
                for r in range(3):
                    f = feature(c, p, q, r)
                    parts[f * 8 : (f + 1) * 8, :] = totals[p][r]
    out_ref[...] = add_tiles(parts, 27 * comps)


def patches(velocity, xlo, xhi, cells, z_face):
    comps, size_x, size_y, size_z = velocity.shape
    samples = cells.shape[1]
    face = jax.ShapeDtypeStruct(z_face.shape, F32)
    return pl.pallas_call(
        patch_kernel,
        out_shape=(jax.ShapeDtypeStruct((ROWS, samples), F32), face, face),
        in_specs=whole(4),
        out_specs=tuple(whole(3)),
        scratch_shapes=[
            pltpu.VMEM((comps * (size_x + 2) * size_y, 3 * samples), F32),
            pltpu.VMEM((27 * comps * 8, samples), F32),
        ],
        compiler_params=params(),
        cost_estimate=cost(2.5),
        name="patches",
    )(velocity, xlo, xhi, cells)


def pack_kernel(
    own_ref,
    ylo_ref,
    yhi_ref,
    zlo_ref,
    zhi_ref,
    cells_ref,
    tail_ref,
    placing_ref,
    out_ref,
    picked,
    parts,
    *,
    size_x,
    size_y,
):
    comps, pad_x, size_z = ylo_ref.shape
    samples = cells_ref.shape[1]
    rows = comps * pad_x
    cell_x, cell_y, cell_z = split_cells(cells_ref[...], size_x, size_y, size_z)
    y_before, y_after = inside("gy")
    z_before, z_after = inside("gz")

    choose = depth_choice(cell_z, size_z)
    along_y = jnp.concatenate(
        [ylo_ref[...].reshape(rows, size_z) * y_before, yhi_ref[...].reshape(rows, size_z) * y_after],
        axis=0,
    ).astype(BF16)
    picked[: 2 * rows, :] = jnp.dot(along_y, choose, preferred_element_type=F32)
    width = iota((WIDE, samples), 0)
    choose = jnp.concatenate([ones_where(width == cell_y + q) for q in range(3)], axis=1)
    along_z = jnp.concatenate([zlo_ref[...] * z_before, zhi_ref[...] * z_after], axis=0).astype(BF16)
    picked[2 * rows :, :] = jnp.dot(along_z, choose, preferred_element_type=F32)

    sub = iota((8, samples), 0)
    at_edge = [cell_y == 0, cell_y == size_y - 1, cell_z == 0, cell_z == size_z - 1]
    edge_x = [jnp.where(at, cell_x, -100) for at in at_edge]
    for c in range(comps):
        for p in range(3):
            sums = [
                fold(
                    picked,
                    e * rows + c * pad_x,
                    pad_x,
                    [sub + (8 * k - p) == edge_x[e] for k in range(pad_x // 8)],
                    samples,
                )
                for e in range(4)
            ]
            for q in range(3):
                for r in range(3):
                    terms = []
                    if q != 1:
                        terms.append(sums[q // 2][r])
                    if r != 1:
                        terms.append(sums[2 + r // 2][q])
                    total = terms[0] if terms else jnp.zeros((8, samples), F32)
                    if len(terms) > 1:
                        total = total + terms[1]
                    f = feature(c, p, q, r)
                    parts[f * 8 : (f + 1) * 8, :] = total

    features = own_ref[...] + add_tiles(parts, 27 * comps)
    payload = jnp.concatenate(
        [features[:TAIL], tail_ref[...], jnp.zeros((WIDE - ROWS, samples), F32)], axis=0
    ).astype(BF16)
    out_ref[...] = lax.dot_general(
        placing_ref[...], payload, NT, preferred_element_type=F32
    ).astype(BF16)


def pack(own, ylo, yhi, zlo, zhi, cells, tail, placing, size_x, size_y):
    samples = cells.shape[1]
    comps, pad_x, _ = ylo.shape
    return pl.pallas_call(
        functools.partial(pack_kernel, size_x=size_x, size_y=size_y),
        out_shape=jax.ShapeDtypeStruct((placing.shape[0], WIDE), BF16),
        in_specs=whole(8),
        out_specs=pl.BlockSpec(memory_space=pltpu.VMEM),
        scratch_shapes=[
            pltpu.VMEM((4 * comps * pad_x, 3 * samples), F32),
            pltpu.VMEM((27 * comps * 8, samples), F32),
        ],
        compiler_params=params(),
        cost_estimate=cost(1.0),
        name="pack",
    )(own, ylo, yhi, zlo, zhi, cells, tail, placing)


def advance_kernel(v_ref, xlo_ref, xhi_ref, ylo_ref, yhi_ref, zlo_ref, zhi_ref, out_ref):
    comps, size_x, size_y, size_z = v_ref.shape
    x_before, x_after = inside("gx")
    y_before, y_after = inside("gy")
    z_before, z_after = inside("gz")

    def columns(ref, scale):
        face = ref[...] * scale
        face = jnp.concatenate([face, jnp.zeros((WIDE - face.shape[0], WIDE), F32)], axis=0)
        return pltpu.roll(face.T, WIDE - 1, 0)[:size_y, :]

    z_low, z_high = columns(zlo_ref, z_before), columns(zhi_ref, z_after)
    y_at = iota((size_y, size_z), 0)
    z_at = iota((size_y, size_z), 1)

    def plane(c, x):
        if x < 0:
            return xlo_ref[c] * x_before
        if x >= size_x:
            return xhi_ref[c] * x_after
        return v_ref[c, x]

    for x in range(size_x):
        here = [plane(c, x) for c in range(comps)]
        after = [plane(c, x + 1) for c in range(comps)]
        prior = [plane(c, x - 1) for c in range(comps)]
        y_up, y_down, z_up, z_down = [], [], [], []
        for c in range(comps):
            at = c * PAD_X + x + 1
            above = yhi_ref[c, x + 1 : x + 2, :] * y_after
            below = ylo_ref[c, x + 1 : x + 2, :] * y_before
            y_up.append(jnp.where(y_at == size_y - 1, above, pltpu.roll(here[c], size_y - 1, 0)))
            y_down.append(jnp.where(y_at == 0, below, pltpu.roll(here[c], 1, 0)))
            z_up.append(
                jnp.where(z_at == size_z - 1, z_high[:, at : at + 1], pltpu.roll(here[c], size_z - 1, 1))
            )
            z_down.append(jnp.where(z_at == 0, z_low[:, at : at + 1], pltpu.roll(here[c], 1, 1)))
        for c in range(comps):
            diverge = after[c] * after[0] - prior[c] * prior[0]
            diverge = diverge + y_up[c] * y_up[1] - y_down[c] * y_down[1]
            diverge = diverge + z_up[c] * z_up[2] - z_down[c] * z_down[2]
            beside = after[c] + prior[c]
            beside = beside + y_up[c] + y_down[c]
            beside = beside + z_up[c] + z_down[c]
            tendency = -0.5 * diverge + VISCOSITY * (beside - 6.0 * here[c])
            out_ref[c, x] = here[c] + DT_STEP * tendency


def advance(velocity, halos):
    return pl.pallas_call(
        advance_kernel,
        out_shape=jax.ShapeDtypeStruct(velocity.shape, F32),
        in_specs=whole(7),
        out_specs=pl.BlockSpec(memory_space=pltpu.VMEM),
        compiler_params=params(),
        cost_estimate=cost(1.5),
        name="advance",
    )(velocity, *halos)


def turn_kernel(in_ref, out_ref):
    shape = (out_ref.shape[0], in_ref.shape[1])
    eye = ones_where(iota(shape, 0) == iota(shape, 1))
    out_ref[...] = lax.dot_general(eye, in_ref[...], NT, preferred_element_type=F32).astype(BF16)


def turn(arrived):
    return pl.pallas_call(
        turn_kernel,
        out_shape=jax.ShapeDtypeStruct((ROWS, arrived.shape[0]), BF16),
        in_specs=whole(1),
        out_specs=pl.BlockSpec(memory_space=pltpu.VMEM),
        compiler_params=params(),
        cost_estimate=cost(0.2),
        name="turn",
    )(arrived)


def lane_sum(value):
    total = value[:, :WIDE]
    for k in range(1, value.shape[1] // WIDE):
        total = total + value[:, k * WIDE : (k + 1) * WIDE]
    return total


def train_kernel(*refs, planes, row_count, first, last, own_rows):
    refs = list(refs)
    take = lambda n: [refs.pop(0) for _ in range(n)]
    x_refs = take(len(planes))
    w1_ref, w2_ref, w2t_ref, w3_ref, w3t_ref, bias_ref, bias3_ref = take(7)
    held = [] if first else take(6)
    if last:
        momentum_ref, master_ref = take(2)
        first_ref, last_ref, bias_grads_ref, master_new_ref, momentum_new_ref = take(5)
        sums = take(6)
    else:
        sums = take(6)
    if first:
        loss_ref = take(1)[0]
    back_two_ref = take(1)[0]
    g1, g2, g3, s1, s2, s3 = sums
    hidden = w2_ref.shape[0]
    factor = 2.0 / (6.0 * row_count)
    if first:
        for ref in sums:
            ref[...] = jnp.zeros_like(ref)
    else:
        for ref, old in zip(sums, held):
            ref[...] = old[...]
    own = pl.multiple_of(lax.axis_index("gz") * own_rows, own_rows)

    def plane(x):
        slots = x.shape[1]
        reps = slots // WIDE
        spread = lambda b: jnp.concatenate([b] * reps, axis=1)
        act_one = jnp.tanh(
            jnp.dot(w1_ref[...], x, preferred_element_type=F32) + spread(bias_ref[:hidden, :])
        ).astype(BF16)
        act_two = jnp.tanh(
            jnp.dot(w2_ref[...], act_one, preferred_element_type=F32) + spread(bias_ref[hidden:, :])
        ).astype(BF16)
        ending = x[ROWS - 16 :, :].astype(F32)[8:, :]
        predicted = jnp.dot(w3_ref[...], act_two, preferred_element_type=F32)[:8, :]
        predicted = predicted + spread(bias3_ref[...])
        mismatch = jnp.where(
            iota((8, slots), 0) < 6, (predicted - ending) * ending[6:7, :], 0.0
        )
        delta_three = mismatch * factor
        back_three = jnp.concatenate([delta_three, jnp.zeros_like(delta_three)], axis=0).astype(BF16)
        g3[...] += lax.dot_general(back_three, act_two, NT, preferred_element_type=F32)
        wide_two = act_two.astype(F32)
        delta_two = jnp.dot(w3t_ref[...], back_three, preferred_element_type=F32) * (
            1.0 - wide_two * wide_two
        )
        s2[...] += lane_sum(delta_two)
        back_two = delta_two.astype(BF16)
        back_two_ref[...] = back_two
        g2[...] += lax.dot_general(
            back_two_ref[pl.ds(own, own_rows), :], act_one, NT, preferred_element_type=F32
        )
        wide_one = act_one.astype(F32)
        delta_one = jnp.dot(w2t_ref[...], back_two, preferred_element_type=F32) * (
            1.0 - wide_one * wide_one
        )
        s1[...] += lane_sum(delta_one)
        g1[...] += lax.dot_general(delta_one.astype(BF16), x, NT, preferred_element_type=F32)
        s3[...] += lane_sum(delta_three)
        return mismatch

    pieces = []
    for ref, count in zip(x_refs, planes):
        pieces += [ref[...]] if count == 1 else [ref[k] for k in range(count)]
    mismatch = plane(pieces[0] if len(pieces) == 1 else jnp.concatenate(pieces, axis=1))

    if first:
        row_loss = jnp.sum(mismatch * mismatch, axis=0, keepdims=True) / (6.0 * row_count)
        loss_ref[...] = jnp.sum(row_loss, axis=1, keepdims=True)
    if last:
        wide = jnp.concatenate([g1[...], jnp.zeros((hidden, WIDE - ROWS), F32)], axis=1)
        for ref, grads in ((first_ref, wide.T), (last_ref, g3[...])):
            for k in range(ref.shape[0]):
                ref[k] = grads[k : k + 1, :]
        ones = jnp.ones((8, WIDE), F32)
        across = lambda s: lax.dot_general(ones, s, NT, precision=EXACT, preferred_element_type=F32)
        bias_grads_ref[:, :hidden] = across(s1[...])[0:1]
        bias_grads_ref[:, hidden : 2 * hidden] = across(s2[...])[0:1]
        third = across(jnp.concatenate([s3[...], jnp.zeros((WIDE - 8, WIDE), F32)], axis=0))
        bias_grads_ref[:, 2 * hidden :] = third[0:1, :6]
        grads = g2[...]
        per_row = hidden // WIDE
        for k in range(per_row):
            at = pl.ds(k, own_rows, stride=per_row)
            momentum = MOMENTUM_KEEP * momentum_ref[at, :] + grads[:, k * WIDE : (k + 1) * WIDE]
            momentum_new_ref[at, :] = momentum
            master_new_ref[at, :] = master_ref[at, :] - LEARN_RATE * momentum


def train(xs, weights, held, optimizer, row_count, own_rows):
    planes = tuple(x.shape[0] if x.ndim == 3 else 1 for x in xs)
    slots = xs[0].shape[-1]
    hidden = weights[1].shape[0]
    first, last = held is None, optimizer is not None
    sums = [
        jax.ShapeDtypeStruct(s, F32)
        for s in (
            (hidden, ROWS),
            (own_rows, hidden),
            (16, hidden),
            (hidden, WIDE),
            (hidden, WIDE),
            (8, WIDE),
        )
    ]
    scratch = [pltpu.VMEM((hidden, slots * sum(planes)), BF16)]
    if last:
        out = [
            jax.ShapeDtypeStruct(s, F32)
            for s in (
                (81, 1, hidden),
                (6, 1, hidden),
                (1, 2 * hidden + 6),
                optimizer[0].shape,
                optimizer[0].shape,
            )
        ]
        scratch = [pltpu.VMEM(s.shape, F32) for s in sums] + scratch
    else:
        out = list(sums)
    if first:
        out.append(jax.ShapeDtypeStruct((1, 1), F32))
    operands = [*xs, *weights, *(held or ()), *(optimizer or ())]
    count = sum(planes)
    return pl.pallas_call(
        functools.partial(
            train_kernel,
            planes=planes,
            row_count=row_count,
            first=first,
            last=last,
            own_rows=own_rows,
        ),
        out_shape=tuple(out),
        in_specs=whole(len(operands)),
        out_specs=tuple(whole(len(out))),
        scratch_shapes=scratch,
        compiler_params=params(),
        cost_estimate=cost(1.6 * count),
        name="train",
    )(*operands)


def on_device(
    velocity,
    sample_cells,
    trainer_of,
    targets,
    w_first,
    w_middle,
    w_last,
    biases,
    middle_master,
    middle_momentum,
):
    comps, size_x, size_y, size_z = velocity.shape
    samples = sample_cells.shape[0]
    trainers = lax.axis_size("gx") * lax.axis_size("gy")
    capacity = 2 * samples // trainers
    slots = trainers * capacity
    hidden = w_middle.shape[1]
    planes = lax.axis_size("gz")
    own_rows = hidden // planes

    cells = sample_cells.reshape(1, samples)
    forward, backward = shifts("gx")
    xlo = lax.ppermute(velocity[:, size_x - 1], "gx", forward)
    xhi = lax.ppermute(velocity[:, 0], "gx", backward)
    y_low, y_high, z_low, z_high, placing = plan(
        velocity, trainer_of.reshape(1, samples), trainers, slots
    )
    y_low, y_high = y_faces(y_low, y_high, xlo, xhi, size_x)
    forward, backward = shifts("gy")
    ylo = lax.ppermute(y_high, "gy", forward)
    yhi = lax.ppermute(y_low, "gy", backward)
    features, x_low, x_high = patches(velocity, xlo, xhi, cells, z_low)
    z_low, z_high = z_faces(z_low, z_high, x_low, x_high, ylo, yhi, size_y)
    forward, backward = shifts("gz")
    zlo = lax.ppermute(z_high, "gz", forward)
    zhi = lax.ppermute(z_low, "gz", backward)
    tail = jnp.concatenate(
        [targets.astype(F32), jnp.ones((1, samples), F32), jnp.zeros((1, samples), F32)], axis=0
    )
    packed = pack(features, ylo, yhi, zlo, zhi, cells, tail, placing, size_x, size_y)
    arrived = lax.all_to_all(
        packed.reshape(trainers, capacity, WIDE),
        ("gx", "gy"),
        split_axis=0,
        concat_axis=0,
        tiled=True,
    ).reshape(slots, WIDE)
    new_velocity = advance(velocity, (xlo, xhi, ylo, yhi, zlo, zhi))

    feats = w_first.shape[2]
    w1 = jnp.pad(w_first[0], ((0, 0), (0, ROWS - feats)))
    w2 = w_middle[0]
    w3 = jnp.pad(w_last[0], ((0, 16 - w_last.shape[1]), (0, 0)))
    bias = jnp.broadcast_to(biases[0, : 2 * hidden, None], (2 * hidden, WIDE))
    bias3 = jnp.broadcast_to(
        jnp.pad(biases[0, 2 * hidden :], (0, 8 - w_last.shape[1]))[:, None], (8, WIDE)
    )
    weights = (w1, w2, w2.T, w3, w3.T, bias, bias3)
    optimizer = (
        middle_momentum.reshape(-1, WIDE),
        middle_master.reshape(-1, WIDE),
    )

    arrived, new_velocity = lax.optimization_barrier((arrived, new_velocity))
    mine = turn(arrived)
    call = functools.partial(train, weights=weights, row_count=samples, own_rows=own_rows)
    swap = [(i, i ^ 1) for i in range(planes)]
    move = lambda k: [(i, (i + k) % planes) for i in range(planes)]
    beside = lax.ppermute(mine, "gz", swap)
    far = lax.ppermute(mine, "gz", move(planes // 2))
    *held, loss = call([mine], held=None, optimizer=None)
    beside, far, *held = lax.optimization_barrier((beside, far, *held))
    both = jnp.stack([mine, beside])
    near = [lax.ppermute(both, "gz", move(k)) for k in (2, planes - 2)]
    far_beside = lax.ppermute(far, "gz", swap)
    held = call([beside, far], held=held, optimizer=None)
    first_grads, last_grads, bias_grads, master_new, momentum_new = call(
        [*near, far_beside], held=held, optimizer=optimizer
    )
    return (
        new_velocity,
        loss.reshape(1, 1, 1),
        first_grads.transpose(1, 2, 0),
        last_grads.transpose(1, 0, 2),
        bias_grads,
        master_new.reshape(middle_master.shape),
        momentum_new.reshape(middle_momentum.shape),
    )


def solution(mesh):
    placed = (
        P(None, "gx", "gy", "gz"),
        P(("gx", "gy", "gz")),
        P(("gx", "gy", "gz"), None),
        P(None, ("gx", "gy", "gz")),
        P(("gx", "gy"), None, None),
        P(("gx", "gy"), None, None),
        P(("gx", "gy"), None, None),
        P(("gx", "gy"), None),
        P(("gx", "gy"), "gz"),
        P(("gx", "gy"), "gz"),
    )
    return jax.shard_map(
        on_device,
        mesh=mesh,
        in_specs=placed,
        out_specs=(
            P(None, "gx", "gy", "gz"),
            P("gx", "gy", "gz"),
            P(("gx", "gy"), None, None),
            P(("gx", "gy"), None, None),
            P(("gx", "gy"), None),
            P(("gx", "gy"), "gz"),
            P(("gx", "gy"), "gz"),
        ),
        check_vma=False,
    )
```

```python
import functools

import jax
import jax.numpy as jnp
from jax import lax
from jax.experimental import pallas as pl
from jax.experimental.pallas import tpu as pltpu
from jax.sharding import PartitionSpec as P

DT_STEP = 0.1
VISCOSITY = 0.2
LEARN_RATE = 0.05
MOMENTUM_KEEP = 0.9

BF16 = jnp.bfloat16
F32 = jnp.float32
I32 = jnp.int32
NT = (((1,), (1,)), ((), ()))
TN = (((0,), (0,)), ((), ()))
EXACT = lax.Precision.HIGHEST
VMEM_LIMIT = 48 * 1024 * 1024
ROWS = 96
TAIL = 88
WIDE = 128
PAD_X = 16


def params(limit=VMEM_LIMIT):
    return pltpu.CompilerParams(vmem_limit_bytes=limit)


def cost(micros):
    return pl.CostEstimate(
        flops=int(micros * 800_000_000), bytes_accessed=1_000_000, transcendentals=0
    )


def inside(axis):
    at = lax.axis_index(axis)
    return (
        jnp.where(at > 0, 1.0, 0.0).astype(F32),
        jnp.where(at < lax.axis_size(axis) - 1, 1.0, 0.0).astype(F32),
    )


def whole(count):
    return [pl.BlockSpec(memory_space=pltpu.VMEM)] * count


def iota(shape, dim):
    return lax.broadcasted_iota(I32, shape, dim)


def ones_where(mask):
    return jnp.where(mask, 1.0, 0.0).astype(BF16)


def exchange(axis, low_face, high_face):
    count = lax.axis_size(axis)
    forward = [(i, (i + 1) % count) for i in range(count)]
    backward = [(b, a) for a, b in forward]
    return lax.ppermute(high_face, axis, forward), lax.ppermute(low_face, axis, backward)


def faces_kernel(low_ref, high_ref, to_low_ref, to_high_ref):
    to_low_ref[...] = low_ref[:, 0]
    to_high_ref[...] = high_ref[:, 0]


def x_faces(velocity):
    comps, size_x, size_y, size_z = velocity.shape
    spec = lambda at: pl.BlockSpec((comps, 1, size_y, size_z), lambda i: (0, at, 0, 0))
    out = pl.BlockSpec((comps, size_y, size_z), lambda i: (0, 0, 0))
    return pl.pallas_call(
        faces_kernel,
        grid=(1,),
        out_shape=tuple([jax.ShapeDtypeStruct((comps, size_y, size_z), F32)] * 2),
        in_specs=[spec(0), spec(size_x - 1)],
        out_specs=(out, out),
        compiler_params=params(),
        cost_estimate=cost(0.3),
        name="x_faces",
    )(velocity, velocity)


def end_rows(block, low_ref, high_ref, row_of, size_y):
    size_z = block.shape[1]
    row, lane = iota((8, size_z), 0), iota((8, size_z), 1)
    pick = jnp.where(
        ((row == 0) & (lane == 0)) | ((row == 1) & (lane == size_z - 1)), 1.0, 0.0
    ).astype(F32)
    ends = lax.dot_general(pick, block, NT, precision=EXACT, preferred_element_type=F32)
    for k in range(block.shape[0] // size_y):
        at = row_of(k)
        low_ref[at : at + 1, 1 : size_y + 1] = ends[0:1, k * size_y : (k + 1) * size_y]
        high_ref[at : at + 1, 1 : size_y + 1] = ends[1:2, k * size_y : (k + 1) * size_y]


def plan_kernel(
    v_ref, xlo_ref, xhi_ref, trainer_ref, z_low_ref, z_high_ref, placing_ref, *, trainers
):
    comps, size_x, size_y, size_z = v_ref.shape
    for ref in (z_low_ref, z_high_ref):
        ref[...] = jnp.zeros_like(ref)
    end_rows(
        v_ref[...].reshape(-1, size_z),
        z_low_ref,
        z_high_ref,
        lambda k: k // size_x * PAD_X + k % size_x + 1,
        size_y,
    )
    before, after = inside("gx")
    for ref, scale, x in ((xlo_ref, before, 0), (xhi_ref, after, size_x + 1)):
        block = ref[...].reshape(-1, size_z) * scale
        end_rows(block, z_low_ref, z_high_ref, lambda k: k * PAD_X + x, size_y)

    trainer = trainer_ref[...]
    samples = trainer.shape[1]
    slots = placing_ref.shape[0]
    capacity = slots // trainers
    same = iota((trainers, samples), 0) == trainer
    earlier = ones_where(iota((samples, samples), 0) < iota((samples, samples), 1))
    before = jnp.dot(ones_where(same), earlier, preferred_element_type=F32)
    position = jnp.sum(jnp.where(same, before, 0.0), axis=0, keepdims=True).astype(I32)
    slot = trainer * capacity + position
    placing_ref[...] = ones_where(iota((slots, samples), 0) == slot)


def plan(velocity, x_halos, trainer, trainers, slots):
    comps, size_x, size_y, size_z = velocity.shape
    z_face = jax.ShapeDtypeStruct((comps * PAD_X, WIDE), F32)
    placing = jax.ShapeDtypeStruct((slots, trainer.shape[1]), BF16)
    return pl.pallas_call(
        functools.partial(plan_kernel, trainers=trainers),
        out_shape=(z_face, z_face, placing),
        in_specs=whole(4),
        out_specs=tuple(whole(3)),
        compiler_params=params(),
        cost_estimate=cost(1.5),
        name="plan",
    )(velocity, *x_halos, trainer)


def y_faces_kernel(low_ref, high_ref, xlo_ref, xhi_ref, to_low_ref, to_high_ref):
    comps, size_x = low_ref.shape[0], low_ref.shape[1]
    before, after = inside("gx")
    last = xlo_ref.shape[1] - 1
    for to, own, row, y in ((to_low_ref, low_ref, 0, 0), (to_high_ref, high_ref, 7, last)):
        to[...] = jnp.zeros_like(to)
        for c in range(comps):
            to[c, 0:1, :] = xlo_ref[c, y : y + 1, :] * before
            for x in range(size_x):
                to[c, x + 1 : x + 2, :] = own[c, x, row : row + 1, :]
            to[c, size_x + 1 : size_x + 2, :] = xhi_ref[c, y : y + 1, :] * after


def y_faces(velocity, x_halos):
    comps, size_x, size_y, size_z = velocity.shape
    shape = (comps, PAD_X, size_z)
    spec = lambda at: pl.BlockSpec((comps, size_x, 8, size_z), lambda i: (0, 0, at, 0))
    full = lambda a: pl.BlockSpec(a, lambda i: (0,) * len(a))
    return pl.pallas_call(
        y_faces_kernel,
        grid=(1,),
        out_shape=tuple([jax.ShapeDtypeStruct(shape, F32)] * 2),
        in_specs=[spec(0), spec(size_y // 8 - 1)] + [full(x_halos[0].shape)] * 2,
        out_specs=(full(shape), full(shape)),
        compiler_params=params(),
        cost_estimate=cost(0.3),
        name="y_faces",
    )(velocity, velocity, *x_halos)


def z_faces_kernel(low_ref, high_ref, ylo_ref, yhi_ref, to_low_ref, to_high_ref, *, size_y):
    before, after = inside("gy")
    size_z = ylo_ref.shape[2]
    ylo = ylo_ref[...].reshape(-1, size_z) * before
    yhi = yhi_ref[...].reshape(-1, size_z) * after
    lane = iota(low_ref.shape, 1)
    for own, to, z in ((low_ref, to_low_ref, 0), (high_ref, to_high_ref, size_z - 1)):
        face = jnp.where(lane == 0, ylo[:, z : z + 1], own[...])
        to[...] = jnp.where(lane == size_y + 1, yhi[:, z : z + 1], face)


def z_faces(low, high, y_halos, size_y):
    return pl.pallas_call(
        functools.partial(z_faces_kernel, size_y=size_y),
        out_shape=tuple([jax.ShapeDtypeStruct(low.shape, F32)] * 2),
        in_specs=whole(4),
        out_specs=tuple(whole(2)),
        compiler_params=params(),
        cost_estimate=cost(0.3),
        name="z_faces",
    )(low, high, *y_halos)


def split_cells(cells, size_x, size_y, size_z):
    return cells // (size_y * size_z), cells // size_z % size_y, cells % size_z


def depth_choice(cell_z, size_z):
    depth = iota((size_z, cell_z.shape[1]), 0)
    return jnp.concatenate([ones_where(depth == cell_z + (r - 1)) for r in range(3)], axis=1)


def fold(ref, first, rows, masks, samples):
    sums = [None] * 3
    for k in range(rows // 8):
        for r in range(3):
            piece = ref[first + 8 * k : first + 8 * k + 8, r * samples : (r + 1) * samples]
            piece = jnp.where(masks[k], piece, 0.0)
            sums[r] = piece if sums[r] is None else sums[r] + piece
    return sums


def feature(c, p, q, r):
    return 27 * c + 9 * p + 3 * q + r


def add_tiles(parts, feats):
    shape = (ROWS, feats * 8)
    gather = ones_where(lax.shift_right_logical(iota(shape, 1), 3) == iota(shape, 0))
    return jnp.dot(gather, parts[...].astype(BF16), preferred_element_type=F32)


def patch_kernel(
    v_ref, xlo_ref, xhi_ref, cells_ref, after_ref, out_ref, picked, parts
):
    comps, size_x, size_y, size_z = v_ref.shape
    samples = cells_ref.shape[1]
    before, after = inside("gx")
    cell_x, cell_y, cell_z = split_cells(cells_ref[...], size_x, size_y, size_z)
    choose = depth_choice(cell_z, size_z)
    starts, start = [], 0
    for ref, scale in ((v_ref, None), (xlo_ref, before), (xhi_ref, after)):
        block = ref[...].reshape(-1, size_z)
        if scale is not None:
            block = block * scale
        picked[start : start + block.shape[0], :] = jnp.dot(
            block.astype(BF16), choose, preferred_element_type=F32
        )
        starts.append(start)
        start += block.shape[0]
    sub = iota((8, samples), 0)
    at_x = [cell_x == j for j in range(size_x)]
    for c in range(comps):
        for q in range(3):
            masks = [sub + (8 * k - q + 1) == cell_y for k in range(size_y // 8)]
            totals = [[None] * 3 for _ in range(3)]
            for x in range(size_x + 2):
                if x == 0:
                    first = starts[1] + c * size_y
                elif x == size_x + 1:
                    first = starts[2] + c * size_y
                else:
                    first = (c * size_x + x - 1) * size_y
                sums = fold(picked, first, size_y, masks, samples)
                for p in range(3):
                    j = x - p
                    if 0 <= j < size_x:
                        for r in range(3):
                            piece = jnp.where(at_x[j], sums[r], 0.0)
                            totals[p][r] = piece if totals[p][r] is None else totals[p][r] + piece
            for p in range(3):
                for r in range(3):
                    f = feature(c, p, q, r)
                    parts[f * 8 : (f + 1) * 8, :] = totals[p][r]
    out_ref[...] = add_tiles(parts, 27 * comps)


def patches(velocity, x_halos, cells, after):
    comps, size_x, size_y, size_z = velocity.shape
    samples = cells.shape[1]
    return pl.pallas_call(
        patch_kernel,
        out_shape=jax.ShapeDtypeStruct((ROWS, samples), F32),
        in_specs=whole(5),
        out_specs=pl.BlockSpec(memory_space=pltpu.VMEM),
        scratch_shapes=[
            pltpu.VMEM((comps * (size_x + 2) * size_y, 3 * samples), F32),
            pltpu.VMEM((27 * comps * 8, samples), F32),
        ],
        compiler_params=params(),
        cost_estimate=cost(2.5),
        name="patches",
    )(velocity, *x_halos, cells, after)


def pack_kernel(
    own_ref,
    ylo_ref,
    yhi_ref,
    zlo_ref,
    zhi_ref,
    cells_ref,
    tail_ref,
    placing_ref,
    out_ref,
    picked,
    parts,
    *,
    size_x,
    size_y,
):
    comps, pad_x, size_z = ylo_ref.shape
    samples = cells_ref.shape[1]
    rows = comps * pad_x
    cell_x, cell_y, cell_z = split_cells(cells_ref[...], size_x, size_y, size_z)
    y_before, y_after = inside("gy")
    z_before, z_after = inside("gz")

    choose = depth_choice(cell_z, size_z)
    along_y = jnp.concatenate(
        [ylo_ref[...].reshape(rows, size_z) * y_before, yhi_ref[...].reshape(rows, size_z) * y_after],
        axis=0,
    ).astype(BF16)
    picked[: 2 * rows, :] = jnp.dot(along_y, choose, preferred_element_type=F32)
    width = iota((WIDE, samples), 0)
    choose = jnp.concatenate([ones_where(width == cell_y + q) for q in range(3)], axis=1)
    along_z = jnp.concatenate([zlo_ref[...] * z_before, zhi_ref[...] * z_after], axis=0).astype(BF16)
    picked[2 * rows :, :] = jnp.dot(along_z, choose, preferred_element_type=F32)

    sub = iota((8, samples), 0)
    at_edge = [cell_y == 0, cell_y == size_y - 1, cell_z == 0, cell_z == size_z - 1]
    edge_x = [jnp.where(at, cell_x, -100) for at in at_edge]
    for c in range(comps):
        for p in range(3):
            sums = [
                fold(
                    picked,
                    e * rows + c * pad_x,
                    pad_x,
                    [sub + (8 * k - p) == edge_x[e] for k in range(pad_x // 8)],
                    samples,
                )
                for e in range(4)
            ]
            for q in range(3):
                for r in range(3):
                    terms = []
                    if q != 1:
                        terms.append(sums[q // 2][r])
                    if r != 1:
                        terms.append(sums[2 + r // 2][q])
                    total = terms[0] if terms else jnp.zeros((8, samples), F32)
                    if len(terms) > 1:
                        total = total + terms[1]
                    f = feature(c, p, q, r)
                    parts[f * 8 : (f + 1) * 8, :] = total

    features = own_ref[...] + add_tiles(parts, 27 * comps)
    payload = jnp.concatenate(
        [features[:TAIL], tail_ref[...], jnp.zeros((WIDE - ROWS, samples), F32)], axis=0
    ).astype(BF16)
    out_ref[...] = lax.dot_general(
        placing_ref[...], payload, NT, preferred_element_type=F32
    ).astype(BF16)


def pack(own, y_halos, z_halos, cells, tail, placing, size_x, size_y):
    samples = cells.shape[1]
    comps, pad_x, _ = y_halos[0].shape
    return pl.pallas_call(
        functools.partial(pack_kernel, size_x=size_x, size_y=size_y),
        out_shape=jax.ShapeDtypeStruct((placing.shape[0], WIDE), BF16),
        in_specs=whole(8),
        out_specs=pl.BlockSpec(memory_space=pltpu.VMEM),
        scratch_shapes=[
            pltpu.VMEM((4 * comps * pad_x, 3 * samples), F32),
            pltpu.VMEM((27 * comps * 8, samples), F32),
        ],
        compiler_params=params(),
        cost_estimate=cost(1.0),
        name="pack",
    )(own, *y_halos, *z_halos, cells, tail, placing)


def advance_kernel(
    v_ref, xlo_ref, xhi_ref, ylo_ref, yhi_ref, zlo_ref, zhi_ref, out_ref, done_ref
):
    comps, size_x, size_y, size_z = v_ref.shape
    done_ref[...] = jnp.zeros_like(done_ref)
    x_before, x_after = inside("gx")
    y_before, y_after = inside("gy")
    z_before, z_after = inside("gz")

    xlo, xhi = xlo_ref[...] * x_before, xhi_ref[...] * x_after
    ylo, yhi = ylo_ref[...] * y_before, yhi_ref[...] * y_after

    def columns(face, scale):
        face = face * scale
        face = jnp.concatenate([face, jnp.zeros((WIDE - face.shape[0], WIDE), F32)], axis=0)
        return pltpu.roll(face.T, WIDE - 1, 0)[:size_y, :]

    z_low, z_high = columns(zlo_ref[...], z_before), columns(zhi_ref[...], z_after)
    y_at = iota((size_y, size_z), 0)
    z_at = iota((size_y, size_z), 1)

    def plane(c, x):
        if x < 0:
            return xlo[c]
        if x >= size_x:
            return xhi[c]
        return v_ref[c, x]

    for x in range(size_x):
        here = [plane(c, x) for c in range(comps)]
        after = [plane(c, x + 1) for c in range(comps)]
        prior = [plane(c, x - 1) for c in range(comps)]
        y_up, y_down, z_up, z_down = [], [], [], []
        for c in range(comps):
            at = c * PAD_X + x + 1
            above = yhi[c, x + 1 : x + 2, :]
            below = ylo[c, x + 1 : x + 2, :]
            y_up.append(jnp.where(y_at == size_y - 1, above, pltpu.roll(here[c], size_y - 1, 0)))
            y_down.append(jnp.where(y_at == 0, below, pltpu.roll(here[c], 1, 0)))
            z_up.append(
                jnp.where(z_at == size_z - 1, z_high[:, at : at + 1], pltpu.roll(here[c], size_z - 1, 1))
            )
            z_down.append(jnp.where(z_at == 0, z_low[:, at : at + 1], pltpu.roll(here[c], 1, 1)))
        for c in range(comps):
            diverge = after[c] * after[0] - prior[c] * prior[0]
            diverge = diverge + y_up[c] * y_up[1] - y_down[c] * y_down[1]
            diverge = diverge + z_up[c] * z_up[2] - z_down[c] * z_down[2]
            beside = after[c] + prior[c]
            beside = beside + y_up[c] + y_down[c]
            beside = beside + z_up[c] + z_down[c]
            tendency = -0.5 * diverge + VISCOSITY * (beside - 6.0 * here[c])
            out_ref[c, x] = here[c] + DT_STEP * tendency


def advance(velocity, halos):
    return pl.pallas_call(
        advance_kernel,
        out_shape=(
            jax.ShapeDtypeStruct(velocity.shape, F32),
            jax.ShapeDtypeStruct((8, WIDE), F32),
        ),
        in_specs=whole(7),
        out_specs=tuple(whole(2)),
        compiler_params=params(),
        cost_estimate=cost(1.5),
        name="advance",
    )(velocity, *halos)


def prepare_kernel(
    first_ref, middle_ref, last_ref, biases_ref, w1_ref, w2t_ref, w3_ref, w3t_ref, bias_ref, bias3_ref
):
    feats, hidden = first_ref.shape
    count = last_ref.shape[0]
    wide = jnp.concatenate(
        [first_ref[...].astype(F32), jnp.zeros((WIDE - feats, hidden), F32)], axis=0
    )
    w1_ref[...] = wide.T[:, :ROWS].astype(BF16)
    eye = ones_where(iota((hidden, hidden), 0) == iota((hidden, hidden), 1))
    w2t_ref[...] = lax.dot_general(
        eye, middle_ref[...], NT, preferred_element_type=F32
    ).astype(BF16)
    last = last_ref[...].astype(F32)
    w3_ref[...] = jnp.concatenate([last, jnp.zeros((16 - count, hidden), F32)], axis=0).astype(BF16)
    wide = jnp.concatenate([last, jnp.zeros((WIDE - count, hidden), F32)], axis=0)
    w3t_ref[...] = wide.T[:, :16].astype(BF16)
    for k in range(2 * hidden // WIDE):
        row = biases_ref[:, k * WIDE : (k + 1) * WIDE]
        bias_ref[k * WIDE : (k + 1) * WIDE, :] = jnp.broadcast_to(row, (WIDE, WIDE)).T
    tail = jnp.concatenate(
        [biases_ref[:, 2 * hidden :], jnp.zeros((1, WIDE - count), F32)], axis=1
    )
    bias3_ref[...] = jnp.broadcast_to(tail, (WIDE, WIDE)).T[:8]


def prepare(first, middle, last, biases):
    hidden = middle.shape[0]
    shapes = [
        ((hidden, ROWS), BF16),
        ((hidden, hidden), BF16),
        ((16, hidden), BF16),
        ((hidden, 16), BF16),
        ((2 * hidden, WIDE), F32),
        ((8, WIDE), F32),
    ]
    w1, w2t, w3, w3t, bias, bias3 = pl.pallas_call(
        prepare_kernel,
        out_shape=tuple(jax.ShapeDtypeStruct(*s) for s in shapes),
        in_specs=whole(4),
        out_specs=tuple(whole(6)),
        compiler_params=params(),
        cost_estimate=cost(1.0),
        name="prepare",
    )(first, middle, last, biases)
    return w1, middle, w2t, w3, w3t, bias, bias3


def turn_kernel(in_ref, prepared_ref, done_ref, out_ref):
    shape = (out_ref.shape[0], in_ref.shape[1])
    eye = ones_where(iota(shape, 0) == iota(shape, 1))
    out_ref[...] = lax.dot_general(eye, in_ref[...], NT, preferred_element_type=F32).astype(BF16)


def turn(arrived, prepared, done):
    return pl.pallas_call(
        turn_kernel,
        out_shape=jax.ShapeDtypeStruct((ROWS, arrived.shape[0]), BF16),
        in_specs=whole(3),
        out_specs=pl.BlockSpec(memory_space=pltpu.VMEM),
        compiler_params=params(),
        cost_estimate=cost(0.2),
        name="turn",
    )(arrived, prepared, done)


def lane_sum(value):
    total = value[:, :WIDE]
    for k in range(1, value.shape[1] // WIDE):
        total = total + value[:, k * WIDE : (k + 1) * WIDE]
    return total


def train_kernel(*refs, planes, row_count, first, last, own_rows):
    refs = list(refs)
    take = lambda n: [refs.pop(0) for _ in range(n)]
    x_refs = take(len(planes))
    w1_ref, w2_ref, w2t_ref, w3_ref, w3t_ref, bias_ref, bias3_ref = take(7)
    held = [] if first else take(6)
    if last:
        momentum_ref, master_ref = take(2)
        first_ref, last_ref, bias_grads_ref, master_new_ref, momentum_new_ref = take(5)
        sums = take(6)
    else:
        sums = take(6)
    if first:
        loss_ref = take(1)[0]
    back_two_ref = take(1)[0]
    g1, g2, g3, s1, s2, s3 = sums
    hidden = w2_ref.shape[0]
    factor = 2.0 / (6.0 * row_count)
    olds = dict(zip(map(id, sums), held))

    def add(ref, value):
        ref[...] = value if first else olds[id(ref)][...] + value

    own = pl.multiple_of(lax.axis_index("gz") * own_rows, own_rows)

    def plane(x):
        slots = x.shape[1]
        reps = slots // WIDE
        spread = lambda b: jnp.concatenate([b] * reps, axis=1)
        act_one = jnp.tanh(
            jnp.dot(w1_ref[...], x, preferred_element_type=F32) + spread(bias_ref[:hidden, :])
        ).astype(BF16)
        act_two = jnp.tanh(
            jnp.dot(w2_ref[...], act_one, preferred_element_type=F32) + spread(bias_ref[hidden:, :])
        ).astype(BF16)
        ending = x[ROWS - 16 :, :].astype(F32)[8:, :]
        predicted = jnp.dot(w3_ref[...], act_two, preferred_element_type=F32)[:8, :]
        predicted = predicted + spread(bias3_ref[...])
        mismatch = jnp.where(
            iota((8, slots), 0) < 6, (predicted - ending) * ending[6:7, :], 0.0
        )
        delta_three = mismatch * factor
        back_three = jnp.concatenate([delta_three, jnp.zeros_like(delta_three)], axis=0).astype(BF16)
        add(g3, lax.dot_general(back_three, act_two, NT, preferred_element_type=F32))
        wide_two = act_two.astype(F32)
        delta_two = jnp.dot(w3t_ref[...], back_three, preferred_element_type=F32) * (
            1.0 - wide_two * wide_two
        )
        add(s2, lane_sum(delta_two))
        back_two = delta_two.astype(BF16)
        back_two_ref[...] = back_two
        mine = back_two_ref[pl.ds(own, own_rows), :]
        add(g2, lax.dot_general(mine, act_one, NT, preferred_element_type=F32))
        wide_one = act_one.astype(F32)
        delta_one = jnp.dot(w2t_ref[...], back_two, preferred_element_type=F32) * (
            1.0 - wide_one * wide_one
        )
        add(s1, lane_sum(delta_one))
        back_one = delta_one.astype(BF16)
        add(g1, lax.dot_general(back_one, x, NT, preferred_element_type=F32))
        add(s3, lane_sum(delta_three))
        return mismatch

    pieces = []
    for ref, count in zip(x_refs, planes):
        pieces += [ref[...]] if count == 1 else [ref[k] for k in range(count)]
    mismatch = plane(pieces[0] if len(pieces) == 1 else jnp.concatenate(pieces, axis=1))

    if first:
        row_loss = jnp.sum(mismatch * mismatch, axis=0, keepdims=True) / (6.0 * row_count)
        loss_ref[...] = jnp.sum(row_loss, axis=1, keepdims=True)
    if last:
        per_row = hidden // WIDE
        wide = jnp.concatenate([g1[...], jnp.zeros((hidden, WIDE - ROWS), F32)], axis=1)
        for ref, grads in ((first_ref, wide.T), (last_ref, g3[...])):
            for k in range(ref.shape[0]):
                ref[k] = grads[k : k + 1, :]
        across = lambda s: jnp.sum(s.T, axis=0, keepdims=True)
        bias_grads_ref[:, :hidden] = across(s1[...])
        bias_grads_ref[:, hidden : 2 * hidden] = across(s2[...])
        third = across(jnp.concatenate([s3[...], jnp.zeros((WIDE - 8, WIDE), F32)], axis=0))
        bias_grads_ref[:, 2 * hidden :] = third[:, :6]
        grads = g2[...]
        for k in range(per_row):
            at = pl.ds(k, own_rows, stride=per_row)
            momentum = MOMENTUM_KEEP * momentum_ref[at, :] + grads[:, k * WIDE : (k + 1) * WIDE]
            momentum_new_ref[at, :] = momentum
            master_new_ref[at, :] = master_ref[at, :] - LEARN_RATE * momentum


def train(xs, weights, held, optimizer, row_count, own_rows):
    planes = tuple(x.shape[0] if x.ndim == 3 else 1 for x in xs)
    slots = xs[0].shape[-1]
    hidden = weights[1].shape[0]
    first, last = held is None, optimizer is not None
    sums = [
        jax.ShapeDtypeStruct(s, F32)
        for s in (
            (hidden, ROWS),
            (own_rows, hidden),
            (16, hidden),
            (hidden, WIDE),
            (hidden, WIDE),
            (8, WIDE),
        )
    ]
    scratch = [pltpu.VMEM((hidden, slots * sum(planes)), BF16)]
    if last:
        out = [
            jax.ShapeDtypeStruct(s, F32)
            for s in (
                (81, 1, hidden),
                (6, 1, hidden),
                (1, 2 * hidden + 6),
                optimizer[0].shape,
                optimizer[0].shape,
            )
        ]
        scratch = [pltpu.VMEM(s.shape, F32) for s in sums] + scratch
    else:
        out = list(sums)
    if first:
        out.append(jax.ShapeDtypeStruct((1, 1), F32))
    operands = [*xs, *weights, *(held or ()), *(optimizer or ())]
    count = sum(planes)
    return pl.pallas_call(
        functools.partial(
            train_kernel,
            planes=planes,
            row_count=row_count,
            first=first,
            last=last,
            own_rows=own_rows,
        ),
        out_shape=tuple(out),
        in_specs=whole(len(operands)),
        out_specs=tuple(whole(len(out))),
        scratch_shapes=scratch,
        compiler_params=params(),
        cost_estimate=cost(1.6 * count),
        name="train",
    )(*operands)


def on_device(
    velocity,
    sample_cells,
    trainer_of,
    targets,
    w_first,
    w_middle,
    w_last,
    biases,
    middle_master,
    middle_momentum,
):
    comps, size_x, size_y, size_z = velocity.shape
    samples = sample_cells.shape[0]
    trainers = lax.axis_size("gx") * lax.axis_size("gy")
    capacity = 2 * samples // trainers
    slots = trainers * capacity
    hidden = w_middle.shape[1]
    planes = lax.axis_size("gz")
    own_rows = hidden // planes

    cells = sample_cells.reshape(1, samples)
    x_halos = exchange("gx", *x_faces(velocity))
    y_halos = exchange("gy", *y_faces(velocity, x_halos))
    z_low, z_high, placing = plan(
        velocity, x_halos, trainer_of.reshape(1, samples), trainers, slots
    )
    z_ends = z_faces(z_low, z_high, y_halos, size_y)
    z_halos = exchange("gz", *z_ends)
    features = patches(velocity, x_halos, cells, z_ends[0])
    tail = jnp.concatenate(
        [targets.astype(F32), jnp.ones((1, samples), F32), jnp.zeros((1, samples), F32)], axis=0
    )
    packed = pack(features, y_halos, z_halos, cells, tail, placing, size_x, size_y)
    arrived = lax.all_to_all(
        packed.reshape(trainers, capacity, WIDE),
        ("gx", "gy"),
        split_axis=0,
        concat_axis=0,
        tiled=True,
    ).reshape(slots, WIDE)
    new_velocity, done = advance(velocity, (*x_halos, *y_halos, *z_halos))

    weights = prepare(w_first[0].T, w_middle[0], w_last[0], biases)
    optimizer = (
        middle_momentum.reshape(-1, WIDE),
        middle_master.reshape(-1, WIDE),
    )

    mine = turn(arrived, weights[-1], done)
    call = functools.partial(train, weights=weights, row_count=samples, own_rows=own_rows)
    swap = [(i, i ^ 1) for i in range(planes)]
    chips = planes // 2
    along = lambda to: [(i, 2 * (to(i // 2) % chips) + i % 2) for i in range(planes)]
    beside = lax.ppermute(mine, "gz", swap)
    far = lax.ppermute(mine, "gz", along(lambda x: x + 2))
    *held, loss = call([mine], held=None, optimizer=None)
    beside, far, *held = lax.optimization_barrier((beside, far, *held))
    both = jnp.stack([mine, beside])
    near = [
        lax.ppermute(both, "gz", along(lambda x: x ^ 1)),
        lax.ppermute(both, "gz", along(lambda x: x + 1 if x % 2 else x - 1)),
    ]
    far_beside = lax.ppermute(far, "gz", swap)
    held = call([beside, far], held=held, optimizer=None)
    first_grads, last_grads, bias_grads, master_new, momentum_new = call(
        [*near, far_beside], held=held, optimizer=optimizer
    )
    return (
        new_velocity,
        loss.reshape(1, 1, 1),
        first_grads.transpose(1, 2, 0),
        last_grads.transpose(1, 0, 2),
        bias_grads,
        master_new.reshape(middle_master.shape),
        momentum_new.reshape(middle_momentum.shape),
    )


def solution(mesh):
    placed = (
        P(None, "gx", "gy", "gz"),
        P(("gx", "gy", "gz")),
        P(("gx", "gy", "gz"), None),
        P(None, ("gx", "gy", "gz")),
        P(("gx", "gy"), None, None),
        P(("gx", "gy"), None, None),
        P(("gx", "gy"), None, None),
        P(("gx", "gy"), None),
        P(("gx", "gy"), "gz"),
        P(("gx", "gy"), "gz"),
    )
    return jax.shard_map(
        on_device,
        mesh=mesh,
        in_specs=placed,
        out_specs=(
            P(None, "gx", "gy", "gz"),
            P("gx", "gy", "gz"),
            P(("gx", "gy"), None, None),
            P(("gx", "gy"), None, None),
            P(("gx", "gy"), None),
            P(("gx", "gy"), "gz"),
            P(("gx", "gy"), "gz"),
        ),
        check_vma=False,
    )
```

```python
import functools

import jax
import jax.numpy as jnp
from jax import lax
from jax.experimental import pallas as pl
from jax.experimental.pallas import tpu as pltpu
from jax.sharding import PartitionSpec as P

DT_STEP = 0.1
VISCOSITY = 0.2
LEARN_RATE = 0.05
MOMENTUM_KEEP = 0.9

BF16 = jnp.bfloat16
F32 = jnp.float32
I32 = jnp.int32
NT = (((1,), (1,)), ((), ()))
TN = (((0,), (0,)), ((), ()))
EXACT = lax.Precision.HIGHEST
VMEM_LIMIT = 48 * 1024 * 1024
ROWS = 96
TAIL = 88
WIDE = 128
PAD_X = 16


def params(limit=VMEM_LIMIT):
    return pltpu.CompilerParams(vmem_limit_bytes=limit)


def cost(micros):
    return pl.CostEstimate(
        flops=int(micros * 800_000_000), bytes_accessed=1_000_000, transcendentals=0
    )


def inside(axis):
    at = lax.axis_index(axis)
    return (
        jnp.where(at > 0, 1.0, 0.0).astype(F32),
        jnp.where(at < lax.axis_size(axis) - 1, 1.0, 0.0).astype(F32),
    )


def whole(count):
    return [pl.BlockSpec(memory_space=pltpu.VMEM)] * count


def iota(shape, dim):
    return lax.broadcasted_iota(I32, shape, dim)


def ones_where(mask):
    return jnp.where(mask, 1.0, 0.0).astype(BF16)


def exchange(axis, low_face, high_face):
    count = lax.axis_size(axis)
    forward = [(i, (i + 1) % count) for i in range(count)]
    backward = [(b, a) for a, b in forward]
    return lax.ppermute(high_face, axis, forward), lax.ppermute(low_face, axis, backward)


def faces_kernel(low_ref, high_ref, to_low_ref, to_high_ref):
    to_low_ref[...] = low_ref[:, 0]
    to_high_ref[...] = high_ref[:, 0]


def x_faces(velocity):
    comps, size_x, size_y, size_z = velocity.shape
    spec = lambda at: pl.BlockSpec((comps, 1, size_y, size_z), lambda i: (0, at, 0, 0))
    out = pl.BlockSpec((comps, size_y, size_z), lambda i: (0, 0, 0))
    return pl.pallas_call(
        faces_kernel,
        grid=(1,),
        out_shape=tuple([jax.ShapeDtypeStruct((comps, size_y, size_z), F32)] * 2),
        in_specs=[spec(0), spec(size_x - 1)],
        out_specs=(out, out),
        compiler_params=params(),
        cost_estimate=cost(0.3),
        name="x_faces",
    )(velocity, velocity)


def end_rows(block, low_ref, high_ref, row_of, size_y):
    size_z = block.shape[1]
    row, lane = iota((8, size_z), 0), iota((8, size_z), 1)
    pick = jnp.where(
        ((row == 0) & (lane == 0)) | ((row == 1) & (lane == size_z - 1)), 1.0, 0.0
    ).astype(F32)
    ends = lax.dot_general(pick, block, NT, precision=EXACT, preferred_element_type=F32)
    for k in range(block.shape[0] // size_y):
        at = row_of(k)
        low_ref[at : at + 1, 1 : size_y + 1] = ends[0:1, k * size_y : (k + 1) * size_y]
        high_ref[at : at + 1, 1 : size_y + 1] = ends[1:2, k * size_y : (k + 1) * size_y]


def split_cells(cells, size_x, size_y, size_z):
    return cells // (size_y * size_z), cells // size_z % size_y, cells % size_z


def depth_choice(cell_z, size_z):
    depth = iota((size_z, cell_z.shape[1]), 0)
    return jnp.concatenate([ones_where(depth == cell_z + (r - 1)) for r in range(3)], axis=1)


def fold(ref, first, rows, masks, samples):
    sums = [None] * 3
    for k in range(rows // 8):
        for r in range(3):
            piece = ref[first + 8 * k : first + 8 * k + 8, r * samples : (r + 1) * samples]
            piece = jnp.where(masks[k], piece, 0.0)
            sums[r] = piece if sums[r] is None else sums[r] + piece
    return sums


def feature(c, p, q, r):
    return 27 * c + 9 * p + 3 * q + r


def tile_sums(feats):
    shape = (ROWS, feats * 8)
    return ones_where(lax.shift_right_logical(iota(shape, 1), 3) == iota(shape, 0))


def put_tile(parts, f, total):
    parts[f * 8 : (f + 1) * 8, :] = jnp.zeros((8, parts.shape[1]), F32) if total is None else total


def add_tiles(summing, parts):
    return jnp.dot(summing[...], parts[...].astype(BF16), preferred_element_type=F32)


def plan_kernel(
    v_ref,
    xlo_ref,
    xhi_ref,
    info_ref,
    own_ref,
    choose_ref,
    summing_ref,
    z_low_ref,
    z_high_ref,
    placing_ref,
    out_ref,
    picked,
    parts,
    *,
    trainers,
):
    comps, size_x, size_y, size_z = v_ref.shape
    for ref in (z_low_ref, z_high_ref):
        ref[...] = jnp.zeros_like(ref)
    end_rows(
        v_ref[...].reshape(-1, size_z),
        z_low_ref,
        z_high_ref,
        lambda k: k // size_x * PAD_X + k % size_x + 1,
        size_y,
    )
    before, after = inside("gx")
    for ref, scale, x in ((xlo_ref, before, 0), (xhi_ref, after, size_x + 1)):
        block = ref[...].reshape(-1, size_z) * scale
        end_rows(block, z_low_ref, z_high_ref, lambda k: k * PAD_X + x, size_y)
        first = 0 if x == 0 else block.shape[0]
        picked[first : first + block.shape[0], :] = jnp.dot(
            block.astype(BF16), choose_ref[...], preferred_element_type=F32
        )
    samples = info_ref.shape[1]
    cell_x, cell_y, _ = split_cells(info_ref[0:1, :], size_x, size_y, size_z)
    sub = iota((8, samples), 0)
    for side, at in ((0, cell_x == 0), (1, cell_x == size_x - 1)):
        edge_y = jnp.where(at, cell_y, -100)
        for c in range(comps):
            for q in range(3):
                masks = [sub + (8 * k - q + 1) == edge_y for k in range(size_y // 8)]
                sums = fold(picked, (side * comps + c) * size_y, size_y, masks, samples)
                for r in range(3):
                    put_tile(parts, feature(c, 2 * side, q, r), sums[r])
                    if side == 0:
                        put_tile(parts, feature(c, 1, q, r), None)
    out_ref[...] = own_ref[...] + add_tiles(summing_ref, parts)

    trainer = info_ref[1:2, :]
    slots = placing_ref.shape[0]
    capacity = slots // trainers
    same = iota((trainers, samples), 0) == trainer
    earlier = ones_where(iota((samples, samples), 0) < iota((samples, samples), 1))
    before = jnp.dot(ones_where(same), earlier, preferred_element_type=F32)
    position = jnp.sum(jnp.where(same, before, 0.0), axis=0, keepdims=True).astype(I32)
    slot = trainer * capacity + position
    placing_ref[...] = ones_where(iota((slots, samples), 0) == slot)


def plan(velocity, x_halos, info, own, choose, summing, trainers, slots):
    comps, size_x, size_y, size_z = velocity.shape
    z_face = jax.ShapeDtypeStruct((comps * PAD_X, WIDE), F32)
    placing = jax.ShapeDtypeStruct((slots, info.shape[1]), BF16)
    return pl.pallas_call(
        functools.partial(plan_kernel, trainers=trainers),
        out_shape=(z_face, z_face, placing, jax.ShapeDtypeStruct(own.shape, F32)),
        in_specs=whole(7),
        out_specs=tuple(whole(4)),
        scratch_shapes=[
            pltpu.VMEM((2 * comps * size_y, choose.shape[1]), F32),
            pltpu.VMEM((summing.shape[1], own.shape[1]), F32),
        ],
        compiler_params=params(),
        cost_estimate=cost(1.5),
        name="plan",
    )(velocity, *x_halos, info, own, choose, summing)


def y_faces_kernel(low_ref, high_ref, xlo_ref, xhi_ref, after_ref, to_low_ref, to_high_ref):
    comps, size_x = low_ref.shape[0], low_ref.shape[1]
    before, after = inside("gx")
    last = xlo_ref.shape[1] - 1
    for to, own, row, y in ((to_low_ref, low_ref, 0, 0), (to_high_ref, high_ref, 7, last)):
        to[...] = jnp.zeros_like(to)
        for c in range(comps):
            to[c, 0:1, :] = xlo_ref[c, y : y + 1, :] * before
            for x in range(size_x):
                to[c, x + 1 : x + 2, :] = own[c, x, row : row + 1, :]
            to[c, size_x + 1 : size_x + 2, :] = xhi_ref[c, y : y + 1, :] * after


def y_faces(velocity, x_halos, after):
    comps, size_x, size_y, size_z = velocity.shape
    shape = (comps, PAD_X, size_z)
    spec = lambda at: pl.BlockSpec((comps, size_x, 8, size_z), lambda i: (0, 0, at, 0))
    full = lambda a: pl.BlockSpec(a, lambda i: (0,) * len(a))
    return pl.pallas_call(
        y_faces_kernel,
        grid=(1,),
        out_shape=tuple([jax.ShapeDtypeStruct(shape, F32)] * 2),
        in_specs=[spec(0), spec(size_y // 8 - 1)] + [full(x_halos[0].shape)] * 2 + [full(after.shape)],
        out_specs=(full(shape), full(shape)),
        compiler_params=params(),
        cost_estimate=cost(0.3),
        name="y_faces",
    )(velocity, velocity, *x_halos, after)


def z_faces_kernel(low_ref, high_ref, ylo_ref, yhi_ref, to_low_ref, to_high_ref, *, size_y):
    before, after = inside("gy")
    size_z = ylo_ref.shape[2]
    ylo = ylo_ref[...].reshape(-1, size_z) * before
    yhi = yhi_ref[...].reshape(-1, size_z) * after
    lane = iota(low_ref.shape, 1)
    for own, to, z in ((low_ref, to_low_ref, 0), (high_ref, to_high_ref, size_z - 1)):
        face = jnp.where(lane == 0, ylo[:, z : z + 1], own[...])
        to[...] = jnp.where(lane == size_y + 1, yhi[:, z : z + 1], face)


def z_faces(low, high, y_halos, size_y):
    return pl.pallas_call(
        functools.partial(z_faces_kernel, size_y=size_y),
        out_shape=tuple([jax.ShapeDtypeStruct(low.shape, F32)] * 2),
        in_specs=whole(4),
        out_specs=tuple(whole(2)),
        compiler_params=params(),
        cost_estimate=cost(0.3),
        name="z_faces",
    )(low, high, *y_halos)


def patch_kernel(v_ref, info_ref, out_ref, choose_ref, summing_ref, picked, parts):
    comps, size_x, size_y, size_z = v_ref.shape
    samples = info_ref.shape[1]
    cell_x, cell_y, cell_z = split_cells(info_ref[0:1, :], size_x, size_y, size_z)
    choose_ref[...] = depth_choice(cell_z, size_z)
    picked[...] = jnp.dot(
        v_ref[...].reshape(-1, size_z).astype(BF16), choose_ref[...], preferred_element_type=F32
    )
    sub = iota((8, samples), 0)
    at_x = [cell_x == j for j in range(size_x)]
    for c in range(comps):
        for q in range(3):
            masks = [sub + (8 * k - q + 1) == cell_y for k in range(size_y // 8)]
            totals = [[None] * 3 for _ in range(3)]
            for x in range(size_x):
                sums = fold(picked, (c * size_x + x) * size_y, size_y, masks, samples)
                for p in range(3):
                    j = x + 1 - p
                    if 0 <= j < size_x:
                        for r in range(3):
                            piece = jnp.where(at_x[j], sums[r], 0.0)
                            totals[p][r] = piece if totals[p][r] is None else totals[p][r] + piece
            for p in range(3):
                for r in range(3):
                    put_tile(parts, feature(c, p, q, r), totals[p][r])
    summing_ref[...] = tile_sums(27 * comps)
    out_ref[...] = add_tiles(summing_ref, parts)


def patches(velocity, cells):
    comps, size_x, size_y, size_z = velocity.shape
    samples = cells.shape[1]
    feats = 27 * comps
    return pl.pallas_call(
        patch_kernel,
        out_shape=(
            jax.ShapeDtypeStruct((ROWS, samples), F32),
            jax.ShapeDtypeStruct((size_z, 3 * samples), BF16),
            jax.ShapeDtypeStruct((ROWS, feats * 8), BF16),
        ),
        in_specs=whole(2),
        out_specs=tuple(whole(3)),
        scratch_shapes=[
            pltpu.VMEM((comps * size_x * size_y, 3 * samples), F32),
            pltpu.VMEM((feats * 8, samples), F32),
        ],
        compiler_params=params(),
        cost_estimate=cost(1.2),
        name="patches",
    )(velocity, cells)


def edge_kernel(
    own_ref, ylo_ref, yhi_ref, info_ref, choose_ref, summing_ref, after_ref, out_ref, rows_ref,
    picked, parts, *, size_x, size_y
):
    comps, pad_x, size_z = ylo_ref.shape
    samples = info_ref.shape[1]
    rows = comps * pad_x
    cell_x, cell_y, _ = split_cells(info_ref[0:1, :], size_x, size_y, size_z)
    before, after = inside("gy")
    along = jnp.concatenate(
        [ylo_ref[...].reshape(rows, size_z) * before, yhi_ref[...].reshape(rows, size_z) * after],
        axis=0,
    ).astype(BF16)
    picked[...] = jnp.dot(along, choose_ref[...], preferred_element_type=F32)
    sub = iota((8, samples), 0)
    for side, at in ((0, cell_y == 0), (1, cell_y == size_y - 1)):
        edge_x = jnp.where(at, cell_x, -100)
        for c in range(comps):
            for p in range(3):
                masks = [sub + (8 * k - p) == edge_x for k in range(pad_x // 8)]
                sums = fold(picked, side * rows + c * pad_x, pad_x, masks, samples)
                for r in range(3):
                    put_tile(parts, feature(c, p, 2 * side, r), sums[r])
                    if side == 0:
                        put_tile(parts, feature(c, p, 1, r), None)
    out_ref[...] = own_ref[...] + add_tiles(summing_ref, parts)
    width = iota((WIDE, samples), 0)
    rows_ref[...] = jnp.concatenate([ones_where(width == cell_y + q) for q in range(3)], axis=1)


def edges(own, y_halos, cells, choose, summing, after, size_x, size_y):
    samples = cells.shape[1]
    comps, pad_x, _ = y_halos[0].shape
    return pl.pallas_call(
        functools.partial(edge_kernel, size_x=size_x, size_y=size_y),
        out_shape=(
            jax.ShapeDtypeStruct(own.shape, F32),
            jax.ShapeDtypeStruct((WIDE, 3 * samples), BF16),
        ),
        in_specs=whole(7),
        out_specs=tuple(whole(2)),
        scratch_shapes=[
            pltpu.VMEM((2 * comps * pad_x, 3 * samples), F32),
            pltpu.VMEM((summing.shape[1], samples), F32),
        ],
        compiler_params=params(),
        cost_estimate=cost(0.6),
        name="edges",
    )(own, *y_halos, cells, choose, summing, after)


def pack_kernel(
    own_ref, zlo_ref, zhi_ref, info_ref, rows_ref, summing_ref, tail_ref, placing_ref, out_ref,
    picked, parts, *, comps, sizes
):
    samples = info_ref.shape[1]
    rows = zlo_ref.shape[0]
    pad_x = rows // comps
    cell_x, _, cell_z = split_cells(info_ref[0:1, :], *sizes)
    before, after = inside("gz")
    along = jnp.concatenate([zlo_ref[...] * before, zhi_ref[...] * after], axis=0).astype(BF16)
    picked[...] = jnp.dot(along, rows_ref[...], preferred_element_type=F32)
    sub = iota((8, samples), 0)
    for side, at in ((0, cell_z == 0), (1, cell_z == sizes[2] - 1)):
        edge_x = jnp.where(at, cell_x, -100)
        for c in range(comps):
            for p in range(3):
                masks = [sub + (8 * k - p) == edge_x for k in range(pad_x // 8)]
                sums = fold(picked, side * rows + c * pad_x, pad_x, masks, samples)
                for q in range(3):
                    put_tile(parts, feature(c, p, q, 2 * side), sums[q])
                    if side == 0:
                        put_tile(parts, feature(c, p, q, 1), None)
    features = own_ref[...] + add_tiles(summing_ref, parts)
    payload = jnp.concatenate(
        [features[:TAIL], tail_ref[...], jnp.zeros((WIDE - ROWS, samples), F32)], axis=0
    ).astype(BF16)
    out_ref[...] = lax.dot_general(
        placing_ref[...], payload, NT, preferred_element_type=F32
    ).astype(BF16)


def pack(own, z_halos, cells, rows, summing, tail, placing, comps, sizes):
    samples = cells.shape[1]
    return pl.pallas_call(
        functools.partial(pack_kernel, comps=comps, sizes=sizes),
        out_shape=jax.ShapeDtypeStruct((placing.shape[0], WIDE), BF16),
        in_specs=whole(8),
        out_specs=pl.BlockSpec(memory_space=pltpu.VMEM),
        scratch_shapes=[
            pltpu.VMEM((2 * z_halos[0].shape[0], 3 * samples), F32),
            pltpu.VMEM((summing.shape[1], samples), F32),
        ],
        compiler_params=params(),
        cost_estimate=cost(0.7),
        name="pack",
    )(own, *z_halos, cells, rows, summing, tail, placing)


def advance_kernel(
    v_ref, xlo_ref, xhi_ref, ylo_ref, yhi_ref, zlo_ref, zhi_ref, out_ref, done_ref
):
    comps, size_x, size_y, size_z = v_ref.shape
    done_ref[...] = jnp.zeros_like(done_ref)
    x_before, x_after = inside("gx")
    y_before, y_after = inside("gy")
    z_before, z_after = inside("gz")

    xlo, xhi = xlo_ref[...] * x_before, xhi_ref[...] * x_after
    ylo, yhi = ylo_ref[...] * y_before, yhi_ref[...] * y_after

    def columns(face, scale):
        face = face * scale
        face = jnp.concatenate([face, jnp.zeros((WIDE - face.shape[0], WIDE), F32)], axis=0)
        return pltpu.roll(face.T, WIDE - 1, 0)[:size_y, :]

    z_low, z_high = columns(zlo_ref[...], z_before), columns(zhi_ref[...], z_after)
    y_at = iota((size_y, size_z), 0)
    z_at = iota((size_y, size_z), 1)

    def plane(c, x):
        if x < 0:
            return xlo[c]
        if x >= size_x:
            return xhi[c]
        return v_ref[c, x]

    for x in range(size_x):
        here = [plane(c, x) for c in range(comps)]
        after = [plane(c, x + 1) for c in range(comps)]
        prior = [plane(c, x - 1) for c in range(comps)]
        y_up, y_down, z_up, z_down = [], [], [], []
        for c in range(comps):
            at = c * PAD_X + x + 1
            above = yhi[c, x + 1 : x + 2, :]
            below = ylo[c, x + 1 : x + 2, :]
            y_up.append(jnp.where(y_at == size_y - 1, above, pltpu.roll(here[c], size_y - 1, 0)))
            y_down.append(jnp.where(y_at == 0, below, pltpu.roll(here[c], 1, 0)))
            z_up.append(
                jnp.where(z_at == size_z - 1, z_high[:, at : at + 1], pltpu.roll(here[c], size_z - 1, 1))
            )
            z_down.append(jnp.where(z_at == 0, z_low[:, at : at + 1], pltpu.roll(here[c], 1, 1)))
        for c in range(comps):
            diverge = after[c] * after[0] - prior[c] * prior[0]
            diverge = diverge + y_up[c] * y_up[1] - y_down[c] * y_down[1]
            diverge = diverge + z_up[c] * z_up[2] - z_down[c] * z_down[2]
            beside = after[c] + prior[c]
            beside = beside + y_up[c] + y_down[c]
            beside = beside + z_up[c] + z_down[c]
            tendency = -0.5 * diverge + VISCOSITY * (beside - 6.0 * here[c])
            out_ref[c, x] = here[c] + DT_STEP * tendency


def advance(velocity, halos):
    return pl.pallas_call(
        advance_kernel,
        out_shape=(
            jax.ShapeDtypeStruct(velocity.shape, F32),
            jax.ShapeDtypeStruct((8, WIDE), F32),
        ),
        in_specs=whole(7),
        out_specs=tuple(whole(2)),
        compiler_params=params(),
        cost_estimate=cost(1.5),
        name="advance",
    )(velocity, *halos)


def prepare_kernel(
    first_ref, middle_ref, last_ref, biases_ref, w1_ref, w2t_ref, w3_ref, w3t_ref, bias_ref, bias3_ref
):
    feats, hidden = first_ref.shape
    count = last_ref.shape[0]
    wide = jnp.concatenate(
        [first_ref[...].astype(F32), jnp.zeros((WIDE - feats, hidden), F32)], axis=0
    )
    w1_ref[...] = wide.T[:, :ROWS].astype(BF16)
    eye = ones_where(iota((hidden, hidden), 0) == iota((hidden, hidden), 1))
    w2t_ref[...] = lax.dot_general(
        eye, middle_ref[...], NT, preferred_element_type=F32
    ).astype(BF16)
    last = last_ref[...].astype(F32)
    w3_ref[...] = jnp.concatenate([last, jnp.zeros((16 - count, hidden), F32)], axis=0).astype(BF16)
    wide = jnp.concatenate([last, jnp.zeros((WIDE - count, hidden), F32)], axis=0)
    w3t_ref[...] = wide.T[:, :16].astype(BF16)
    for k in range(2 * hidden // WIDE):
        row = biases_ref[:, k * WIDE : (k + 1) * WIDE]
        bias_ref[k * WIDE : (k + 1) * WIDE, :] = jnp.broadcast_to(row, (WIDE, WIDE)).T
    tail = jnp.concatenate(
        [biases_ref[:, 2 * hidden :], jnp.zeros((1, WIDE - count), F32)], axis=1
    )
    bias3_ref[...] = jnp.broadcast_to(tail, (WIDE, WIDE)).T[:8]


def prepare(first, middle, last, biases):
    hidden = middle.shape[0]
    shapes = [
        ((hidden, ROWS), BF16),
        ((hidden, hidden), BF16),
        ((16, hidden), BF16),
        ((hidden, 16), BF16),
        ((2 * hidden, WIDE), F32),
        ((8, WIDE), F32),
    ]
    w1, w2t, w3, w3t, bias, bias3 = pl.pallas_call(
        prepare_kernel,
        out_shape=tuple(jax.ShapeDtypeStruct(*s) for s in shapes),
        in_specs=whole(4),
        out_specs=tuple(whole(6)),
        compiler_params=params(),
        cost_estimate=cost(1.0),
        name="prepare",
    )(first, middle, last, biases)
    return w1, middle, w2t, w3, w3t, bias, bias3


def turn_kernel(in_ref, prepared_ref, done_ref, out_ref):
    shape = (out_ref.shape[0], in_ref.shape[1])
    eye = ones_where(iota(shape, 0) == iota(shape, 1))
    out_ref[...] = lax.dot_general(eye, in_ref[...], NT, preferred_element_type=F32).astype(BF16)


def turn(arrived, prepared, done):
    return pl.pallas_call(
        turn_kernel,
        out_shape=jax.ShapeDtypeStruct((ROWS, arrived.shape[0]), BF16),
        in_specs=whole(3),
        out_specs=pl.BlockSpec(memory_space=pltpu.VMEM),
        compiler_params=params(),
        cost_estimate=cost(0.2),
        name="turn",
    )(arrived, prepared, done)


def lane_sum(value):
    total = value[:, :WIDE]
    for k in range(1, value.shape[1] // WIDE):
        total = total + value[:, k * WIDE : (k + 1) * WIDE]
    return total


def train_kernel(*refs, planes, row_count, first, last, own_rows):
    refs = list(refs)
    take = lambda n: [refs.pop(0) for _ in range(n)]
    x_refs = take(len(planes))
    w1_ref, w2_ref, w2t_ref, w3_ref, w3t_ref, bias_ref, bias3_ref = take(7)
    held = [] if first else take(6)
    if last:
        momentum_ref, master_ref = take(2)
        first_ref, last_ref, bias_grads_ref, master_new_ref, momentum_new_ref = take(5)
        sums = take(6)
    else:
        sums = take(6)
    if first:
        loss_ref = take(1)[0]
    back_two_ref = take(1)[0]
    g1, g2, g3, s1, s2, s3 = sums
    hidden = w2_ref.shape[0]
    factor = 2.0 / (6.0 * row_count)
    olds = dict(zip(map(id, sums), held))

    def add(ref, value):
        ref[...] = value if first else olds[id(ref)][...] + value

    own = pl.multiple_of(lax.axis_index("gz") * own_rows, own_rows)

    per_row = hidden // WIDE
    across = lambda s: jnp.sum(s.T, axis=0, keepdims=True)

    def finish_early():
        grads = g2[...]
        for k in range(per_row):
            at = pl.ds(k, own_rows, stride=per_row)
            momentum = MOMENTUM_KEEP * momentum_ref[at, :] + grads[:, k * WIDE : (k + 1) * WIDE]
            momentum_new_ref[at, :] = momentum
            master_new_ref[at, :] = master_ref[at, :] - LEARN_RATE * momentum
        for k in range(last_ref.shape[0]):
            last_ref[k] = g3[k : k + 1, :]
        bias_grads_ref[:, hidden : 2 * hidden] = across(s2[...])
        third = across(jnp.concatenate([s3[...], jnp.zeros((WIDE - 8, WIDE), F32)], axis=0))
        bias_grads_ref[:, 2 * hidden :] = third[:, :6]

    def plane(x):
        slots = x.shape[1]
        reps = slots // WIDE
        spread = lambda b: jnp.concatenate([b] * reps, axis=1)
        act_one = jnp.tanh(
            jnp.dot(w1_ref[...], x, preferred_element_type=F32) + spread(bias_ref[:hidden, :])
        ).astype(BF16)
        act_two = jnp.tanh(
            jnp.dot(w2_ref[...], act_one, preferred_element_type=F32) + spread(bias_ref[hidden:, :])
        ).astype(BF16)
        ending = x[ROWS - 16 :, :].astype(F32)[8:, :]
        predicted = jnp.dot(w3_ref[...], act_two, preferred_element_type=F32)[:8, :]
        predicted = predicted + spread(bias3_ref[...])
        mismatch = jnp.where(
            iota((8, slots), 0) < 6, (predicted - ending) * ending[6:7, :], 0.0
        )
        delta_three = mismatch * factor
        add(s3, lane_sum(delta_three))
        back_three = jnp.concatenate([delta_three, jnp.zeros_like(delta_three)], axis=0).astype(BF16)
        add(g3, lax.dot_general(back_three, act_two, NT, preferred_element_type=F32))
        wide_two = act_two.astype(F32)
        delta_two = jnp.dot(w3t_ref[...], back_three, preferred_element_type=F32) * (
            1.0 - wide_two * wide_two
        )
        add(s2, lane_sum(delta_two))
        back_two = delta_two.astype(BF16)
        back_two_ref[...] = back_two
        mine = back_two_ref[pl.ds(own, own_rows), :]
        add(g2, lax.dot_general(mine, act_one, NT, preferred_element_type=F32))
        if last:
            finish_early()
        wide_one = act_one.astype(F32)
        delta_one = jnp.dot(w2t_ref[...], back_two, preferred_element_type=F32) * (
            1.0 - wide_one * wide_one
        )
        add(s1, lane_sum(delta_one))
        back_one = delta_one.astype(BF16)
        add(g1, lax.dot_general(back_one, x, NT, preferred_element_type=F32))
        return mismatch

    pieces = []
    for ref, count in zip(x_refs, planes):
        pieces += [ref[...]] if count == 1 else [ref[k] for k in range(count)]
    mismatch = plane(pieces[0] if len(pieces) == 1 else jnp.concatenate(pieces, axis=1))

    if first:
        row_loss = jnp.sum(mismatch * mismatch, axis=0, keepdims=True) / (6.0 * row_count)
        loss_ref[...] = jnp.sum(row_loss, axis=1, keepdims=True)
    if last:
        wide = jnp.concatenate([g1[...], jnp.zeros((hidden, WIDE - ROWS), F32)], axis=1).T
        for k in range(first_ref.shape[0]):
            first_ref[k] = wide[k : k + 1, :]
        bias_grads_ref[:, :hidden] = across(s1[...])


def train(xs, weights, held, optimizer, row_count, own_rows):
    planes = tuple(x.shape[0] if x.ndim == 3 else 1 for x in xs)
    slots = xs[0].shape[-1]
    hidden = weights[1].shape[0]
    first, last = held is None, optimizer is not None
    sums = [
        jax.ShapeDtypeStruct(s, F32)
        for s in (
            (hidden, ROWS),
            (own_rows, hidden),
            (16, hidden),
            (hidden, WIDE),
            (hidden, WIDE),
            (8, WIDE),
        )
    ]
    scratch = [pltpu.VMEM((hidden, slots * sum(planes)), BF16)]
    if last:
        out = [
            jax.ShapeDtypeStruct(s, F32)
            for s in (
                (81, 1, hidden),
                (6, 1, hidden),
                (1, 2 * hidden + 6),
                optimizer[0].shape,
                optimizer[0].shape,
            )
        ]
        scratch = [pltpu.VMEM(s.shape, F32) for s in sums] + scratch
    else:
        out = list(sums)
    if first:
        out.append(jax.ShapeDtypeStruct((1, 1), F32))
    operands = [*xs, *weights, *(held or ()), *(optimizer or ())]
    count = sum(planes)
    return pl.pallas_call(
        functools.partial(
            train_kernel,
            planes=planes,
            row_count=row_count,
            first=first,
            last=last,
            own_rows=own_rows,
        ),
        out_shape=tuple(out),
        in_specs=whole(len(operands)),
        out_specs=tuple(whole(len(out))),
        scratch_shapes=scratch,
        compiler_params=params(),
        cost_estimate=cost(1.6 * count),
        name="train",
    )(*operands)


def on_device(
    velocity,
    sample_cells,
    trainer_of,
    targets,
    w_first,
    w_middle,
    w_last,
    biases,
    middle_master,
    middle_momentum,
):
    comps, size_x, size_y, size_z = velocity.shape
    samples = sample_cells.shape[0]
    trainers = lax.axis_size("gx") * lax.axis_size("gy")
    capacity = 2 * samples // trainers
    slots = trainers * capacity
    hidden = w_middle.shape[1]
    planes = lax.axis_size("gz")
    own_rows = hidden // planes

    info = jnp.stack([sample_cells, trainer_of[:, 0]])
    x_halos = exchange("gx", *x_faces(velocity))
    features, choose, summing = patches(velocity, info)
    y_halos = exchange("gy", *y_faces(velocity, x_halos, features))
    z_low, z_high, placing, features = plan(
        velocity,
        x_halos,
        info,
        features,
        choose,
        summing,
        trainers,
        slots,
    )
    z_ends = z_faces(z_low, z_high, y_halos, size_y)
    z_halos = exchange("gz", *z_ends)
    features, rows = edges(features, y_halos, info, choose, summing, z_ends[0], size_x, size_y)
    tail = jnp.concatenate(
        [targets.astype(F32), jnp.ones((1, samples), F32), jnp.zeros((1, samples), F32)], axis=0
    )
    packed = pack(
        features, z_halos, info, rows, summing, tail, placing, comps, (size_x, size_y, size_z)
    )
    arrived = lax.all_to_all(
        packed.reshape(trainers, capacity, WIDE),
        ("gx", "gy"),
        split_axis=0,
        concat_axis=0,
        tiled=True,
    ).reshape(slots, WIDE)
    new_velocity, done = advance(velocity, (*x_halos, *y_halos, *z_halos))

    weights = prepare(w_first[0].T, w_middle[0], w_last[0], biases)
    optimizer = (
        middle_momentum.reshape(-1, WIDE),
        middle_master.reshape(-1, WIDE),
    )

    mine = turn(arrived, weights[-1], done)
    call = functools.partial(train, weights=weights, row_count=samples, own_rows=own_rows)
    swap = [(i, i ^ 1) for i in range(planes)]
    chips = planes // 2
    along = lambda to: [(i, 2 * (to(i // 2) % chips) + i % 2) for i in range(planes)]
    beside = lax.ppermute(mine, "gz", swap)
    far = lax.ppermute(mine, "gz", along(lambda x: x + 2))
    *held, loss = call([mine], held=None, optimizer=None)
    beside, far, *held = lax.optimization_barrier((beside, far, *held))
    both = jnp.stack([mine, beside])
    near = [
        lax.ppermute(both, "gz", along(lambda x: x ^ 1)),
        lax.ppermute(both, "gz", along(lambda x: x + 1 if x % 2 else x - 1)),
    ]
    far_beside = lax.ppermute(far, "gz", swap)
    held = call([beside, far], held=held, optimizer=None)
    first_grads, last_grads, bias_grads, master_new, momentum_new = call(
        [*near, far_beside], held=held, optimizer=optimizer
    )
    return (
        new_velocity,
        loss.reshape(1, 1, 1),
        first_grads.transpose(1, 2, 0),
        last_grads.transpose(1, 0, 2),
        bias_grads,
        master_new.reshape(middle_master.shape),
        momentum_new.reshape(middle_momentum.shape),
    )


def solution(mesh):
    placed = (
        P(None, "gx", "gy", "gz"),
        P(("gx", "gy", "gz")),
        P(("gx", "gy", "gz"), None),
        P(None, ("gx", "gy", "gz")),
        P(("gx", "gy"), None, None),
        P(("gx", "gy"), None, None),
        P(("gx", "gy"), None, None),
        P(("gx", "gy"), None),
        P(("gx", "gy"), "gz"),
        P(("gx", "gy"), "gz"),
    )
    return jax.shard_map(
        on_device,
        mesh=mesh,
        in_specs=placed,
        out_specs=(
            P(None, "gx", "gy", "gz"),
            P("gx", "gy", "gz"),
            P(("gx", "gy"), None, None),
            P(("gx", "gy"), None, None),
            P(("gx", "gy"), None),
            P(("gx", "gy"), "gz"),
            P(("gx", "gy"), "gz"),
        ),
        check_vma=False,
    )
```

```python
import functools

import jax
import jax.numpy as jnp
from jax import lax
from jax.experimental import pallas as pl
from jax.experimental.pallas import tpu as pltpu
from jax.sharding import PartitionSpec as P

DT_STEP = 0.1
VISCOSITY = 0.2
LEARN_RATE = 0.05
MOMENTUM_KEEP = 0.9

BF16 = jnp.bfloat16
F32 = jnp.float32
I32 = jnp.int32
NT = (((1,), (1,)), ((), ()))
TN = (((0,), (0,)), ((), ()))
EXACT = lax.Precision.HIGHEST
VMEM_LIMIT = 48 * 1024 * 1024
ROWS = 96
TAIL = 88
WIDE = 128
PAD_X = 16


def params(limit=VMEM_LIMIT):
    return pltpu.CompilerParams(vmem_limit_bytes=limit)


def cost(micros):
    return pl.CostEstimate(
        flops=int(micros * 800_000_000), bytes_accessed=1_000_000, transcendentals=0
    )


def inside(axis):
    at = lax.axis_index(axis)
    return (
        jnp.where(at > 0, 1.0, 0.0).astype(F32),
        jnp.where(at < lax.axis_size(axis) - 1, 1.0, 0.0).astype(F32),
    )


def whole(count):
    return [pl.BlockSpec(memory_space=pltpu.VMEM)] * count


def iota(shape, dim):
    return lax.broadcasted_iota(I32, shape, dim)


def ones_where(mask):
    return jnp.where(mask, 1.0, 0.0).astype(BF16)


def exchange(axis, low_face, high_face):
    count = lax.axis_size(axis)
    forward = [(i, (i + 1) % count) for i in range(count)]
    backward = [(b, a) for a, b in forward]
    return lax.ppermute(high_face, axis, forward), lax.ppermute(low_face, axis, backward)


def faces_kernel(low_ref, high_ref, to_low_ref, to_high_ref):
    to_low_ref[...] = low_ref[:, 0]
    to_high_ref[...] = high_ref[:, 0]


def x_faces(velocity):
    comps, size_x, size_y, size_z = velocity.shape
    spec = lambda at: pl.BlockSpec((comps, 1, size_y, size_z), lambda i: (0, at, 0, 0))
    out = pl.BlockSpec((comps, size_y, size_z), lambda i: (0, 0, 0))
    return pl.pallas_call(
        faces_kernel,
        grid=(1,),
        out_shape=tuple([jax.ShapeDtypeStruct((comps, size_y, size_z), F32)] * 2),
        in_specs=[spec(0), spec(size_x - 1)],
        out_specs=(out, out),
        compiler_params=params(),
        cost_estimate=cost(0.3),
        name="x_faces",
    )(velocity, velocity)


def end_rows(block, low_ref, high_ref, row_of, size_y):
    size_z = block.shape[1]
    row, lane = iota((8, size_z), 0), iota((8, size_z), 1)
    pick = jnp.where(
        ((row == 0) & (lane == 0)) | ((row == 1) & (lane == size_z - 1)), 1.0, 0.0
    ).astype(F32)
    ends = lax.dot_general(pick, block, NT, precision=EXACT, preferred_element_type=F32)
    for k in range(block.shape[0] // size_y):
        at = row_of(k)
        low_ref[at : at + 1, 1 : size_y + 1] = ends[0:1, k * size_y : (k + 1) * size_y]
        high_ref[at : at + 1, 1 : size_y + 1] = ends[1:2, k * size_y : (k + 1) * size_y]


def split_cells(cells, size_x, size_y, size_z):
    return cells // (size_y * size_z), cells // size_z % size_y, cells % size_z


def depth_choice(cell_z, size_z):
    depth = iota((size_z, cell_z.shape[1]), 0)
    return jnp.concatenate([ones_where(depth == cell_z + (r - 1)) for r in range(3)], axis=1)


def fold(ref, first, rows, masks, samples):
    sums = [None] * 3
    for k in range(rows // 8):
        for r in range(3):
            piece = ref[first + 8 * k : first + 8 * k + 8, r * samples : (r + 1) * samples]
            piece = jnp.where(masks[k], piece, 0.0)
            sums[r] = piece if sums[r] is None else sums[r] + piece
    return sums


def feature(c, p, q, r):
    return 27 * c + 9 * p + 3 * q + r


def tile_sums(feats):
    shape = (ROWS, feats * 8)
    return ones_where(lax.shift_right_logical(iota(shape, 1), 3) == iota(shape, 0))


def put_tile(parts, f, total):
    parts[f * 8 : (f + 1) * 8, :] = jnp.zeros((8, parts.shape[1]), F32) if total is None else total


def add_tiles(summing, parts):
    return jnp.dot(summing[...], parts[...].astype(BF16), preferred_element_type=F32)


def plan_kernel(
    v_ref,
    xlo_ref,
    xhi_ref,
    info_ref,
    own_ref,
    choose_ref,
    summing_ref,
    z_low_ref,
    z_high_ref,
    placing_ref,
    out_ref,
    picked,
    parts,
    *,
    trainers,
):
    comps, size_x, size_y, size_z = v_ref.shape
    for ref in (z_low_ref, z_high_ref):
        ref[...] = jnp.zeros_like(ref)
    end_rows(
        v_ref[...].reshape(-1, size_z),
        z_low_ref,
        z_high_ref,
        lambda k: k // size_x * PAD_X + k % size_x + 1,
        size_y,
    )
    before, after = inside("gx")
    for ref, scale, x in ((xlo_ref, before, 0), (xhi_ref, after, size_x + 1)):
        block = ref[...].reshape(-1, size_z) * scale
        end_rows(block, z_low_ref, z_high_ref, lambda k: k * PAD_X + x, size_y)
        first = 0 if x == 0 else block.shape[0]
        picked[first : first + block.shape[0], :] = jnp.dot(
            block.astype(BF16), choose_ref[...], preferred_element_type=F32
        )
    samples = info_ref.shape[1]
    cell_x, cell_y, _ = split_cells(info_ref[0:1, :], size_x, size_y, size_z)
    sub = iota((8, samples), 0)
    for side, at in ((0, cell_x == 0), (1, cell_x == size_x - 1)):
        edge_y = jnp.where(at, cell_y, -100)
        for c in range(comps):
            for q in range(3):
                masks = [sub + (8 * k - q + 1) == edge_y for k in range(size_y // 8)]
                sums = fold(picked, (side * comps + c) * size_y, size_y, masks, samples)
                for r in range(3):
                    put_tile(parts, feature(c, 2 * side, q, r), sums[r])
                    if side == 0:
                        put_tile(parts, feature(c, 1, q, r), None)
    out_ref[...] = own_ref[...] + add_tiles(summing_ref, parts)

    trainer = info_ref[1:2, :]
    slots = placing_ref.shape[0]
    capacity = slots // trainers
    same = iota((trainers, samples), 0) == trainer
    earlier = ones_where(iota((samples, samples), 0) < iota((samples, samples), 1))
    before = jnp.dot(ones_where(same), earlier, preferred_element_type=F32)
    position = jnp.sum(jnp.where(same, before, 0.0), axis=0, keepdims=True).astype(I32)
    columns = lax.axis_size("gy")
    block = trainer % columns * (trainers // columns) + trainer // columns
    slot = block * capacity + position
    placing_ref[...] = ones_where(iota((slots, samples), 0) == slot)


def plan(velocity, x_halos, info, own, choose, summing, trainers, slots):
    comps, size_x, size_y, size_z = velocity.shape
    z_face = jax.ShapeDtypeStruct((comps * PAD_X, WIDE), F32)
    placing = jax.ShapeDtypeStruct((slots, info.shape[1]), BF16)
    return pl.pallas_call(
        functools.partial(plan_kernel, trainers=trainers),
        out_shape=(z_face, z_face, placing, jax.ShapeDtypeStruct(own.shape, F32)),
        in_specs=whole(7),
        out_specs=tuple(whole(4)),
        scratch_shapes=[
            pltpu.VMEM((2 * comps * size_y, choose.shape[1]), F32),
            pltpu.VMEM((summing.shape[1], own.shape[1]), F32),
        ],
        compiler_params=params(),
        cost_estimate=cost(1.5),
        name="plan",
    )(velocity, *x_halos, info, own, choose, summing)


def y_faces_kernel(low_ref, high_ref, xlo_ref, xhi_ref, after_ref, to_low_ref, to_high_ref):
    comps, size_x = low_ref.shape[0], low_ref.shape[1]
    before, after = inside("gx")
    last = xlo_ref.shape[1] - 1
    for to, own, row, y in ((to_low_ref, low_ref, 0, 0), (to_high_ref, high_ref, 7, last)):
        to[...] = jnp.zeros_like(to)
        for c in range(comps):
            to[c, 0:1, :] = xlo_ref[c, y : y + 1, :] * before
            for x in range(size_x):
                to[c, x + 1 : x + 2, :] = own[c, x, row : row + 1, :]
            to[c, size_x + 1 : size_x + 2, :] = xhi_ref[c, y : y + 1, :] * after


def y_faces(velocity, x_halos, after):
    comps, size_x, size_y, size_z = velocity.shape
    shape = (comps, PAD_X, size_z)
    spec = lambda at: pl.BlockSpec((comps, size_x, 8, size_z), lambda i: (0, 0, at, 0))
    full = lambda a: pl.BlockSpec(a, lambda i: (0,) * len(a))
    return pl.pallas_call(
        y_faces_kernel,
        grid=(1,),
        out_shape=tuple([jax.ShapeDtypeStruct(shape, F32)] * 2),
        in_specs=[spec(0), spec(size_y // 8 - 1)] + [full(x_halos[0].shape)] * 2 + [full(after.shape)],
        out_specs=(full(shape), full(shape)),
        compiler_params=params(),
        cost_estimate=cost(0.3),
        name="y_faces",
    )(velocity, velocity, *x_halos, after)


def z_faces_kernel(low_ref, high_ref, ylo_ref, yhi_ref, to_low_ref, to_high_ref, *, size_y):
    before, after = inside("gy")
    size_z = ylo_ref.shape[2]
    ylo = ylo_ref[...].reshape(-1, size_z) * before
    yhi = yhi_ref[...].reshape(-1, size_z) * after
    lane = iota(low_ref.shape, 1)
    for own, to, z in ((low_ref, to_low_ref, 0), (high_ref, to_high_ref, size_z - 1)):
        face = jnp.where(lane == 0, ylo[:, z : z + 1], own[...])
        to[...] = jnp.where(lane == size_y + 1, yhi[:, z : z + 1], face)


def z_faces(low, high, y_halos, size_y):
    return pl.pallas_call(
        functools.partial(z_faces_kernel, size_y=size_y),
        out_shape=tuple([jax.ShapeDtypeStruct(low.shape, F32)] * 2),
        in_specs=whole(4),
        out_specs=tuple(whole(2)),
        compiler_params=params(),
        cost_estimate=cost(0.3),
        name="z_faces",
    )(low, high, *y_halos)


def patch_kernel(v_ref, info_ref, out_ref, choose_ref, summing_ref, picked, parts):
    comps, size_x, size_y, size_z = v_ref.shape
    samples = info_ref.shape[1]
    cell_x, cell_y, cell_z = split_cells(info_ref[0:1, :], size_x, size_y, size_z)
    choose_ref[...] = depth_choice(cell_z, size_z)
    picked[...] = jnp.dot(
        v_ref[...].reshape(-1, size_z).astype(BF16), choose_ref[...], preferred_element_type=F32
    )
    sub = iota((8, samples), 0)
    at_x = [cell_x == j for j in range(size_x)]
    for c in range(comps):
        for q in range(3):
            masks = [sub + (8 * k - q + 1) == cell_y for k in range(size_y // 8)]
            totals = [[None] * 3 for _ in range(3)]
            for x in range(size_x):
                sums = fold(picked, (c * size_x + x) * size_y, size_y, masks, samples)
                for p in range(3):
                    j = x + 1 - p
                    if 0 <= j < size_x:
                        for r in range(3):
                            piece = jnp.where(at_x[j], sums[r], 0.0)
                            totals[p][r] = piece if totals[p][r] is None else totals[p][r] + piece
            for p in range(3):
                for r in range(3):
                    put_tile(parts, feature(c, p, q, r), totals[p][r])
    summing_ref[...] = tile_sums(27 * comps)
    out_ref[...] = add_tiles(summing_ref, parts)


def patches(velocity, cells):
    comps, size_x, size_y, size_z = velocity.shape
    samples = cells.shape[1]
    feats = 27 * comps
    return pl.pallas_call(
        patch_kernel,
        out_shape=(
            jax.ShapeDtypeStruct((ROWS, samples), F32),
            jax.ShapeDtypeStruct((size_z, 3 * samples), BF16),
            jax.ShapeDtypeStruct((ROWS, feats * 8), BF16),
        ),
        in_specs=whole(2),
        out_specs=tuple(whole(3)),
        scratch_shapes=[
            pltpu.VMEM((comps * size_x * size_y, 3 * samples), F32),
            pltpu.VMEM((feats * 8, samples), F32),
        ],
        compiler_params=params(),
        cost_estimate=cost(1.2),
        name="patches",
    )(velocity, cells)


def edge_kernel(
    own_ref, ylo_ref, yhi_ref, info_ref, choose_ref, summing_ref, after_ref, out_ref, rows_ref,
    picked, parts, *, size_x, size_y
):
    comps, pad_x, size_z = ylo_ref.shape
    samples = info_ref.shape[1]
    rows = comps * pad_x
    cell_x, cell_y, _ = split_cells(info_ref[0:1, :], size_x, size_y, size_z)
    before, after = inside("gy")
    along = jnp.concatenate(
        [ylo_ref[...].reshape(rows, size_z) * before, yhi_ref[...].reshape(rows, size_z) * after],
        axis=0,
    ).astype(BF16)
    picked[...] = jnp.dot(along, choose_ref[...], preferred_element_type=F32)
    sub = iota((8, samples), 0)
    for side, at in ((0, cell_y == 0), (1, cell_y == size_y - 1)):
        edge_x = jnp.where(at, cell_x, -100)
        for c in range(comps):
            for p in range(3):
                masks = [sub + (8 * k - p) == edge_x for k in range(pad_x // 8)]
                sums = fold(picked, side * rows + c * pad_x, pad_x, masks, samples)
                for r in range(3):
                    put_tile(parts, feature(c, p, 2 * side, r), sums[r])
                    if side == 0:
                        put_tile(parts, feature(c, p, 1, r), None)
    out_ref[...] = own_ref[...] + add_tiles(summing_ref, parts)
    width = iota((WIDE, samples), 0)
    rows_ref[...] = jnp.concatenate([ones_where(width == cell_y + q) for q in range(3)], axis=1)


def edges(own, y_halos, cells, choose, summing, after, size_x, size_y):
    samples = cells.shape[1]
    comps, pad_x, _ = y_halos[0].shape
    return pl.pallas_call(
        functools.partial(edge_kernel, size_x=size_x, size_y=size_y),
        out_shape=(
            jax.ShapeDtypeStruct(own.shape, F32),
            jax.ShapeDtypeStruct((WIDE, 3 * samples), BF16),
        ),
        in_specs=whole(7),
        out_specs=tuple(whole(2)),
        scratch_shapes=[
            pltpu.VMEM((2 * comps * pad_x, 3 * samples), F32),
            pltpu.VMEM((summing.shape[1], samples), F32),
        ],
        compiler_params=params(),
        cost_estimate=cost(0.6),
        name="edges",
    )(own, *y_halos, cells, choose, summing, after)


def pack_kernel(
    own_ref, zlo_ref, zhi_ref, info_ref, rows_ref, summing_ref, tail_ref, placing_ref, out_ref,
    picked, parts, *, comps, sizes
):
    samples = info_ref.shape[1]
    rows = zlo_ref.shape[0]
    pad_x = rows // comps
    cell_x, _, cell_z = split_cells(info_ref[0:1, :], *sizes)
    before, after = inside("gz")
    along = jnp.concatenate([zlo_ref[...] * before, zhi_ref[...] * after], axis=0).astype(BF16)
    picked[...] = jnp.dot(along, rows_ref[...], preferred_element_type=F32)
    sub = iota((8, samples), 0)
    for side, at in ((0, cell_z == 0), (1, cell_z == sizes[2] - 1)):
        edge_x = jnp.where(at, cell_x, -100)
        for c in range(comps):
            for p in range(3):
                masks = [sub + (8 * k - p) == edge_x for k in range(pad_x // 8)]
                sums = fold(picked, side * rows + c * pad_x, pad_x, masks, samples)
                for q in range(3):
                    put_tile(parts, feature(c, p, q, 2 * side), sums[q])
                    if side == 0:
                        put_tile(parts, feature(c, p, q, 1), None)
    features = own_ref[...] + add_tiles(summing_ref, parts)
    payload = jnp.concatenate(
        [features[:TAIL], tail_ref[...], jnp.zeros((WIDE - ROWS, samples), F32)], axis=0
    ).astype(BF16)
    out_ref[...] = lax.dot_general(
        placing_ref[...], payload, NT, preferred_element_type=F32
    ).astype(BF16)


def pack(own, z_halos, cells, rows, summing, tail, placing, comps, sizes):
    samples = cells.shape[1]
    return pl.pallas_call(
        functools.partial(pack_kernel, comps=comps, sizes=sizes),
        out_shape=jax.ShapeDtypeStruct((placing.shape[0], WIDE), BF16),
        in_specs=whole(8),
        out_specs=pl.BlockSpec(memory_space=pltpu.VMEM),
        scratch_shapes=[
            pltpu.VMEM((2 * z_halos[0].shape[0], 3 * samples), F32),
            pltpu.VMEM((summing.shape[1], samples), F32),
        ],
        compiler_params=params(),
        cost_estimate=cost(0.7),
        name="pack",
    )(own, *z_halos, cells, rows, summing, tail, placing)


def advance_kernel(
    v_ref, xlo_ref, xhi_ref, ylo_ref, yhi_ref, zlo_ref, zhi_ref, out_ref, done_ref
):
    comps, size_x, size_y, size_z = v_ref.shape
    done_ref[...] = jnp.zeros_like(done_ref)
    x_before, x_after = inside("gx")
    y_before, y_after = inside("gy")
    z_before, z_after = inside("gz")

    xlo, xhi = xlo_ref[...] * x_before, xhi_ref[...] * x_after
    ylo, yhi = ylo_ref[...] * y_before, yhi_ref[...] * y_after

    def columns(face, scale):
        face = face * scale
        face = jnp.concatenate([face, jnp.zeros((WIDE - face.shape[0], WIDE), F32)], axis=0)
        return pltpu.roll(face.T, WIDE - 1, 0)[:size_y, :]

    z_low, z_high = columns(zlo_ref[...], z_before), columns(zhi_ref[...], z_after)
    y_at = iota((size_y, size_z), 0)
    z_at = iota((size_y, size_z), 1)

    def plane(c, x):
        if x < 0:
            return xlo[c]
        if x >= size_x:
            return xhi[c]
        return v_ref[c, x]

    for x in range(size_x):
        here = [plane(c, x) for c in range(comps)]
        after = [plane(c, x + 1) for c in range(comps)]
        prior = [plane(c, x - 1) for c in range(comps)]
        y_up, y_down, z_up, z_down = [], [], [], []
        for c in range(comps):
            at = c * PAD_X + x + 1
            above = yhi[c, x + 1 : x + 2, :]
            below = ylo[c, x + 1 : x + 2, :]
            y_up.append(jnp.where(y_at == size_y - 1, above, pltpu.roll(here[c], size_y - 1, 0)))
            y_down.append(jnp.where(y_at == 0, below, pltpu.roll(here[c], 1, 0)))
            z_up.append(
                jnp.where(z_at == size_z - 1, z_high[:, at : at + 1], pltpu.roll(here[c], size_z - 1, 1))
            )
            z_down.append(jnp.where(z_at == 0, z_low[:, at : at + 1], pltpu.roll(here[c], 1, 1)))
        for c in range(comps):
            diverge = after[c] * after[0] - prior[c] * prior[0]
            diverge = diverge + y_up[c] * y_up[1] - y_down[c] * y_down[1]
            diverge = diverge + z_up[c] * z_up[2] - z_down[c] * z_down[2]
            beside = after[c] + prior[c]
            beside = beside + y_up[c] + y_down[c]
            beside = beside + z_up[c] + z_down[c]
            tendency = -0.5 * diverge + VISCOSITY * (beside - 6.0 * here[c])
            out_ref[c, x] = here[c] + DT_STEP * tendency


def advance(velocity, halos):
    return pl.pallas_call(
        advance_kernel,
        out_shape=(
            jax.ShapeDtypeStruct(velocity.shape, F32),
            jax.ShapeDtypeStruct((8, WIDE), F32),
        ),
        in_specs=whole(7),
        out_specs=tuple(whole(2)),
        compiler_params=params(),
        cost_estimate=cost(1.5),
        name="advance",
    )(velocity, *halos)


def prepare_kernel(
    first_ref, middle_ref, last_ref, biases_ref, w1_ref, w2t_ref, w3_ref, w3t_ref, bias_ref, bias3_ref
):
    feats, hidden = first_ref.shape
    count = last_ref.shape[0]
    wide = jnp.concatenate(
        [first_ref[...].astype(F32), jnp.zeros((WIDE - feats, hidden), F32)], axis=0
    )
    w1_ref[...] = wide.T[:, :ROWS].astype(BF16)
    eye = ones_where(iota((hidden, hidden), 0) == iota((hidden, hidden), 1))
    w2t_ref[...] = lax.dot_general(
        eye, middle_ref[...], NT, preferred_element_type=F32
    ).astype(BF16)
    last = last_ref[...].astype(F32)
    w3_ref[...] = jnp.concatenate([last, jnp.zeros((16 - count, hidden), F32)], axis=0).astype(BF16)
    wide = jnp.concatenate([last, jnp.zeros((WIDE - count, hidden), F32)], axis=0)
    w3t_ref[...] = wide.T[:, :16].astype(BF16)
    for k in range(2 * hidden // WIDE):
        row = biases_ref[:, k * WIDE : (k + 1) * WIDE]
        bias_ref[k * WIDE : (k + 1) * WIDE, :] = jnp.broadcast_to(row, (WIDE, WIDE)).T
    tail = jnp.concatenate(
        [biases_ref[:, 2 * hidden :], jnp.zeros((1, WIDE - count), F32)], axis=1
    )
    bias3_ref[...] = jnp.broadcast_to(tail, (WIDE, WIDE)).T[:8]


def prepare(first, middle, last, biases):
    hidden = middle.shape[0]
    shapes = [
        ((hidden, ROWS), BF16),
        ((hidden, hidden), BF16),
        ((16, hidden), BF16),
        ((hidden, 16), BF16),
        ((2 * hidden, WIDE), F32),
        ((8, WIDE), F32),
    ]
    w1, w2t, w3, w3t, bias, bias3 = pl.pallas_call(
        prepare_kernel,
        out_shape=tuple(jax.ShapeDtypeStruct(*s) for s in shapes),
        in_specs=whole(4),
        out_specs=tuple(whole(6)),
        compiler_params=params(),
        cost_estimate=cost(1.0),
        name="prepare",
    )(first, middle, last, biases)
    return w1, middle, w2t, w3, w3t, bias, bias3


def turn_kernel(in_ref, prepared_ref, done_ref, out_ref):
    shape = (out_ref.shape[0], in_ref.shape[1])
    eye = ones_where(iota(shape, 0) == iota(shape, 1))
    out_ref[...] = lax.dot_general(eye, in_ref[...], NT, preferred_element_type=F32).astype(BF16)


def turn(arrived, prepared, done):
    return pl.pallas_call(
        turn_kernel,
        out_shape=jax.ShapeDtypeStruct((ROWS, arrived.shape[0]), BF16),
        in_specs=whole(3),
        out_specs=pl.BlockSpec(memory_space=pltpu.VMEM),
        compiler_params=params(),
        cost_estimate=cost(0.2),
        name="turn",
    )(arrived, prepared, done)


def lane_sum(value):
    total = value[:, :WIDE]
    for k in range(1, value.shape[1] // WIDE):
        total = total + value[:, k * WIDE : (k + 1) * WIDE]
    return total


def train_kernel(*refs, planes, row_count, first, last, own_rows):
    refs = list(refs)
    take = lambda n: [refs.pop(0) for _ in range(n)]
    x_refs = take(len(planes))
    w1_ref, w2_ref, w2t_ref, w3_ref, w3t_ref, bias_ref, bias3_ref = take(7)
    held = [] if first else take(6)
    if last:
        momentum_ref, master_ref = take(2)
        first_ref, last_ref, bias_grads_ref, master_new_ref, momentum_new_ref = take(5)
        sums = take(6)
    else:
        sums = take(6)
    if first:
        loss_ref = take(1)[0]
    back_two_ref = take(1)[0]
    g1, g2, g3, s1, s2, s3 = sums
    hidden = w2_ref.shape[0]
    factor = 2.0 / (6.0 * row_count)
    olds = dict(zip(map(id, sums), held))

    def add(ref, value):
        ref[...] = value if first else olds[id(ref)][...] + value

    own = pl.multiple_of(lax.axis_index("gz") * own_rows, own_rows)

    per_row = hidden // WIDE
    across = lambda s: jnp.sum(s.T, axis=0, keepdims=True)

    def finish_early():
        grads = g2[...]
        for k in range(per_row):
            at = pl.ds(k, own_rows, stride=per_row)
            momentum = MOMENTUM_KEEP * momentum_ref[at, :] + grads[:, k * WIDE : (k + 1) * WIDE]
            momentum_new_ref[at, :] = momentum
            master_new_ref[at, :] = master_ref[at, :] - LEARN_RATE * momentum
        for k in range(last_ref.shape[0]):
            last_ref[k] = g3[k : k + 1, :]
        bias_grads_ref[:, hidden : 2 * hidden] = across(s2[...])
        third = across(jnp.concatenate([s3[...], jnp.zeros((WIDE - 8, WIDE), F32)], axis=0))
        bias_grads_ref[:, 2 * hidden :] = third[:, :6]

    def plane(x):
        slots = x.shape[1]
        reps = slots // WIDE
        spread = lambda b: jnp.concatenate([b] * reps, axis=1)
        act_one = jnp.tanh(
            jnp.dot(w1_ref[...], x, preferred_element_type=F32) + spread(bias_ref[:hidden, :])
        ).astype(BF16)
        act_two = jnp.tanh(
            jnp.dot(w2_ref[...], act_one, preferred_element_type=F32) + spread(bias_ref[hidden:, :])
        ).astype(BF16)
        ending = x[ROWS - 16 :, :].astype(F32)[8:, :]
        predicted = jnp.dot(w3_ref[...], act_two, preferred_element_type=F32)[:8, :]
        predicted = predicted + spread(bias3_ref[...])
        mismatch = jnp.where(
            iota((8, slots), 0) < 6, (predicted - ending) * ending[6:7, :], 0.0
        )
        delta_three = mismatch * factor
        add(s3, lane_sum(delta_three))
        back_three = jnp.concatenate([delta_three, jnp.zeros_like(delta_three)], axis=0).astype(BF16)
        add(g3, lax.dot_general(back_three, act_two, NT, preferred_element_type=F32))
        wide_two = act_two.astype(F32)
        delta_two = jnp.dot(w3t_ref[...], back_three, preferred_element_type=F32) * (
            1.0 - wide_two * wide_two
        )
        add(s2, lane_sum(delta_two))
        back_two = delta_two.astype(BF16)
        back_two_ref[...] = back_two
        mine = back_two_ref[pl.ds(own, own_rows), :]
        add(g2, lax.dot_general(mine, act_one, NT, preferred_element_type=F32))
        if last:
            finish_early()
        wide_one = act_one.astype(F32)
        delta_one = jnp.dot(w2t_ref[...], back_two, preferred_element_type=F32) * (
            1.0 - wide_one * wide_one
        )
        add(s1, lane_sum(delta_one))
        back_one = delta_one.astype(BF16)
        add(g1, lax.dot_general(back_one, x, NT, preferred_element_type=F32))
        return mismatch

    pieces = []
    for ref, count in zip(x_refs, planes):
        pieces += [ref[...]] if count == 1 else [ref[k] for k in range(count)]
    mismatch = plane(pieces[0] if len(pieces) == 1 else jnp.concatenate(pieces, axis=1))

    if first:
        row_loss = jnp.sum(mismatch * mismatch, axis=0, keepdims=True) / (6.0 * row_count)
        loss_ref[...] = jnp.sum(row_loss, axis=1, keepdims=True)
    if last:
        wide = jnp.concatenate([g1[...], jnp.zeros((hidden, WIDE - ROWS), F32)], axis=1).T
        for k in range(first_ref.shape[0]):
            first_ref[k] = wide[k : k + 1, :]
        bias_grads_ref[:, :hidden] = across(s1[...])


def train(xs, weights, held, optimizer, row_count, own_rows):
    planes = tuple(x.shape[0] if x.ndim == 3 else 1 for x in xs)
    slots = xs[0].shape[-1]
    hidden = weights[1].shape[0]
    first, last = held is None, optimizer is not None
    sums = [
        jax.ShapeDtypeStruct(s, F32)
        for s in (
            (hidden, ROWS),
            (own_rows, hidden),
            (16, hidden),
            (hidden, WIDE),
            (hidden, WIDE),
            (8, WIDE),
        )
    ]
    scratch = [pltpu.VMEM((hidden, slots * sum(planes)), BF16)]
    if last:
        out = [
            jax.ShapeDtypeStruct(s, F32)
            for s in (
                (81, 1, hidden),
                (6, 1, hidden),
                (1, 2 * hidden + 6),
                optimizer[0].shape,
                optimizer[0].shape,
            )
        ]
        scratch = [pltpu.VMEM(s.shape, F32) for s in sums] + scratch
    else:
        out = list(sums)
    if first:
        out.append(jax.ShapeDtypeStruct((1, 1), F32))
    operands = [*xs, *weights, *(held or ()), *(optimizer or ())]
    count = sum(planes)
    return pl.pallas_call(
        functools.partial(
            train_kernel,
            planes=planes,
            row_count=row_count,
            first=first,
            last=last,
            own_rows=own_rows,
        ),
        out_shape=tuple(out),
        in_specs=whole(len(operands)),
        out_specs=tuple(whole(len(out))),
        scratch_shapes=scratch,
        compiler_params=params(),
        cost_estimate=cost(1.6 * count),
        name="train",
    )(*operands)


def on_device(
    velocity,
    sample_cells,
    trainer_of,
    targets,
    w_first,
    w_middle,
    w_last,
    biases,
    middle_master,
    middle_momentum,
):
    comps, size_x, size_y, size_z = velocity.shape
    samples = sample_cells.shape[0]
    trainers = lax.axis_size("gx") * lax.axis_size("gy")
    capacity = 2 * samples // trainers
    slots = trainers * capacity
    hidden = w_middle.shape[1]
    planes = lax.axis_size("gz")
    own_rows = hidden // planes

    info = jnp.stack([sample_cells, trainer_of[:, 0]])
    x_halos = exchange("gx", *x_faces(velocity))
    features, choose, summing = patches(velocity, info)
    y_halos = exchange("gy", *y_faces(velocity, x_halos, features))
    z_low, z_high, placing, features = plan(
        velocity,
        x_halos,
        info,
        features,
        choose,
        summing,
        trainers,
        slots,
    )
    z_ends = z_faces(z_low, z_high, y_halos, size_y)
    z_halos = exchange("gz", *z_ends)
    features, rows = edges(features, y_halos, info, choose, summing, z_ends[0], size_x, size_y)
    tail = jnp.concatenate(
        [targets.astype(F32), jnp.ones((1, samples), F32), jnp.zeros((1, samples), F32)], axis=0
    )
    packed = pack(
        features, z_halos, info, rows, summing, tail, placing, comps, (size_x, size_y, size_z)
    )
    arrived = lax.all_to_all(
        packed.reshape(trainers, capacity, WIDE),
        ("gy", "gx"),
        split_axis=0,
        concat_axis=0,
        tiled=True,
    ).reshape(slots, WIDE)
    new_velocity, done = advance(velocity, (*x_halos, *y_halos, *z_halos))

    weights = prepare(w_first[0].T, w_middle[0], w_last[0], biases)
    optimizer = (
        middle_momentum.reshape(-1, WIDE),
        middle_master.reshape(-1, WIDE),
    )

    mine = turn(arrived, weights[-1], done)
    call = functools.partial(train, weights=weights, row_count=samples, own_rows=own_rows)
    swap = [(i, i ^ 1) for i in range(planes)]
    chips = planes // 2
    along = lambda to: [(i, 2 * (to(i // 2) % chips) + i % 2) for i in range(planes)]
    beside = lax.ppermute(mine, "gz", swap)
    far = lax.ppermute(mine, "gz", along(lambda x: x + 2))
    *held, loss = call([mine], held=None, optimizer=None)
    beside, far, *held = lax.optimization_barrier((beside, far, *held))
    both = jnp.stack([mine, beside])
    near = [
        lax.ppermute(both, "gz", along(lambda x: x ^ 1)),
        lax.ppermute(both, "gz", along(lambda x: x + 1 if x % 2 else x - 1)),
    ]
    far_beside = lax.ppermute(far, "gz", swap)
    held = call([beside, far], held=held, optimizer=None)
    first_grads, last_grads, bias_grads, master_new, momentum_new = call(
        [*near, far_beside], held=held, optimizer=optimizer
    )
    return (
        new_velocity,
        loss.reshape(1, 1, 1),
        first_grads.transpose(1, 2, 0),
        last_grads.transpose(1, 0, 2),
        bias_grads,
        master_new.reshape(middle_master.shape),
        momentum_new.reshape(middle_momentum.shape),
    )


def solution(mesh):
    placed = (
        P(None, "gx", "gy", "gz"),
        P(("gx", "gy", "gz")),
        P(("gx", "gy", "gz"), None),
        P(None, ("gx", "gy", "gz")),
        P(("gx", "gy"), None, None),
        P(("gx", "gy"), None, None),
        P(("gx", "gy"), None, None),
        P(("gx", "gy"), None),
        P(("gx", "gy"), "gz"),
        P(("gx", "gy"), "gz"),
    )
    return jax.shard_map(
        on_device,
        mesh=mesh,
        in_specs=placed,
        out_specs=(
            P(None, "gx", "gy", "gz"),
            P("gx", "gy", "gz"),
            P(("gx", "gy"), None, None),
            P(("gx", "gy"), None, None),
            P(("gx", "gy"), None),
            P(("gx", "gy"), "gz"),
            P(("gx", "gy"), "gz"),
        ),
        check_vma=False,
    )
```

```python
import functools

import jax
import jax.numpy as jnp
from jax import lax
from jax.experimental import pallas as pl
from jax.experimental.pallas import tpu as pltpu
from jax.sharding import PartitionSpec as P

DT_STEP = 0.1
VISCOSITY = 0.2
LEARN_RATE = 0.05
MOMENTUM_KEEP = 0.9

BF16 = jnp.bfloat16
F32 = jnp.float32
I32 = jnp.int32
NT = (((1,), (1,)), ((), ()))
TN = (((0,), (0,)), ((), ()))
EXACT = lax.Precision.HIGHEST
VMEM_LIMIT = 48 * 1024 * 1024
ROWS = 96
TAIL = 88
WIDE = 128
PAD_X = 16


def params(limit=VMEM_LIMIT):
    return pltpu.CompilerParams(vmem_limit_bytes=limit)


def cost(micros):
    return pl.CostEstimate(
        flops=int(micros * 800_000_000), bytes_accessed=1_000_000, transcendentals=0
    )


def inside(axis):
    at = lax.axis_index(axis)
    return (
        jnp.where(at > 0, 1.0, 0.0).astype(F32),
        jnp.where(at < lax.axis_size(axis) - 1, 1.0, 0.0).astype(F32),
    )


def whole(count):
    return [pl.BlockSpec(memory_space=pltpu.VMEM)] * count


def iota(shape, dim):
    return lax.broadcasted_iota(I32, shape, dim)


def ones_where(mask):
    return jnp.where(mask, 1.0, 0.0).astype(BF16)


def exchange(axis, low_face, high_face):
    count = lax.axis_size(axis)
    forward = [(i, (i + 1) % count) for i in range(count)]
    backward = [(b, a) for a, b in forward]
    return lax.ppermute(high_face, axis, forward), lax.ppermute(low_face, axis, backward)


def faces_kernel(low_ref, high_ref, to_low_ref, to_high_ref):
    to_low_ref[...] = low_ref[:, 0]
    to_high_ref[...] = high_ref[:, 0]


def x_faces(velocity):
    comps, size_x, size_y, size_z = velocity.shape
    spec = lambda at: pl.BlockSpec((comps, 1, size_y, size_z), lambda i: (0, at, 0, 0))
    out = pl.BlockSpec((comps, size_y, size_z), lambda i: (0, 0, 0))
    return pl.pallas_call(
        faces_kernel,
        grid=(1,),
        out_shape=tuple([jax.ShapeDtypeStruct((comps, size_y, size_z), F32)] * 2),
        in_specs=[spec(0), spec(size_x - 1)],
        out_specs=(out, out),
        compiler_params=params(),
        cost_estimate=cost(0.3),
        name="x_faces",
    )(velocity, velocity)


def end_rows(block, low_ref, high_ref, row_of, size_y):
    size_z = block.shape[1]
    row, lane = iota((8, size_z), 0), iota((8, size_z), 1)
    pick = jnp.where(
        ((row == 0) & (lane == 0)) | ((row == 1) & (lane == size_z - 1)), 1.0, 0.0
    ).astype(F32)
    ends = lax.dot_general(pick, block, NT, precision=EXACT, preferred_element_type=F32)
    for k in range(block.shape[0] // size_y):
        at = row_of(k)
        low_ref[at : at + 1, 1 : size_y + 1] = ends[0:1, k * size_y : (k + 1) * size_y]
        high_ref[at : at + 1, 1 : size_y + 1] = ends[1:2, k * size_y : (k + 1) * size_y]


def split_cells(cells, size_x, size_y, size_z):
    return cells // (size_y * size_z), cells // size_z % size_y, cells % size_z


def depth_choice(cell_z, size_z):
    depth = iota((size_z, cell_z.shape[1]), 0)
    return jnp.concatenate([ones_where(depth == cell_z + (r - 1)) for r in range(3)], axis=1)


def fold(ref, first, rows, masks, samples):
    sums = [None] * 3
    for k in range(rows // 8):
        for r in range(3):
            piece = ref[first + 8 * k : first + 8 * k + 8, r * samples : (r + 1) * samples]
            piece = jnp.where(masks[k], piece, 0.0)
            sums[r] = piece if sums[r] is None else sums[r] + piece
    return sums


def feature(c, p, q, r):
    return 27 * c + 9 * p + 3 * q + r


def tile_sums(feats):
    shape = (ROWS, feats * 8)
    return ones_where(lax.shift_right_logical(iota(shape, 1), 3) == iota(shape, 0))


def put_tile(parts, f, total):
    parts[f * 8 : (f + 1) * 8, :] = jnp.zeros((8, parts.shape[1]), F32) if total is None else total


def add_tiles(summing, parts):
    return jnp.dot(summing[...], parts[...].astype(BF16), preferred_element_type=F32)


def plan_kernel(
    v_ref,
    xlo_ref,
    xhi_ref,
    info_ref,
    own_ref,
    choose_ref,
    summing_ref,
    z_low_ref,
    z_high_ref,
    placing_ref,
    out_ref,
    picked,
    parts,
    *,
    trainers,
):
    comps, size_x, size_y, size_z = v_ref.shape
    for ref in (z_low_ref, z_high_ref):
        ref[...] = jnp.zeros_like(ref)
    end_rows(
        v_ref[...].reshape(-1, size_z),
        z_low_ref,
        z_high_ref,
        lambda k: k // size_x * PAD_X + k % size_x + 1,
        size_y,
    )
    before, after = inside("gx")
    for ref, scale, x in ((xlo_ref, before, 0), (xhi_ref, after, size_x + 1)):
        block = ref[...].reshape(-1, size_z) * scale
        end_rows(block, z_low_ref, z_high_ref, lambda k: k * PAD_X + x, size_y)
        first = 0 if x == 0 else block.shape[0]
        picked[first : first + block.shape[0], :] = jnp.dot(
            block.astype(BF16), choose_ref[...], preferred_element_type=F32
        )
    samples = info_ref.shape[1]
    cell_x, cell_y, _ = split_cells(info_ref[0:1, :], size_x, size_y, size_z)
    sub = iota((8, samples), 0)
    for side, at in ((0, cell_x == 0), (1, cell_x == size_x - 1)):
        edge_y = jnp.where(at, cell_y, -100)
        for c in range(comps):
            for q in range(3):
                masks = [sub + (8 * k - q + 1) == edge_y for k in range(size_y // 8)]
                sums = fold(picked, (side * comps + c) * size_y, size_y, masks, samples)
                for r in range(3):
                    put_tile(parts, feature(c, 2 * side, q, r), sums[r])
                    if side == 0:
                        put_tile(parts, feature(c, 1, q, r), None)
    out_ref[...] = own_ref[...] + add_tiles(summing_ref, parts)

    trainer = info_ref[1:2, :]
    slots = placing_ref.shape[0]
    capacity = slots // trainers
    same = iota((trainers, samples), 0) == trainer
    earlier = ones_where(iota((samples, samples), 0) < iota((samples, samples), 1))
    before = jnp.dot(ones_where(same), earlier, preferred_element_type=F32)
    position = jnp.sum(jnp.where(same, before, 0.0), axis=0, keepdims=True).astype(I32)
    columns = lax.axis_size("gy")
    block = trainer % columns * (trainers // columns) + trainer // columns
    slot = block * capacity + position
    placing_ref[...] = ones_where(iota((slots, samples), 0) == slot)


def plan(velocity, x_halos, info, own, choose, summing, trainers, slots):
    comps, size_x, size_y, size_z = velocity.shape
    z_face = jax.ShapeDtypeStruct((comps * PAD_X, WIDE), F32)
    placing = jax.ShapeDtypeStruct((slots, info.shape[1]), BF16)
    return pl.pallas_call(
        functools.partial(plan_kernel, trainers=trainers),
        out_shape=(z_face, z_face, placing, jax.ShapeDtypeStruct(own.shape, F32)),
        in_specs=whole(7),
        out_specs=tuple(whole(4)),
        scratch_shapes=[
            pltpu.VMEM((2 * comps * size_y, choose.shape[1]), F32),
            pltpu.VMEM((summing.shape[1], own.shape[1]), F32),
        ],
        compiler_params=params(),
        cost_estimate=cost(1.5),
        name="plan",
    )(velocity, *x_halos, info, own, choose, summing)


def y_faces_kernel(low_ref, high_ref, xlo_ref, xhi_ref, after_ref, to_low_ref, to_high_ref):
    comps, size_x = low_ref.shape[0], low_ref.shape[1]
    before, after = inside("gx")
    last = xlo_ref.shape[1] - 1
    for to, own, row, y in ((to_low_ref, low_ref, 0, 0), (to_high_ref, high_ref, 7, last)):
        to[...] = jnp.zeros_like(to)
        for c in range(comps):
            to[c, 0:1, :] = xlo_ref[c, y : y + 1, :] * before
            for x in range(size_x):
                to[c, x + 1 : x + 2, :] = own[c, x, row : row + 1, :]
            to[c, size_x + 1 : size_x + 2, :] = xhi_ref[c, y : y + 1, :] * after


def y_faces(velocity, x_halos, after):
    comps, size_x, size_y, size_z = velocity.shape
    shape = (comps, PAD_X, size_z)
    spec = lambda at: pl.BlockSpec((comps, size_x, 8, size_z), lambda i: (0, 0, at, 0))
    full = lambda a: pl.BlockSpec(a, lambda i: (0,) * len(a))
    return pl.pallas_call(
        y_faces_kernel,
        grid=(1,),
        out_shape=tuple([jax.ShapeDtypeStruct(shape, F32)] * 2),
        in_specs=[spec(0), spec(size_y // 8 - 1)] + [full(x_halos[0].shape)] * 2 + [full(after.shape)],
        out_specs=(full(shape), full(shape)),
        compiler_params=params(),
        cost_estimate=cost(0.3),
        name="y_faces",
    )(velocity, velocity, *x_halos, after)


def z_faces_kernel(low_ref, high_ref, ylo_ref, yhi_ref, to_low_ref, to_high_ref, *, size_y):
    before, after = inside("gy")
    size_z = ylo_ref.shape[2]
    ylo = ylo_ref[...].reshape(-1, size_z) * before
    yhi = yhi_ref[...].reshape(-1, size_z) * after
    lane = iota(low_ref.shape, 1)
    for own, to, z in ((low_ref, to_low_ref, 0), (high_ref, to_high_ref, size_z - 1)):
        face = jnp.where(lane == 0, ylo[:, z : z + 1], own[...])
        to[...] = jnp.where(lane == size_y + 1, yhi[:, z : z + 1], face)


def z_faces(low, high, y_halos, size_y):
    return pl.pallas_call(
        functools.partial(z_faces_kernel, size_y=size_y),
        out_shape=tuple([jax.ShapeDtypeStruct(low.shape, F32)] * 2),
        in_specs=whole(4),
        out_specs=tuple(whole(2)),
        compiler_params=params(),
        cost_estimate=cost(0.3),
        name="z_faces",
    )(low, high, *y_halos)


def patch_kernel(v_ref, info_ref, out_ref, choose_ref, summing_ref, picked, parts):
    comps, size_x, size_y, size_z = v_ref.shape
    samples = info_ref.shape[1]
    cell_x, cell_y, cell_z = split_cells(info_ref[0:1, :], size_x, size_y, size_z)
    choose_ref[...] = depth_choice(cell_z, size_z)
    picked[...] = jnp.dot(
        v_ref[...].reshape(-1, size_z).astype(BF16), choose_ref[...], preferred_element_type=F32
    )
    sub = iota((8, samples), 0)
    at_x = [cell_x == j for j in range(size_x)]
    for c in range(comps):
        for q in range(3):
            masks = [sub + (8 * k - q + 1) == cell_y for k in range(size_y // 8)]
            totals = [[None] * 3 for _ in range(3)]
            for x in range(size_x):
                sums = fold(picked, (c * size_x + x) * size_y, size_y, masks, samples)
                for p in range(3):
                    j = x + 1 - p
                    if 0 <= j < size_x:
                        for r in range(3):
                            piece = jnp.where(at_x[j], sums[r], 0.0)
                            totals[p][r] = piece if totals[p][r] is None else totals[p][r] + piece
            for p in range(3):
                for r in range(3):
                    put_tile(parts, feature(c, p, q, r), totals[p][r])
    summing_ref[...] = tile_sums(27 * comps)
    out_ref[...] = add_tiles(summing_ref, parts)


def patches(velocity, cells):
    comps, size_x, size_y, size_z = velocity.shape
    samples = cells.shape[1]
    feats = 27 * comps
    return pl.pallas_call(
        patch_kernel,
        out_shape=(
            jax.ShapeDtypeStruct((ROWS, samples), F32),
            jax.ShapeDtypeStruct((size_z, 3 * samples), BF16),
            jax.ShapeDtypeStruct((ROWS, feats * 8), BF16),
        ),
        in_specs=whole(2),
        out_specs=tuple(whole(3)),
        scratch_shapes=[
            pltpu.VMEM((comps * size_x * size_y, 3 * samples), F32),
            pltpu.VMEM((feats * 8, samples), F32),
        ],
        compiler_params=params(),
        cost_estimate=cost(1.2),
        name="patches",
    )(velocity, cells)


def edge_kernel(
    own_ref, ylo_ref, yhi_ref, info_ref, choose_ref, summing_ref, after_ref, out_ref, rows_ref,
    picked, parts, *, size_x, size_y
):
    comps, pad_x, size_z = ylo_ref.shape
    samples = info_ref.shape[1]
    rows = comps * pad_x
    cell_x, cell_y, _ = split_cells(info_ref[0:1, :], size_x, size_y, size_z)
    before, after = inside("gy")
    along = jnp.concatenate(
        [ylo_ref[...].reshape(rows, size_z) * before, yhi_ref[...].reshape(rows, size_z) * after],
        axis=0,
    ).astype(BF16)
    picked[...] = jnp.dot(along, choose_ref[...], preferred_element_type=F32)
    sub = iota((8, samples), 0)
    for side, at in ((0, cell_y == 0), (1, cell_y == size_y - 1)):
        edge_x = jnp.where(at, cell_x, -100)
        for c in range(comps):
            for p in range(3):
                masks = [sub + (8 * k - p) == edge_x for k in range(pad_x // 8)]
                sums = fold(picked, side * rows + c * pad_x, pad_x, masks, samples)
                for r in range(3):
                    put_tile(parts, feature(c, p, 2 * side, r), sums[r])
                    if side == 0:
                        put_tile(parts, feature(c, p, 1, r), None)
    out_ref[...] = own_ref[...] + add_tiles(summing_ref, parts)
    width = iota((WIDE, samples), 0)
    rows_ref[...] = jnp.concatenate([ones_where(width == cell_y + q) for q in range(3)], axis=1)


def edges(own, y_halos, cells, choose, summing, after, size_x, size_y):
    samples = cells.shape[1]
    comps, pad_x, _ = y_halos[0].shape
    return pl.pallas_call(
        functools.partial(edge_kernel, size_x=size_x, size_y=size_y),
        out_shape=(
            jax.ShapeDtypeStruct(own.shape, F32),
            jax.ShapeDtypeStruct((WIDE, 3 * samples), BF16),
        ),
        in_specs=whole(7),
        out_specs=tuple(whole(2)),
        scratch_shapes=[
            pltpu.VMEM((2 * comps * pad_x, 3 * samples), F32),
            pltpu.VMEM((summing.shape[1], samples), F32),
        ],
        compiler_params=params(),
        cost_estimate=cost(0.6),
        name="edges",
    )(own, *y_halos, cells, choose, summing, after)


def pack_kernel(
    own_ref, zlo_ref, zhi_ref, info_ref, rows_ref, summing_ref, tail_ref, placing_ref, out_ref,
    picked, parts, *, comps, sizes
):
    samples = info_ref.shape[1]
    rows = zlo_ref.shape[0]
    pad_x = rows // comps
    cell_x, _, cell_z = split_cells(info_ref[0:1, :], *sizes)
    before, after = inside("gz")
    along = jnp.concatenate([zlo_ref[...] * before, zhi_ref[...] * after], axis=0).astype(BF16)
    picked[...] = jnp.dot(along, rows_ref[...], preferred_element_type=F32)
    sub = iota((8, samples), 0)
    for side, at in ((0, cell_z == 0), (1, cell_z == sizes[2] - 1)):
        edge_x = jnp.where(at, cell_x, -100)
        for c in range(comps):
            for p in range(3):
                masks = [sub + (8 * k - p) == edge_x for k in range(pad_x // 8)]
                sums = fold(picked, side * rows + c * pad_x, pad_x, masks, samples)
                for q in range(3):
                    put_tile(parts, feature(c, p, q, 2 * side), sums[q])
                    if side == 0:
                        put_tile(parts, feature(c, p, q, 1), None)
    features = own_ref[...] + add_tiles(summing_ref, parts)
    payload = jnp.concatenate(
        [features[:TAIL], tail_ref[...], jnp.zeros((WIDE - ROWS, samples), F32)], axis=0
    ).astype(BF16)
    out_ref[...] = lax.dot_general(
        placing_ref[...], payload, NT, preferred_element_type=F32
    ).astype(BF16)


def pack(own, z_halos, cells, rows, summing, tail, placing, comps, sizes):
    samples = cells.shape[1]
    return pl.pallas_call(
        functools.partial(pack_kernel, comps=comps, sizes=sizes),
        out_shape=jax.ShapeDtypeStruct((placing.shape[0], WIDE), BF16),
        in_specs=whole(8),
        out_specs=pl.BlockSpec(memory_space=pltpu.VMEM),
        scratch_shapes=[
            pltpu.VMEM((2 * z_halos[0].shape[0], 3 * samples), F32),
            pltpu.VMEM((summing.shape[1], samples), F32),
        ],
        compiler_params=params(),
        cost_estimate=cost(0.7),
        name="pack",
    )(own, *z_halos, cells, rows, summing, tail, placing)


def advance_kernel(
    v_ref, xlo_ref, xhi_ref, ylo_ref, yhi_ref, zlo_ref, zhi_ref, out_ref, done_ref
):
    comps, size_x, size_y, size_z = v_ref.shape
    done_ref[...] = jnp.zeros_like(done_ref)
    x_before, x_after = inside("gx")
    y_before, y_after = inside("gy")
    z_before, z_after = inside("gz")

    xlo, xhi = xlo_ref[...] * x_before, xhi_ref[...] * x_after
    ylo, yhi = ylo_ref[...] * y_before, yhi_ref[...] * y_after

    def columns(face, scale):
        face = face * scale
        face = jnp.concatenate([face, jnp.zeros((WIDE - face.shape[0], WIDE), F32)], axis=0)
        return pltpu.roll(face.T, WIDE - 1, 0)[:size_y, :]

    z_low, z_high = columns(zlo_ref[...], z_before), columns(zhi_ref[...], z_after)
    y_at = iota((size_y, size_z), 0)
    z_at = iota((size_y, size_z), 1)

    def plane(c, x):
        if x < 0:
            return xlo[c]
        if x >= size_x:
            return xhi[c]
        return v_ref[c, x]

    for x in range(size_x):
        here = [plane(c, x) for c in range(comps)]
        after = [plane(c, x + 1) for c in range(comps)]
        prior = [plane(c, x - 1) for c in range(comps)]
        y_up, y_down, z_up, z_down = [], [], [], []
        for c in range(comps):
            at = c * PAD_X + x + 1
            above = yhi[c, x + 1 : x + 2, :]
            below = ylo[c, x + 1 : x + 2, :]
            y_up.append(jnp.where(y_at == size_y - 1, above, pltpu.roll(here[c], size_y - 1, 0)))
            y_down.append(jnp.where(y_at == 0, below, pltpu.roll(here[c], 1, 0)))
            z_up.append(
                jnp.where(z_at == size_z - 1, z_high[:, at : at + 1], pltpu.roll(here[c], size_z - 1, 1))
            )
            z_down.append(jnp.where(z_at == 0, z_low[:, at : at + 1], pltpu.roll(here[c], 1, 1)))
        for c in range(comps):
            diverge = after[c] * after[0] - prior[c] * prior[0]
            diverge = diverge + y_up[c] * y_up[1] - y_down[c] * y_down[1]
            diverge = diverge + z_up[c] * z_up[2] - z_down[c] * z_down[2]
            beside = after[c] + prior[c]
            beside = beside + y_up[c] + y_down[c]
            beside = beside + z_up[c] + z_down[c]
            tendency = -0.5 * diverge + VISCOSITY * (beside - 6.0 * here[c])
            out_ref[c, x] = here[c] + DT_STEP * tendency


def advance(velocity, halos):
    return pl.pallas_call(
        advance_kernel,
        out_shape=(
            jax.ShapeDtypeStruct(velocity.shape, F32),
            jax.ShapeDtypeStruct((8, WIDE), F32),
        ),
        in_specs=whole(7),
        out_specs=tuple(whole(2)),
        compiler_params=params(),
        cost_estimate=cost(1.5),
        name="advance",
    )(velocity, *halos)


def prepare_kernel(
    first_ref, middle_ref, last_ref, biases_ref, w1_ref, w2t_ref, w3_ref, w3t_ref, bias_ref, bias3_ref
):
    feats, hidden = first_ref.shape
    count = last_ref.shape[0]
    wide = jnp.concatenate(
        [first_ref[...].astype(F32), jnp.zeros((WIDE - feats, hidden), F32)], axis=0
    )
    w1_ref[...] = wide.T[:, :ROWS].astype(BF16)
    eye = ones_where(iota((hidden, hidden), 0) == iota((hidden, hidden), 1))
    w2t_ref[...] = lax.dot_general(
        eye, middle_ref[...], NT, preferred_element_type=F32
    ).astype(BF16)
    last = last_ref[...].astype(F32)
    w3_ref[...] = jnp.concatenate([last, jnp.zeros((16 - count, hidden), F32)], axis=0).astype(BF16)
    wide = jnp.concatenate([last, jnp.zeros((WIDE - count, hidden), F32)], axis=0)
    w3t_ref[...] = wide.T[:, :16].astype(BF16)
    for k in range(2 * hidden // WIDE):
        row = biases_ref[:, k * WIDE : (k + 1) * WIDE]
        bias_ref[k * WIDE : (k + 1) * WIDE, :] = jnp.broadcast_to(row, (WIDE, WIDE)).T
    tail = jnp.concatenate(
        [biases_ref[:, 2 * hidden :], jnp.zeros((1, WIDE - count), F32)], axis=1
    )
    bias3_ref[...] = jnp.broadcast_to(tail, (WIDE, WIDE)).T[:8]


def prepare(first, middle, last, biases):
    hidden = middle.shape[0]
    shapes = [
        ((hidden, ROWS), BF16),
        ((hidden, hidden), BF16),
        ((16, hidden), BF16),
        ((hidden, 16), BF16),
        ((2 * hidden, WIDE), F32),
        ((8, WIDE), F32),
    ]
    w1, w2t, w3, w3t, bias, bias3 = pl.pallas_call(
        prepare_kernel,
        out_shape=tuple(jax.ShapeDtypeStruct(*s) for s in shapes),
        in_specs=whole(4),
        out_specs=tuple(whole(6)),
        compiler_params=params(),
        cost_estimate=cost(1.0),
        name="prepare",
    )(first, middle, last, biases)
    return w1, middle, w2t, w3, w3t, bias, bias3


def turn_kernel(in_ref, prepared_ref, done_ref, out_ref):
    shape = (out_ref.shape[0], in_ref.shape[1])
    eye = ones_where(iota(shape, 0) == iota(shape, 1))
    out_ref[...] = lax.dot_general(eye, in_ref[...], NT, preferred_element_type=F32).astype(BF16)


def turn(arrived, prepared, done):
    return pl.pallas_call(
        turn_kernel,
        out_shape=jax.ShapeDtypeStruct((ROWS, arrived.shape[0]), BF16),
        in_specs=whole(3),
        out_specs=pl.BlockSpec(memory_space=pltpu.VMEM),
        compiler_params=params(),
        cost_estimate=cost(0.2),
        name="turn",
    )(arrived, prepared, done)


def lane_sum(value):
    total = value[:, :WIDE]
    for k in range(1, value.shape[1] // WIDE):
        total = total + value[:, k * WIDE : (k + 1) * WIDE]
    return total


def train_kernel(*refs, planes, row_count, first, last, own_rows):
    refs = list(refs)
    take = lambda n: [refs.pop(0) for _ in range(n)]
    x_refs = take(len(planes))
    w1_ref, w2_ref, w2t_ref, w3_ref, w3t_ref, bias_ref, bias3_ref = take(7)
    held = [] if first else take(6)
    if last:
        momentum_ref, master_ref = take(2)
        first_ref, last_ref, bias_grads_ref, master_new_ref, momentum_new_ref = take(5)
        sums = take(6)
    else:
        sums = take(6)
    if first:
        loss_ref = take(1)[0]
    back_two_ref = take(1)[0]
    g1, g2, g3, s1, s2, s3 = sums
    hidden = w2_ref.shape[0]
    factor = 2.0 / (6.0 * row_count)
    olds = dict(zip(map(id, sums), held))

    def add(ref, value):
        ref[...] = value if first else olds[id(ref)][...] + value

    own = pl.multiple_of(lax.axis_index("gz") * own_rows, own_rows)

    per_row = hidden // WIDE
    across = lambda s: jnp.sum(s.T, axis=0, keepdims=True)

    def finish_early():
        grads = g2[...]
        for k in range(per_row):
            at = pl.ds(k, own_rows, stride=per_row)
            momentum = MOMENTUM_KEEP * momentum_ref[at, :] + grads[:, k * WIDE : (k + 1) * WIDE]
            momentum_new_ref[at, :] = momentum
            master_new_ref[at, :] = master_ref[at, :] - LEARN_RATE * momentum
        for k in range(last_ref.shape[0]):
            last_ref[k] = g3[k : k + 1, :]
        bias_grads_ref[:, hidden : 2 * hidden] = across(s2[...])
        third = across(jnp.concatenate([s3[...], jnp.zeros((WIDE - 8, WIDE), F32)], axis=0))
        bias_grads_ref[:, 2 * hidden :] = third[:, :6]

    def plane(x):
        slots = x.shape[1]
        reps = slots // WIDE
        spread = lambda b: jnp.concatenate([b] * reps, axis=1)
        act_one = jnp.tanh(
            jnp.dot(w1_ref[...], x, preferred_element_type=F32) + spread(bias_ref[:hidden, :])
        ).astype(BF16)
        act_two = jnp.tanh(
            jnp.dot(w2_ref[...], act_one, preferred_element_type=F32) + spread(bias_ref[hidden:, :])
        ).astype(BF16)
        ending = x[ROWS - 16 :, :].astype(F32)[8:, :]
        predicted = jnp.dot(w3_ref[...], act_two, preferred_element_type=F32)[:8, :]
        predicted = predicted + spread(bias3_ref[...])
        mismatch = jnp.where(
            iota((8, slots), 0) < 6, (predicted - ending) * ending[6:7, :], 0.0
        )
        delta_three = mismatch * factor
        add(s3, lane_sum(delta_three))
        back_three = jnp.concatenate([delta_three, jnp.zeros_like(delta_three)], axis=0).astype(BF16)
        wide_two = act_two.astype(F32)
        delta_two = jnp.dot(w3t_ref[...], back_three, preferred_element_type=F32) * (
            1.0 - wide_two * wide_two
        )
        add(s2, lane_sum(delta_two))
        back_two = delta_two.astype(BF16)
        back_two_ref[...] = back_two
        add(g3, lax.dot_general(back_three, act_two, NT, preferred_element_type=F32))
        mine = back_two_ref[pl.ds(own, own_rows), :]
        add(g2, lax.dot_general(mine, act_one, NT, preferred_element_type=F32))
        if last:
            finish_early()
        wide_one = act_one.astype(F32)
        delta_one = jnp.dot(w2t_ref[...], back_two, preferred_element_type=F32) * (
            1.0 - wide_one * wide_one
        )
        add(s1, lane_sum(delta_one))
        back_one = delta_one.astype(BF16)
        add(g1, lax.dot_general(back_one, x, NT, preferred_element_type=F32))
        return mismatch

    pieces = []
    for ref, count in zip(x_refs, planes):
        pieces += [ref[...]] if count == 1 else [ref[k] for k in range(count)]
    mismatch = plane(pieces[0] if len(pieces) == 1 else jnp.concatenate(pieces, axis=1))

    if first:
        row_loss = jnp.sum(mismatch * mismatch, axis=0, keepdims=True) / (6.0 * row_count)
        loss_ref[...] = jnp.sum(row_loss, axis=1, keepdims=True)
    if last:
        wide = jnp.concatenate([g1[...], jnp.zeros((hidden, WIDE - ROWS), F32)], axis=1).T
        for k in range(first_ref.shape[0]):
            first_ref[k] = wide[k : k + 1, :]
        bias_grads_ref[:, :hidden] = across(s1[...])


def train(xs, weights, held, optimizer, row_count, own_rows):
    planes = tuple(x.shape[0] if x.ndim == 3 else 1 for x in xs)
    slots = xs[0].shape[-1]
    hidden = weights[1].shape[0]
    first, last = held is None, optimizer is not None
    sums = [
        jax.ShapeDtypeStruct(s, F32)
        for s in (
            (hidden, ROWS),
            (own_rows, hidden),
            (16, hidden),
            (hidden, WIDE),
            (hidden, WIDE),
            (8, WIDE),
        )
    ]
    scratch = [pltpu.VMEM((hidden, slots * sum(planes)), BF16)]
    if last:
        out = [
            jax.ShapeDtypeStruct(s, F32)
            for s in (
                (81, 1, hidden),
                (6, 1, hidden),
                (1, 2 * hidden + 6),
                optimizer[0].shape,
                optimizer[0].shape,
            )
        ]
        scratch = [pltpu.VMEM(s.shape, F32) for s in sums] + scratch
    else:
        out = list(sums)
    if first:
        out.append(jax.ShapeDtypeStruct((1, 1), F32))
    operands = [*xs, *weights, *(held or ()), *(optimizer or ())]
    count = sum(planes)
    return pl.pallas_call(
        functools.partial(
            train_kernel,
            planes=planes,
            row_count=row_count,
            first=first,
            last=last,
            own_rows=own_rows,
        ),
        out_shape=tuple(out),
        in_specs=whole(len(operands)),
        out_specs=tuple(whole(len(out))),
        scratch_shapes=scratch,
        compiler_params=params(),
        cost_estimate=cost(1.6 * count),
        name="train",
    )(*operands)


def on_device(
    velocity,
    sample_cells,
    trainer_of,
    targets,
    w_first,
    w_middle,
    w_last,
    biases,
    middle_master,
    middle_momentum,
):
    comps, size_x, size_y, size_z = velocity.shape
    samples = sample_cells.shape[0]
    trainers = lax.axis_size("gx") * lax.axis_size("gy")
    capacity = 2 * samples // trainers
    slots = trainers * capacity
    hidden = w_middle.shape[1]
    planes = lax.axis_size("gz")
    own_rows = hidden // planes

    info = jnp.stack([sample_cells, trainer_of[:, 0]])
    x_halos = exchange("gx", *x_faces(velocity))
    features, choose, summing = patches(velocity, info)
    y_halos = exchange("gy", *y_faces(velocity, x_halos, features))
    z_low, z_high, placing, features = plan(
        velocity,
        x_halos,
        info,
        features,
        choose,
        summing,
        trainers,
        slots,
    )
    z_ends = z_faces(z_low, z_high, y_halos, size_y)
    z_halos = exchange("gz", *z_ends)
    features, rows = edges(features, y_halos, info, choose, summing, z_ends[0], size_x, size_y)
    tail = jnp.concatenate(
        [targets.astype(F32), jnp.ones((1, samples), F32), jnp.zeros((1, samples), F32)], axis=0
    )
    packed = pack(
        features, z_halos, info, rows, summing, tail, placing, comps, (size_x, size_y, size_z)
    )
    arrived = lax.all_to_all(
        packed.reshape(trainers, capacity, WIDE),
        ("gy", "gx"),
        split_axis=0,
        concat_axis=0,
        tiled=True,
    ).reshape(slots, WIDE)
    new_velocity, done = advance(velocity, (*x_halos, *y_halos, *z_halos))

    weights = prepare(w_first[0].T, w_middle[0], w_last[0], biases)
    optimizer = (
        middle_momentum.reshape(-1, WIDE),
        middle_master.reshape(-1, WIDE),
    )

    mine = turn(arrived, weights[-1], done)
    call = functools.partial(train, weights=weights, row_count=samples, own_rows=own_rows)
    swap = [(i, i ^ 1) for i in range(planes)]
    chips = planes // 2
    along = lambda to: [(i, 2 * (to(i // 2) % chips) + i % 2) for i in range(planes)]
    beside = lax.ppermute(mine, "gz", swap)
    far = lax.ppermute(mine, "gz", along(lambda x: x + 2))
    *held, loss = call([mine], held=None, optimizer=None)
    beside, far, *held = lax.optimization_barrier((beside, far, *held))
    both = jnp.stack([mine, beside])
    near = [
        lax.ppermute(both, "gz", along(lambda x: x ^ 1)),
        lax.ppermute(both, "gz", along(lambda x: x + 1 if x % 2 else x - 1)),
    ]
    far_beside = lax.ppermute(far, "gz", swap)
    held = call([beside, far], held=held, optimizer=None)
    first_grads, last_grads, bias_grads, master_new, momentum_new = call(
        [*near, far_beside], held=held, optimizer=optimizer
    )
    return (
        new_velocity,
        loss.reshape(1, 1, 1),
        first_grads.transpose(1, 2, 0),
        last_grads.transpose(1, 0, 2),
        bias_grads,
        master_new.reshape(middle_master.shape),
        momentum_new.reshape(middle_momentum.shape),
    )


def solution(mesh):
    placed = (
        P(None, "gx", "gy", "gz"),
        P(("gx", "gy", "gz")),
        P(("gx", "gy", "gz"), None),
        P(None, ("gx", "gy", "gz")),
        P(("gx", "gy"), None, None),
        P(("gx", "gy"), None, None),
        P(("gx", "gy"), None, None),
        P(("gx", "gy"), None),
        P(("gx", "gy"), "gz"),
        P(("gx", "gy"), "gz"),
    )
    return jax.shard_map(
        on_device,
        mesh=mesh,
        in_specs=placed,
        out_specs=(
            P(None, "gx", "gy", "gz"),
            P("gx", "gy", "gz"),
            P(("gx", "gy"), None, None),
            P(("gx", "gy"), None, None),
            P(("gx", "gy"), None),
            P(("gx", "gy"), "gz"),
            P(("gx", "gy"), "gz"),
        ),
        check_vma=False,
    )
```
